32 devices in a mesh: ta: 4 (over x, core), ha: 4 (over z), wa: 2 (over y).
Axes of the slice: x: 2, y: 2, z: 4, core: 2. Of those that a mesh axis runs over, the one named last changes fastest.
Arguments:
- tokens: bfloat16 [12, 32, 16, 1536], P('ta', 'ha', 'wa'), may hold values from -6 to 6
- modulation: float32 [3, 1536], replicated, may hold values from -4 to 4
- w_query: bfloat16 [1536, 1536], replicated
- w_key: bfloat16 [1536, 1536], replicated
- w_value: bfloat16 [1536, 1536], replicated, may hold values from -0.15625 to 0.15625
- w_out: bfloat16 [1536, 1536], replicated, may hold values from -0.15625 to 0.15625
- norm_q: float32 [1536], replicated, may hold values from 0.8 to 1.6
- norm_k: float32 [1536], replicated, may hold values from 0.8 to 1.6
Outputs:
- branch: bfloat16 [12, 32, 16, 1536], P('ta', 'ha', 'wa')
The draws below stay inside these ranges and needn't reach their ends.
All inputs are finite; a program needn't handle non-finite values.
Results may differ from the reference program's by a relative error of at most 0.0051.
Values may be sent and summed in bfloat16 or wider, within the bound.
No kernel may reach another device: no remote copies, remote signals or barrier semaphores. Data moves between devices by JAX's collectives and lax.ppermute only.
A program may use at most 192 MiB of HBM per device.

```python
import jax
import jax.numpy as jnp
from jax import lax

HEADS = 12
HEAD_DIM = 128
D = 1536
TT = 3
TH = 8
TW = 8
NT = 12
NH = 32
NW = 16


def shared_draw(key, which):
    own = jax.random.normal(jax.random.fold_in(key, which), (D, D), jnp.float32)
    return own * D ** (-0.5)


def draw_w_query(key, part):
    return shared_draw(key, 1).astype(jnp.bfloat16)


def draw_w_key(key, part):
    return shared_draw(key, 2).astype(jnp.bfloat16)


def shard_levels(stream_key, shape, split, least, high):
    level, own = 1.0, jax.random.fold_in(stream_key, 6)
    for position, parts in split:
        steps = jnp.exp(jax.random.uniform(jax.random.fold_in(own, position), (parts,), jnp.float32, least / len(split), high / len(split)))
        level = level * jnp.repeat(steps, shape[position] // parts).reshape([-1 if axis == position else 1 for axis in range(len(shape))])
    return level


def noise(rng, shape, width, bound, pieces=(), kind=jnp.bfloat16):
    values = width * jax.random.normal(rng, shape, jnp.float32)
    if pieces:
        values = values * shard_levels(rng, shape, pieces, -0.22, 0.18)
    return jnp.clip(values, -bound, bound).astype(kind)


def setup_inputs(seed: int = 0) -> dict:
    keys = jax.random.split(jax.random.key(seed), 9)
    tokens = noise(keys[0], (NT, NH, NW, D), 1.0, 6.0, ((0, 4), (1, 4), (2, 2)))
    modulation = noise(keys[1], (3, D), 1.0, 4.0, (), jnp.float32)
    w_query = draw_w_query(jax.random.fold_in(keys[8], 71), 0)
    w_key = draw_w_key(jax.random.fold_in(keys[8], 71), 0)
    w_value = noise(keys[4], (D, D), D ** -0.5, 0.15625)
    w_out = noise(keys[5], (D, D), D ** -0.5, 0.15625)
    norm_q = jnp.clip(jax.random.uniform(keys[6], (D,), jnp.float32, 0.8, 1.6), 0.8, 1.6)
    norm_k = jnp.clip(jax.random.uniform(keys[7], (D,), jnp.float32, 0.8, 1.6), 0.8, 1.6)
    return dict(tokens=tokens, modulation=modulation, w_query=w_query, w_key=w_key, w_value=w_value, w_out=w_out, norm_q=norm_q, norm_k=norm_k)


def modulate(tokens, modulation):
    values = tokens.astype(jnp.float32)
    center = values - lax.optimization_barrier(jnp.mean(values, axis=-1, keepdims=True))
    spread = lax.optimization_barrier(jnp.mean(center * center, axis=-1, keepdims=True))
    return (center * lax.rsqrt(spread + 1e-06) * (1.0 + modulation[1]) + modulation[0]).astype(jnp.bfloat16)

def rms_gain(values, gain):
    return values * lax.rsqrt(lax.optimization_barrier(jnp.mean(values * values, axis=-1, keepdims=True)) + 1e-06) * gain

def rotate_pairs(values, frame_pos, row_pos, column_pos):
    half = HEAD_DIM // 2
    sixth = HEAD_DIM // 6
    first = half - 2 * sixth
    freq_first = 10000.0 ** (-jnp.arange(first, dtype=jnp.float32) / first)
    freq_rest = 10000.0 ** (-jnp.arange(sixth, dtype=jnp.float32) / sixth)
    shape = values.shape[:3]
    angle_frame = frame_pos[:, None] * freq_first
    angle_row = row_pos[:, None] * freq_rest
    angle_column = column_pos[:, None] * freq_rest
    angles = jnp.concatenate([jnp.broadcast_to(angle_frame[:, None, None, :], shape + (first,)), jnp.broadcast_to(angle_row[None, :, None, :], shape + (sixth,)), jnp.broadcast_to(angle_column[None, None, :, :], shape + (sixth,))], axis=-1)
    cosine = jnp.cos(angles)[:, :, :, None, :]
    sine = jnp.sin(angles)[:, :, :, None, :]
    pairs = values.reshape(shape + (HEADS, half, 2))
    even_part = pairs[..., 0]
    odd_part = pairs[..., 1]
    rotated = jnp.stack([even_part * cosine - odd_part * sine, even_part * sine + odd_part * cosine], axis=-1)
    return rotated.reshape(values.shape)

def tile_rows(query, key_pad, value_pad, anchor, extent):
    frame_count, row_count, column_count, width_all = query.shape
    tile_frames = frame_count // TT
    tile_rows_n = row_count // TH
    tile_columns = column_count // TW
    tile_size = TT * TH * TW
    window = 27 * tile_size

    def one_row(index):
        frame_tile = index // tile_rows_n
        row_tile = index % tile_rows_n
        zero = jnp.zeros((), jnp.int32)
        query_row = lax.dynamic_slice(query, (frame_tile * TT, row_tile * TH, zero, zero), (TT, TH, column_count, width_all))
        query_row = query_row.reshape(TT, TH, tile_columns, TW, HEADS, HEAD_DIM).transpose(4, 2, 0, 1, 3, 5)
        query_row = query_row.reshape(HEADS, tile_columns, tile_size, HEAD_DIM)
        key_win = lax.dynamic_slice(key_pad, (frame_tile * TT, row_tile * TH, zero, zero), (3 * TT, 3 * TH, column_count + 2 * TW, width_all))
        value_win = lax.dynamic_slice(value_pad, (frame_tile * TT, row_tile * TH, zero, zero), (3 * TT, 3 * TH, column_count + 2 * TW, width_all))
        key_tiles = jnp.stack([key_win[:, :, column * TW:column * TW + 3 * TW] for column in range(tile_columns)])
        value_tiles = jnp.stack([value_win[:, :, column * TW:column * TW + 3 * TW] for column in range(tile_columns)])
        key_tiles = key_tiles.reshape(tile_columns, window, HEADS, HEAD_DIM).transpose(2, 0, 1, 3)
        value_tiles = value_tiles.reshape(tile_columns, window, HEADS, HEAD_DIM).transpose(2, 0, 1, 3)
        frames_at = anchor[0] + frame_tile * TT - TT + jnp.arange(3 * TT, dtype=jnp.int32)
        rows_at = anchor[1] + row_tile * TH - TH + jnp.arange(3 * TH, dtype=jnp.int32)
        columns_at = anchor[2] + jnp.arange(tile_columns, dtype=jnp.int32)[:, None] * TW - TW + jnp.arange(3 * TW, dtype=jnp.int32)[None, :]
        frame_ok = (frames_at >= 0) & (frames_at < extent[0])
        row_ok = (rows_at >= 0) & (rows_at < extent[1])
        column_ok = (columns_at >= 0) & (columns_at < extent[2])
        valid = frame_ok[None, :, None, None] & row_ok[None, None, :, None] & column_ok[:, None, None, :]
        valid = valid.reshape(tile_columns, window)

        def one_head(operands):
            head_query, head_key, head_value = operands
            scores = jnp.einsum('cqd,ckd->cqk', head_query.astype(jnp.float32), head_key.astype(jnp.float32)) * HEAD_DIM ** (-0.5)
            scores = jnp.where(valid[:, None, :], scores, -1e+30)
            peak = lax.optimization_barrier(jnp.max(scores, axis=-1, keepdims=True))
            expo = jnp.exp(scores - peak)
            weights = (expo / lax.optimization_barrier(jnp.sum(expo, axis=-1, keepdims=True))).astype(jnp.bfloat16)
            return jnp.einsum('cqk,ckd->cqd', weights.astype(jnp.float32), head_value.astype(jnp.float32)).astype(jnp.bfloat16)
        attended = lax.map(one_head, (query_row, key_tiles, value_tiles))
        attended = attended.reshape(HEADS, tile_columns, TT, TH, TW, HEAD_DIM).transpose(2, 3, 1, 4, 0, 5)
        return attended.reshape(TT, TH, column_count, width_all)
    result = lax.map(one_row, jnp.arange(tile_frames * tile_rows_n, dtype=jnp.int32))
    result = result.reshape(tile_frames, tile_rows_n, TT, TH, column_count, width_all).transpose(0, 2, 1, 3, 4, 5)
    return result.reshape(frame_count, row_count, column_count, width_all)

def reference(tokens, modulation, w_query, w_key, w_value, w_out, norm_q, norm_k):
    normed = modulate(tokens, modulation)
    flat = normed.reshape(-1, D)
    grid = (NT, NH, NW, D)
    frame_pos = jnp.arange(NT, dtype=jnp.int32).astype(jnp.float32)
    row_pos = jnp.arange(NH, dtype=jnp.int32).astype(jnp.float32)
    column_pos = jnp.arange(NW, dtype=jnp.int32).astype(jnp.float32)
    query = rms_gain(jnp.dot(flat, w_query, preferred_element_type=jnp.float32), norm_q).reshape(grid)
    query = rotate_pairs(query, frame_pos, row_pos, column_pos).astype(jnp.bfloat16)
    key = rms_gain(jnp.dot(flat, w_key, preferred_element_type=jnp.float32), norm_k).reshape(grid)
    key = rotate_pairs(key, frame_pos, row_pos, column_pos).astype(jnp.bfloat16)
    value = jnp.dot(flat, w_value, preferred_element_type=jnp.float32).astype(jnp.bfloat16).reshape(grid)
    padding = ((TT, TT), (TH, TH), (TW, TW), (0, 0))
    key_pad = jnp.pad(key, padding)
    value_pad = jnp.pad(value, padding)
    attended = tile_rows(query, key_pad, value_pad, (0, 0, 0), (NT, NH, NW))
    branch = jnp.dot(attended.reshape(-1, D), w_out, preferred_element_type=jnp.float32) * modulation[2]
    return branch.astype(jnp.bfloat16).reshape(grid)
```

```python
import functools

import jax
import jax.numpy as jnp
import numpy as np
from jax import lax
from jax.experimental import pallas as pl
from jax.experimental.pallas import tpu as pltpu
from jax.sharding import PartitionSpec as P

HEADS = 12
HEAD_DIM = 128
D = 1536
TT = 3
TH = 8
TW = 8
CT = 3
CH = 8
CW = 8


def with_halo(value, sides, width):
    for axis, dim in sides:
        devices, length = (lax.axis_size(axis), value.shape[dim])
        up = [(i, (i + 1) % devices) for i in range(devices - 1)]
        down = [(j, i) for i, j in up]
        last = lax.slice_in_dim(value, length - width, length, axis=dim)
        first = lax.slice_in_dim(value, 0, width, axis=dim)
        before = lax.ppermute(last, axis, up)
        after = lax.ppermute(first, axis, down)
        value = jnp.concatenate([before, value, after], axis=dim)
    return value


def modulate(tokens, modulation):
    values = tokens.astype(jnp.float32)
    center = values - jnp.mean(values, axis=-1, keepdims=True)
    spread = jnp.mean(center * center, axis=-1, keepdims=True)
    return (center * lax.rsqrt(spread + 1e-06) * (1.0 + modulation[1]) + modulation[0]).astype(
        jnp.bfloat16
    )


def rms_gain(values, gain):
    return values * lax.rsqrt(jnp.mean(values * values, axis=-1, keepdims=True) + 1e-06) * gain


def rotate_pairs(values, frame_pos, row_pos, column_pos):
    half = HEAD_DIM // 2
    sixth = HEAD_DIM // 6
    first = half - 2 * sixth
    freq_first = 10000.0 ** (-jnp.arange(first, dtype=jnp.float32) / first)
    freq_rest = 10000.0 ** (-jnp.arange(sixth, dtype=jnp.float32) / sixth)
    shape = values.shape[:3]
    angle_frame = frame_pos[:, None] * freq_first
    angle_row = row_pos[:, None] * freq_rest
    angle_column = column_pos[:, None] * freq_rest
    angles = jnp.concatenate(
        [
            jnp.broadcast_to(angle_frame[:, None, None, :], shape + (first,)),
            jnp.broadcast_to(angle_row[None, :, None, :], shape + (sixth,)),
            jnp.broadcast_to(angle_column[None, None, :, :], shape + (sixth,)),
        ],
        axis=-1,
    )
    cosine = jnp.cos(angles)[:, :, :, None, :]
    sine = jnp.sin(angles)[:, :, :, None, :]
    pairs = values.reshape(shape + (HEADS, half, 2))
    even_part = pairs[..., 0]
    odd_part = pairs[..., 1]
    rotated = jnp.stack(
        [even_part * cosine - odd_part * sine, even_part * sine + odd_part * cosine], axis=-1
    )
    return rotated.reshape(values.shape)


def tile_rows(query, key_pad, value_pad, anchor, extent):
    tile_frames = CT // TT
    tile_rows_n = CH // TH
    tile_columns = CW // TW
    tile_size = TT * TH * TW
    window = 27 * tile_size

    def one_row(index):
        frame_tile = index // tile_rows_n
        row_tile = index % tile_rows_n
        query_row = query
        query_row = query_row.reshape(TT, TH, tile_columns, TW, HEADS, HEAD_DIM).transpose(
            4, 2, 0, 1, 3, 5
        )
        query_row = query_row.reshape(HEADS, tile_columns, tile_size, HEAD_DIM)
        key_tiles = jnp.stack([key_pad])
        value_tiles = jnp.stack([value_pad])
        key_tiles = key_tiles.reshape(tile_columns, window, HEADS, HEAD_DIM).transpose(2, 0, 1, 3)
        value_tiles = value_tiles.reshape(tile_columns, window, HEADS, HEAD_DIM).transpose(
            2, 0, 1, 3
        )
        frames_at = anchor[0] + frame_tile * TT - TT + jnp.arange(3 * TT, dtype=jnp.int32)
        rows_at = anchor[1] + row_tile * TH - TH + jnp.arange(3 * TH, dtype=jnp.int32)
        columns_at = (
            anchor[2]
            + jnp.arange(tile_columns, dtype=jnp.int32)[:, None] * TW
            - TW
            + jnp.arange(3 * TW, dtype=jnp.int32)[None, :]
        )
        frame_ok = (frames_at >= 0) & (frames_at < extent[0])
        row_ok = (rows_at >= 0) & (rows_at < extent[1])
        column_ok = (columns_at >= 0) & (columns_at < extent[2])
        valid = (
            frame_ok[None, :, None, None]
            & row_ok[None, None, :, None]
            & column_ok[:, None, None, :]
        )
        valid = valid.reshape(tile_columns, window)

        def one_head(operands):
            head_query, head_key, head_value = operands
            scores = jnp.einsum(
                "cqd,ckd->cqk", head_query, head_key, preferred_element_type=jnp.float32
            ) * HEAD_DIM ** (-0.5)
            scores = jnp.where(valid[:, None, :], scores, -1e30)
            peak = jnp.max(scores, axis=-1, keepdims=True)
            expo = jnp.exp(scores - peak)
            weights = (expo / jnp.sum(expo, axis=-1, keepdims=True)).astype(jnp.bfloat16)
            return jnp.einsum(
                "cqk,ckd->cqd", weights, head_value, preferred_element_type=jnp.float32
            ).astype(jnp.bfloat16)

        attended = lax.map(one_head, (query_row, key_tiles, value_tiles))
        attended = attended.reshape(HEADS, tile_columns, TT, TH, TW, HEAD_DIM).transpose(
            2, 3, 1, 4, 0, 5
        )
        return attended.reshape(TT, TH, CW, D)

    result = lax.map(one_row, jnp.arange(tile_frames * tile_rows_n, dtype=jnp.int32))
    result = result.reshape(tile_frames, tile_rows_n, TT, TH, CW, D).transpose(0, 2, 1, 3, 4, 5)
    return result.reshape(CT, CH, CW, D)


def body(tokens, modulation, w_query, w_key, w_value, w_out, norm_q, norm_k):
    anchor = (lax.axis_index("ta") * CT, lax.axis_index("ha") * CH, lax.axis_index("wa") * CW)
    extent = (lax.axis_size("ta") * CT, lax.axis_size("ha") * CH, lax.axis_size("wa") * CW)
    frame_pos = (anchor[0] + jnp.arange(CT, dtype=jnp.int32)).astype(jnp.float32)
    row_pos = (anchor[1] + jnp.arange(CH, dtype=jnp.int32)).astype(jnp.float32)
    column_pos = (anchor[2] + jnp.arange(CW, dtype=jnp.int32)).astype(jnp.float32)
    grid = (CT, CH, CW, D)
    normed = modulate(tokens, modulation)
    flat = normed.reshape(-1, D)
    key = rms_gain(jnp.dot(flat, w_key, preferred_element_type=jnp.float32), norm_k).reshape(grid)
    key = rotate_pairs(key, frame_pos, row_pos, column_pos).astype(jnp.bfloat16)
    value = (
        jnp.dot(flat, w_value, preferred_element_type=jnp.float32)
        .astype(jnp.bfloat16)
        .reshape(grid)
    )
    key_value = jnp.stack([key, value])
    framed = with_halo(key_value, (("ta", 1),), TT)
    padded = with_halo(framed, (("ha", 2), ("wa", 3)), TW)
    query = rms_gain(jnp.dot(flat, w_query, preferred_element_type=jnp.float32), norm_q).reshape(
        grid
    )
    query = rotate_pairs(query, frame_pos, row_pos, column_pos).astype(jnp.bfloat16)
    attended = tile_rows(query, padded[0], padded[1], anchor, extent)
    branch = (
        jnp.dot(attended.reshape(-1, D), w_out, preferred_element_type=jnp.float32) * modulation[2]
    )
    return branch.astype(jnp.bfloat16).reshape(grid)


TILE = TT * TH * TW
GROUPS = 4
GH = HEADS // GROUPS
GW = GH * HEAD_DIM
SCORE_SCALE = float(HEAD_DIM ** (-0.5) * np.log2(np.e))
VMEM_LIMIT = 56 * 1024 * 1024


def rope_tables(devices, per_device, low, count):
    n = np.float32(count)
    freq = np.float32(10000.0) ** (-np.arange(count, dtype=np.float32) / n)
    angle = np.arange(devices * per_device, dtype=np.float32)[:, None] * freq[None, :]
    cosine = np.zeros((devices * per_device, HEAD_DIM), np.float32)
    sine = np.zeros((devices * per_device, HEAD_DIM), np.float32)
    for j in range(count):
        lane = 2 * (low + j)
        cosine[:, lane] = cosine[:, lane + 1] = np.cos(angle[:, j])
        sine[:, lane] = -np.sin(angle[:, j])
        sine[:, lane + 1] = np.sin(angle[:, j])
    tables = np.stack([cosine, sine]).reshape(2, devices, per_device, HEAD_DIM)
    return jnp.asarray(tables.transpose(1, 0, 2, 3))


def layer_norm(tok_ref, mod_ref):
    values = tok_ref[...].astype(jnp.float32)
    center = values - jnp.mean(values, axis=-1, keepdims=True)
    spread = jnp.mean(center * center, axis=-1, keepdims=True)
    shift, scale = mod_ref[0:1, :], mod_ref[1:2, :]
    return (center * lax.rsqrt(spread + 1e-06) * (1.0 + scale) + shift).astype(jnp.bfloat16)


def angle_tables(sc_ref, ft_ref, rt_ref, ct_ref):
    out = []
    for kind in range(2):
        frame = ft_ref[sc_ref[1], kind]
        row = rt_ref[sc_ref[2], kind]
        column = ct_ref[sc_ref[3], kind]
        full = frame[:, None, None, :] + row[None, :, None, :] + column[None, None, :, :]
        out.append(full.reshape(TILE, HEAD_DIM))
    return out


def rope(x, cosine, sine, even):
    swapped = jnp.where(even, pltpu.roll(x, HEAD_DIM - 1, 1), pltpu.roll(x, 1, 1))
    return x * cosine + swapped * sine


def fold_squares(prod):
    total = None
    for h in range(GH):
        piece = prod[:, h * HEAD_DIM : (h + 1) * HEAD_DIM]
        total = piece * piece if total is None else total + piece * piece
    return total


def finish_normed(sc_ref, tables, buf, gains, ssq, write):
    cosine, sine = angle_tables(sc_ref, *tables)
    even = lax.broadcasted_iota(jnp.int32, (TILE, HEAD_DIM), 1) % 2 == 0
    inv = lax.rsqrt(jnp.sum(ssq[...], axis=-1, keepdims=True) / D + 1e-06)
    for m in range(GROUPS):
        for h in range(GH):
            lanes = slice(h * HEAD_DIM, (h + 1) * HEAD_DIM)
            x = buf[m, :, lanes] * inv * gains[m, :, lanes]
            write(m, h, rope(x, cosine, sine, even).astype(jnp.bfloat16))


def kv_kernel(sc_ref, tok_ref, mod_ref, nk_ref, ft_ref, rt_ref, ct_ref, wk_ref, wv_ref, o0, o1, o2, o3, normed_ref, buf, gains, ssq):
    outs = (o0, o1, o2, o3)
    i = pl.program_id(0)

    @pl.when(i == 0)
    def _():
        normed_ref[...] = layer_norm(tok_ref, mod_ref)
        ssq[...] = jnp.zeros_like(ssq)

    @pl.when(i < GROUPS)
    def _():
        prod = jnp.dot(normed_ref[...], wk_ref[...], preferred_element_type=jnp.float32)
        buf[i] = prod
        gains[i] = nk_ref[...]
        ssq[...] += fold_squares(prod)

    @pl.when(i == GROUPS - 1)
    def _():
        def write(m, h, x):
            outs[m][0, h] = x

        finish_normed(sc_ref, (ft_ref, rt_ref, ct_ref), buf, gains, ssq, write)

    for m in range(GROUPS):

        @pl.when(i == GROUPS + m)
        def _():
            prod = jnp.dot(normed_ref[...], wv_ref[...], preferred_element_type=jnp.float32)
            for h in range(GH):
                outs[m][1, h] = prod[:, h * HEAD_DIM : (h + 1) * HEAD_DIM].astype(jnp.bfloat16)


def q_kernel(sc_ref, normed_ref, nq_ref, ft_ref, rt_ref, ct_ref, wq_ref, o0, o1, o2, o3, buf, gains, ssq):
    outs = (o0, o1, o2, o3)
    i = pl.program_id(0)

    @pl.when(i == 0)
    def _():
        ssq[...] = jnp.zeros_like(ssq)

    prod = jnp.dot(normed_ref[...], wq_ref[...], preferred_element_type=jnp.float32)
    buf[i] = prod
    gains[i] = nq_ref[...]
    ssq[...] += fold_squares(prod)

    @pl.when(i == GROUPS - 1)
    def _():
        def write(m, h, x):
            outs[m][h] = x

        finish_normed(sc_ref, (ft_ref, rt_ref, ct_ref), buf, gains, ssq, write)


def whole_spec(shape):
    return pl.BlockSpec(shape, lambda i, sc: (0,) * len(shape))


def project_kv(sc, tokens, modulation, norm_k, tables, w_key, w_value):
    kv_shape = (2, GH, TILE, HEAD_DIM)
    return pl.pallas_call(
        kv_kernel,
        grid_spec=pltpu.PrefetchScalarGridSpec(
            num_scalar_prefetch=1,
            grid=(2 * GROUPS,),
            in_specs=[
                whole_spec((TILE, D)),
                whole_spec((3, D)),
                pl.BlockSpec((1, GW), lambda i, sc: (0, jnp.minimum(i, GROUPS - 1) ^ sc[0])),
                *[whole_spec(t.shape) for t in tables],
                pl.BlockSpec((D, GW), lambda i, sc: (0, jnp.minimum(i, GROUPS - 1) ^ sc[0])),
                pl.BlockSpec((D, GW), lambda i, sc: (0, jnp.maximum(i - GROUPS, 0) ^ sc[0])),
            ],
            out_specs=[whole_spec(kv_shape)] * GROUPS + [whole_spec((TILE, D))],
            scratch_shapes=[
                pltpu.VMEM((GROUPS, TILE, GW), jnp.float32),
                pltpu.VMEM((GROUPS, 1, GW), jnp.float32),
                pltpu.VMEM((TILE, HEAD_DIM), jnp.float32),
            ],
        ),
        out_shape=[jax.ShapeDtypeStruct(kv_shape, jnp.bfloat16)] * GROUPS
        + [jax.ShapeDtypeStruct((TILE, D), jnp.bfloat16)],
        compiler_params=pltpu.CompilerParams(vmem_limit_bytes=VMEM_LIMIT),
        cost_estimate=pl.CostEstimate(flops=4 * TILE * D * D, bytes_accessed=4 * D * D, transcendentals=0),
        name="project_kv",
    )(sc, tokens, modulation, norm_k, *tables, w_key, w_value)


def project_q(sc, normed, norm_q, tables, w_query):
    q_shape = (GH, TILE, HEAD_DIM)
    return pl.pallas_call(
        q_kernel,
        grid_spec=pltpu.PrefetchScalarGridSpec(
            num_scalar_prefetch=1,
            grid=(GROUPS,),
            in_specs=[
                whole_spec((TILE, D)),
                pl.BlockSpec((1, GW), lambda i, sc: (0, i ^ sc[0])),
                *[whole_spec(t.shape) for t in tables],
                pl.BlockSpec((D, GW), lambda i, sc: (0, i ^ sc[0])),
            ],
            out_specs=[whole_spec(q_shape)] * GROUPS,
            scratch_shapes=[
                pltpu.VMEM((GROUPS, TILE, GW), jnp.float32),
                pltpu.VMEM((GROUPS, 1, GW), jnp.float32),
                pltpu.VMEM((TILE, HEAD_DIM), jnp.float32),
            ],
        ),
        out_shape=[jax.ShapeDtypeStruct(q_shape, jnp.bfloat16)] * GROUPS,
        compiler_params=pltpu.CompilerParams(vmem_limit_bytes=VMEM_LIMIT),
        cost_estimate=pl.CostEstimate(flops=2 * TILE * D * D, bytes_accessed=2 * D * D, transcendentals=0),
        name="project_q",
    )(sc, normed, norm_q, *tables, w_query)


def pair_of(refs, kind):
    return jnp.concatenate([ref[kind, 0] for ref in refs], axis=0)


def attend_block(query, keys, values, peak_ref, acc_ref, s, first):
    scores = lax.dot_general(query, keys, (((1,), (1,)), ((), ())), preferred_element_type=jnp.float32) * SCORE_SCALE
    peak = jnp.max(scores, axis=-1, keepdims=True)
    if not first:
        old = peak_ref[0, s][:, :1]
        peak = jnp.maximum(old, peak)
    expo = jnp.exp2(scores - peak).astype(jnp.bfloat16)
    ones = jnp.ones((values.shape[0], HEAD_DIM), jnp.bfloat16)
    part = jnp.dot(expo, jnp.concatenate([values, ones], axis=1), preferred_element_type=jnp.float32)
    if not first:
        part = acc_ref[0, s] * jnp.exp2(old - peak) + part
    acc_ref[0, s] = part
    peak_ref[0, s] = jnp.broadcast_to(peak, (2 * TILE, HEAD_DIM))


def own_row_kernel(sc_ref, *refs):
    q, same, other = refs[0:4], refs[4:8], refs[8:12]
    peak_ref, acc_ref = refs[12:]
    for s in range(2):
        query = jnp.concatenate([q[2 * s][0], q[2 * s + 1][0]], axis=0)
        for n, keys in enumerate((same, other)):
            pair = keys[2 * s : 2 * s + 2]
            attend_block(query, pair_of(pair, 0), pair_of(pair, 1), peak_ref, acc_ref, s, n == 0)

        @pl.when(sc_ref[4] == s)
        def _():
            pair = other[2 * (1 - s) : 2 * (1 - s) + 2]
            attend_block(query, pair_of(pair, 0), pair_of(pair, 1), peak_ref, acc_ref, s, False)


def halo_kernel(slot, final, sc_ref, *refs):
    q = refs[0:4]
    rows = [(refs[4 + 4 * r : 6 + 4 * r], refs[6 + 4 * r : 8 + 4 * r]) for r in range(2)]
    peak_in, acc_in = refs[12:14]
    if final:
        outs, (peak_ref, acc_ref) = refs[14:18], refs[18:20]
    else:
        peak_ref, acc_ref = refs[14:16]
    peak_ref[...] = peak_in[...]
    acc_ref[...] = acc_in[...]
    for r, (same, other) in enumerate(rows):

        @pl.when(sc_ref[5 + r] == 1)
        def _():
            query = jnp.concatenate([q[2 * slot][0], q[2 * slot + 1][0]], axis=0)
            for pair in (same, other):
                attend_block(query, pair_of(pair, 0), pair_of(pair, 1), peak_ref, acc_ref, slot, False)

            @pl.when(sc_ref[4] == 1 - slot)
            def _():
                far = jnp.concatenate([q[2 * (1 - slot)][0], q[2 * (1 - slot) + 1][0]], axis=0)
                attend_block(far, pair_of(other, 0), pair_of(other, 1), peak_ref, acc_ref, 1 - slot, False)

    if final:
        for m in range(GROUPS):
            rows_at = slice((m % 2) * TILE, (m % 2 + 1) * TILE)
            acc = acc_ref[0, m // 2, rows_at]
            outs[m][0] = (acc[:, :HEAD_DIM] / acc[:, HEAD_DIM:]).astype(jnp.bfloat16)


Q_SPEC = pl.BlockSpec((1, TILE, HEAD_DIM), lambda h, sc: (h, 0, 0))
KV_SPEC = pl.BlockSpec((2, 1, TILE, HEAD_DIM), lambda h, sc: (0, h, 0, 0))
PEAK_SPEC = pl.BlockSpec((1, 2, 2 * TILE, HEAD_DIM), lambda h, sc: (h, 0, 0, 0))
ACC_SPEC = pl.BlockSpec((1, 2, 2 * TILE, 2 * HEAD_DIM), lambda h, sc: (h, 0, 0, 0))
STATE_SHAPES = [
    jax.ShapeDtypeStruct((GH, 2, 2 * TILE, HEAD_DIM), jnp.float32),
    jax.ShapeDtypeStruct((GH, 2, 2 * TILE, 2 * HEAD_DIM), jnp.float32),
]


def attend_cost(blocks):
    pairs = GH * blocks * 4 * TILE * TILE
    return pl.CostEstimate(flops=4 * pairs * HEAD_DIM, bytes_accessed=12 * TILE * GW * 2, transcendentals=pairs)


def attend_own(sc, queries, same, other):
    return pl.pallas_call(
        own_row_kernel,
        grid_spec=pltpu.PrefetchScalarGridSpec(
            num_scalar_prefetch=1,
            grid=(GH,),
            in_specs=[Q_SPEC] * 4 + [KV_SPEC] * 8,
            out_specs=[PEAK_SPEC, ACC_SPEC],
        ),
        out_shape=STATE_SHAPES,
        compiler_params=pltpu.CompilerParams(vmem_limit_bytes=VMEM_LIMIT),
        cost_estimate=attend_cost(5),
        name="attend_own",
    )(sc, *queries, *same, *other)


def attend_halo(slot, final, sc, queries, tiles, state):
    if final:
        out_specs = [Q_SPEC] * GROUPS
        out_shape = [jax.ShapeDtypeStruct((GH, TILE, HEAD_DIM), jnp.bfloat16)] * GROUPS
        scratch = [
            pltpu.VMEM((1, 2, 2 * TILE, HEAD_DIM), jnp.float32),
            pltpu.VMEM((1, 2, 2 * TILE, 2 * HEAD_DIM), jnp.float32),
        ]
    else:
        out_specs, out_shape, scratch = [PEAK_SPEC, ACC_SPEC], STATE_SHAPES, []
    return pl.pallas_call(
        functools.partial(halo_kernel, slot, final),
        grid_spec=pltpu.PrefetchScalarGridSpec(
            num_scalar_prefetch=1,
            grid=(GH,),
            in_specs=[Q_SPEC] * 4 + [KV_SPEC] * 8 + [PEAK_SPEC, ACC_SPEC],
            out_specs=out_specs,
            scratch_shapes=scratch,
        ),
        out_shape=out_shape,
        compiler_params=pltpu.CompilerParams(vmem_limit_bytes=VMEM_LIMIT),
        cost_estimate=attend_cost(5),
        name="attend_halo",
    )(sc, *queries, *tiles, *state)


def out_kernel(sc_ref, a0, a1, a2, a3, mod_ref, w_ref, out_ref, acc):
    i = pl.program_id(0)
    for m, ref in enumerate((a0, a1, a2, a3)):

        @pl.when(i == m)
        def _():
            rows = jnp.concatenate([ref[h] for h in range(GH)], axis=1)
            part = jnp.dot(rows, w_ref[...], preferred_element_type=jnp.float32)
            if m == 0:
                acc[...] = part
            elif m < GROUPS - 1:
                acc[...] += part
            else:
                out_ref[...] = ((acc[...] + part) * mod_ref[2:3, :]).astype(jnp.bfloat16)


def project_out(sc, attended, modulation, w_out):
    return pl.pallas_call(
        out_kernel,
        grid_spec=pltpu.PrefetchScalarGridSpec(
            num_scalar_prefetch=1,
            grid=(GROUPS,),
            in_specs=[whole_spec((GH, TILE, HEAD_DIM))] * GROUPS
            + [whole_spec((3, D)), pl.BlockSpec((GW, D), lambda i, sc: (i ^ sc[0], 0))],
            out_specs=whole_spec((TILE, D)),
            scratch_shapes=[pltpu.VMEM((TILE, D), jnp.float32)],
        ),
        out_shape=jax.ShapeDtypeStruct((TILE, D), jnp.bfloat16),
        compiler_params=pltpu.CompilerParams(vmem_limit_bytes=VMEM_LIMIT),
        cost_estimate=pl.CostEstimate(flops=2 * TILE * D * D, bytes_accessed=2 * D * D, transcendentals=0),
        name="project_out",
    )(sc, *attended, modulation, w_out)


def square_swap(value, m):
    if m == 0:
        return value
    flip = (m >> 1) * 4 + (m & 1)
    return lax.ppermute(value, ("ta", "wa"), [(i, i ^ flip) for i in range(8)])


def core_swap(value):
    return lax.ppermute(value, "ta", [(i, i ^ 1) for i in range(4)])


def square_body(tokens, modulation, w_query, w_key, w_value, w_out, norm_q, norm_k):
    ta, ha, wa = (lax.axis_index(name) for name in ("ta", "ha", "wa"))
    rows_n = lax.axis_size("ha")
    place_x, core = ta // 2, ta % 2
    near_slot = 1 - (place_x ^ core)
    sc = jnp.stack(
        [2 * place_x + wa, ta, ha, wa, near_slot, (ha > 0).astype(jnp.int32), (ha < rows_n - 1).astype(jnp.int32)]
    ).astype(jnp.int32)
    half, sixth = HEAD_DIM // 2, HEAD_DIM // 6
    first = half - 2 * sixth
    tables = (
        rope_tables(lax.axis_size("ta"), CT, 0, first),
        rope_tables(rows_n, CH, first, sixth),
        rope_tables(lax.axis_size("wa"), CW, first + sixth, sixth),
    )
    *kv, normed = project_kv(sc, tokens.reshape(TILE, D), modulation, norm_k.reshape(1, D), tables, w_key, w_value)
    up = [(i, i + 1) for i in range(rows_n - 1)]
    down = [(i + 1, i) for i in range(rows_n - 1)]
    same = [square_swap(kv[m], m) for m in range(GROUPS)]
    above = [lax.ppermute(tile, "ha", up) for tile in same]
    below = [lax.ppermute(tile, "ha", down) for tile in same]
    other = [core_swap(tile) for tile in same]
    above_other = [core_swap(tile) for tile in above]
    below_other = [core_swap(tile) for tile in below]
    queries = project_q(sc, normed, norm_q.reshape(1, D), tables, w_query)
    queries = [square_swap(queries[m], m) for m in range(GROUPS)]
    state = attend_own(sc, queries, same, other)
    for slot in range(2):
        at = slice(2 * slot, 2 * slot + 2)
        tiles = [*above[at], *above_other[at], *below[at], *below_other[at]]
        state = attend_halo(slot, slot == 1, sc, queries, tiles, state)
    attended = [square_swap(state[m], m) for m in range(GROUPS)]
    branch = project_out(sc, attended, modulation, w_out)
    return branch.reshape(CT, CH, CW, D)


def solution(mesh):
    square = mesh.shape["ta"] == 4 and mesh.shape["wa"] == 2
    chosen = square_body if square else body
    in_specs = (P("ta", "ha", "wa", None), P(), P(), P(), P(), P(), P(), P())
    out_specs = P("ta", "ha", "wa", None)
    return jax.shard_map(chosen, mesh=mesh, in_specs=in_specs, out_specs=out_specs, check_vma=False)
```

```python
import functools

import jax
import jax.numpy as jnp
import numpy as np
from jax import lax
from jax.experimental import pallas as pl
from jax.experimental.pallas import tpu as pltpu
from jax.sharding import PartitionSpec as P

HEADS = 12
HEAD_DIM = 128
D = 1536
TT = 3
TH = 8
TW = 8
CT = 3
CH = 8
CW = 8


def with_halo(value, sides, width):
    for axis, dim in sides:
        devices, length = (lax.axis_size(axis), value.shape[dim])
        up = [(i, (i + 1) % devices) for i in range(devices - 1)]
        down = [(j, i) for i, j in up]
        last = lax.slice_in_dim(value, length - width, length, axis=dim)
        first = lax.slice_in_dim(value, 0, width, axis=dim)
        before = lax.ppermute(last, axis, up)
        after = lax.ppermute(first, axis, down)
        value = jnp.concatenate([before, value, after], axis=dim)
    return value


def modulate(tokens, modulation):
    values = tokens.astype(jnp.float32)
    center = values - jnp.mean(values, axis=-1, keepdims=True)
    spread = jnp.mean(center * center, axis=-1, keepdims=True)
    return (center * lax.rsqrt(spread + 1e-06) * (1.0 + modulation[1]) + modulation[0]).astype(
        jnp.bfloat16
    )


def rms_gain(values, gain):
    return values * lax.rsqrt(jnp.mean(values * values, axis=-1, keepdims=True) + 1e-06) * gain


def rotate_pairs(values, frame_pos, row_pos, column_pos):
    half = HEAD_DIM // 2
    sixth = HEAD_DIM // 6
    first = half - 2 * sixth
    freq_first = 10000.0 ** (-jnp.arange(first, dtype=jnp.float32) / first)
    freq_rest = 10000.0 ** (-jnp.arange(sixth, dtype=jnp.float32) / sixth)
    shape = values.shape[:3]
    angle_frame = frame_pos[:, None] * freq_first
    angle_row = row_pos[:, None] * freq_rest
    angle_column = column_pos[:, None] * freq_rest
    angles = jnp.concatenate(
        [
            jnp.broadcast_to(angle_frame[:, None, None, :], shape + (first,)),
            jnp.broadcast_to(angle_row[None, :, None, :], shape + (sixth,)),
            jnp.broadcast_to(angle_column[None, None, :, :], shape + (sixth,)),
        ],
        axis=-1,
    )
    cosine = jnp.cos(angles)[:, :, :, None, :]
    sine = jnp.sin(angles)[:, :, :, None, :]
    pairs = values.reshape(shape + (HEADS, half, 2))
    even_part = pairs[..., 0]
    odd_part = pairs[..., 1]
    rotated = jnp.stack(
        [even_part * cosine - odd_part * sine, even_part * sine + odd_part * cosine], axis=-1
    )
    return rotated.reshape(values.shape)


def tile_rows(query, key_pad, value_pad, anchor, extent):
    tile_frames = CT // TT
    tile_rows_n = CH // TH
    tile_columns = CW // TW
    tile_size = TT * TH * TW
    window = 27 * tile_size

    def one_row(index):
        frame_tile = index // tile_rows_n
        row_tile = index % tile_rows_n
        query_row = query
        query_row = query_row.reshape(TT, TH, tile_columns, TW, HEADS, HEAD_DIM).transpose(
            4, 2, 0, 1, 3, 5
        )
        query_row = query_row.reshape(HEADS, tile_columns, tile_size, HEAD_DIM)
        key_tiles = jnp.stack([key_pad])
        value_tiles = jnp.stack([value_pad])
        key_tiles = key_tiles.reshape(tile_columns, window, HEADS, HEAD_DIM).transpose(2, 0, 1, 3)
        value_tiles = value_tiles.reshape(tile_columns, window, HEADS, HEAD_DIM).transpose(
            2, 0, 1, 3
        )
        frames_at = anchor[0] + frame_tile * TT - TT + jnp.arange(3 * TT, dtype=jnp.int32)
        rows_at = anchor[1] + row_tile * TH - TH + jnp.arange(3 * TH, dtype=jnp.int32)
        columns_at = (
            anchor[2]
            + jnp.arange(tile_columns, dtype=jnp.int32)[:, None] * TW
            - TW
            + jnp.arange(3 * TW, dtype=jnp.int32)[None, :]
        )
        frame_ok = (frames_at >= 0) & (frames_at < extent[0])
        row_ok = (rows_at >= 0) & (rows_at < extent[1])
        column_ok = (columns_at >= 0) & (columns_at < extent[2])
        valid = (
            frame_ok[None, :, None, None]
            & row_ok[None, None, :, None]
            & column_ok[:, None, None, :]
        )
        valid = valid.reshape(tile_columns, window)

        def one_head(operands):
            head_query, head_key, head_value = operands
            scores = jnp.einsum(
                "cqd,ckd->cqk", head_query, head_key, preferred_element_type=jnp.float32
            ) * HEAD_DIM ** (-0.5)
            scores = jnp.where(valid[:, None, :], scores, -1e30)
            peak = jnp.max(scores, axis=-1, keepdims=True)
            expo = jnp.exp(scores - peak)
            weights = (expo / jnp.sum(expo, axis=-1, keepdims=True)).astype(jnp.bfloat16)
            return jnp.einsum(
                "cqk,ckd->cqd", weights, head_value, preferred_element_type=jnp.float32
            ).astype(jnp.bfloat16)

        attended = lax.map(one_head, (query_row, key_tiles, value_tiles))
        attended = attended.reshape(HEADS, tile_columns, TT, TH, TW, HEAD_DIM).transpose(
            2, 3, 1, 4, 0, 5
        )
        return attended.reshape(TT, TH, CW, D)

    result = lax.map(one_row, jnp.arange(tile_frames * tile_rows_n, dtype=jnp.int32))
    result = result.reshape(tile_frames, tile_rows_n, TT, TH, CW, D).transpose(0, 2, 1, 3, 4, 5)
    return result.reshape(CT, CH, CW, D)


def body(tokens, modulation, w_query, w_key, w_value, w_out, norm_q, norm_k):
    anchor = (lax.axis_index("ta") * CT, lax.axis_index("ha") * CH, lax.axis_index("wa") * CW)
    extent = (lax.axis_size("ta") * CT, lax.axis_size("ha") * CH, lax.axis_size("wa") * CW)
    frame_pos = (anchor[0] + jnp.arange(CT, dtype=jnp.int32)).astype(jnp.float32)
    row_pos = (anchor[1] + jnp.arange(CH, dtype=jnp.int32)).astype(jnp.float32)
    column_pos = (anchor[2] + jnp.arange(CW, dtype=jnp.int32)).astype(jnp.float32)
    grid = (CT, CH, CW, D)
    normed = modulate(tokens, modulation)
    flat = normed.reshape(-1, D)
    key = rms_gain(jnp.dot(flat, w_key, preferred_element_type=jnp.float32), norm_k).reshape(grid)
    key = rotate_pairs(key, frame_pos, row_pos, column_pos).astype(jnp.bfloat16)
    value = (
        jnp.dot(flat, w_value, preferred_element_type=jnp.float32)
        .astype(jnp.bfloat16)
        .reshape(grid)
    )
    key_value = jnp.stack([key, value])
    framed = with_halo(key_value, (("ta", 1),), TT)
    padded = with_halo(framed, (("ha", 2), ("wa", 3)), TW)
    query = rms_gain(jnp.dot(flat, w_query, preferred_element_type=jnp.float32), norm_q).reshape(
        grid
    )
    query = rotate_pairs(query, frame_pos, row_pos, column_pos).astype(jnp.bfloat16)
    attended = tile_rows(query, padded[0], padded[1], anchor, extent)
    branch = (
        jnp.dot(attended.reshape(-1, D), w_out, preferred_element_type=jnp.float32) * modulation[2]
    )
    return branch.astype(jnp.bfloat16).reshape(grid)


TILE = TT * TH * TW
GROUPS = 4
GH = HEADS // GROUPS
GW = GH * HEAD_DIM
SCORE_SCALE = float(HEAD_DIM ** (-0.5) * np.log2(np.e))


def rope_tables(devices, per_device, low, count):
    n = np.float32(count)
    freq = np.float32(10000.0) ** (-np.arange(count, dtype=np.float32) / n)
    angle = np.arange(devices * per_device, dtype=np.float32)[:, None] * freq[None, :]
    cosine = np.zeros((devices * per_device, HEAD_DIM), np.float32)
    sine = np.zeros((devices * per_device, HEAD_DIM), np.float32)
    for j in range(count):
        lane = 2 * (low + j)
        cosine[:, lane] = cosine[:, lane + 1] = np.cos(angle[:, j])
        sine[:, lane] = -np.sin(angle[:, j])
        sine[:, lane + 1] = np.sin(angle[:, j])
    tables = np.stack([cosine, sine]).reshape(2, devices, per_device, HEAD_DIM)
    return jnp.asarray(tables.transpose(1, 0, 2, 3))


def layer_norm(tokens, mod_ref):
    values = tokens.astype(jnp.float32)
    center = values - jnp.mean(values, axis=-1, keepdims=True)
    spread = jnp.mean(center * center, axis=-1, keepdims=True)
    shift, scale = mod_ref[0:1, :], mod_ref[1:2, :]
    return (center * lax.rsqrt(spread + 1e-06) * (1.0 + scale) + shift).astype(jnp.bfloat16)


def angle_tables(place, ft_ref, rt_ref, ct_ref):
    out = []
    for kind in range(2):
        frame = ft_ref[place[0], kind]
        row = rt_ref[place[1], kind]
        column = ct_ref[place[2], kind]
        full = frame[:, None, None, :] + row[None, :, None, :] + column[None, None, :, :]
        out.append(full.reshape(TILE, HEAD_DIM))
    return out


def rope(x, cosine, sine, even):
    swapped = jnp.where(even, pltpu.roll(x, HEAD_DIM - 1, 1), pltpu.roll(x, 1, 1))
    return x * cosine + swapped * sine


def fold_squares(prod):
    total = None
    for h in range(GH):
        piece = prod[:, h * HEAD_DIM : (h + 1) * HEAD_DIM]
        total = piece * piece if total is None else total + piece * piece
    return total


def group_of(sc_ref, m):
    return pl.multiple_of((sc_ref[0] ^ m) * GW, GW)


def finish_normed(sc_ref, tables, buf, gain_ref, ssq, write):
    cosine, sine = angle_tables((sc_ref[1], sc_ref[2], sc_ref[3]), *tables)
    even = lax.broadcasted_iota(jnp.int32, (TILE, HEAD_DIM), 1) % 2 == 0
    inv = lax.rsqrt(jnp.sum(ssq, axis=-1, keepdims=True) / D + 1e-06)
    for m in range(GROUPS):
        gain = gain_ref[:, pl.ds(group_of(sc_ref, m), GW)]
        for h in range(GH):
            lanes = slice(h * HEAD_DIM, (h + 1) * HEAD_DIM)
            x = buf[m, :, lanes] * inv * gain[:, lanes]
            write(m, h, rope(x, cosine, sine, even).astype(jnp.bfloat16))


def kv_kernel(sc_ref, tok_hbm, mod_hbm, nk_hbm, ft_hbm, rt_hbm, ct_hbm, wk_hbm, wv_hbm, *refs):
    outs, normed_ref, (tok_ref, mod_ref, nk_ref, ft_ref, rt_ref, ct_ref, wbuf, buf, gain_ref, sems) = refs[:4], refs[4], refs[5:]
    small = [
        pltpu.make_async_copy(source, target, sems.at[2, n])
        for n, (source, target) in enumerate(
            zip((tok_hbm, mod_hbm, nk_hbm, ft_hbm, rt_hbm, ct_hbm), (tok_ref, mod_ref, nk_ref, ft_ref, rt_ref, ct_ref))
        )
    ]
    for copy in small:
        copy.start()
    copies = []
    for kind, w_hbm in enumerate((wk_hbm, wv_hbm)):
        for m in range(GROUPS):
            copies.append(
                pltpu.make_async_copy(
                    w_hbm.at[:, pl.ds(group_of(sc_ref, m), GW)], wbuf.at[kind, m], sems.at[kind, m]
                )
            )
            copies[-1].start()
    for copy in small:
        copy.wait()
    gain_ref[...] = nk_ref[...].reshape(1, D)
    normed = layer_norm(tok_ref[...], mod_ref)
    normed_ref[...] = normed
    ssq = None
    for m in range(GROUPS):
        copies[m].wait()
        prod = jnp.dot(normed, wbuf[0, m], preferred_element_type=jnp.float32)
        buf[m] = prod
        squares = fold_squares(prod)
        ssq = squares if ssq is None else ssq + squares

    def write(m, h, x):
        outs[m][0, h] = x

    finish_normed(sc_ref, (ft_ref, rt_ref, ct_ref), buf, gain_ref, ssq, write)
    for m in range(GROUPS):
        copies[GROUPS + m].wait()
        prod = jnp.dot(normed, wbuf[1, m], preferred_element_type=jnp.float32)
        for h in range(GH):
            outs[m][1, h] = prod[:, h * HEAD_DIM : (h + 1) * HEAD_DIM].astype(jnp.bfloat16)


def q_kernel(sc_ref, normed_ref, nq_ref, ft_ref, rt_ref, ct_ref, wq_ref, o0, o1, o2, o3, buf, gain_ref):
    outs = (o0, o1, o2, o3)
    gain_ref[...] = nq_ref[...].reshape(1, D)
    ssq = None
    for m in range(GROUPS):
        prod = jnp.dot(
            normed_ref[...], wq_ref[:, pl.ds(group_of(sc_ref, m), GW)], preferred_element_type=jnp.float32
        )
        buf[m] = prod
        squares = fold_squares(prod)
        ssq = squares if ssq is None else ssq + squares

    def write(m, h, x):
        outs[m][h] = x

    finish_normed(sc_ref, (ft_ref, rt_ref, ct_ref), buf, gain_ref, ssq, write)


SMEM = pl.BlockSpec(memory_space=pltpu.SMEM)
VMEM = pl.BlockSpec(memory_space=pltpu.VMEM)
HBM = pl.BlockSpec(memory_space=pl.ANY)


def limit(mib):
    return pltpu.CompilerParams(vmem_limit_bytes=mib * 1024 * 1024)


def project_kv(sc, tokens, modulation, norm_k, tables, w_key, w_value):
    kv_shape = (2, GH, TILE, HEAD_DIM)
    return pl.pallas_call(
        kv_kernel,
        in_specs=[SMEM] + [HBM] * 8,
        out_specs=[VMEM] * (GROUPS + 1),
        scratch_shapes=[
            pltpu.VMEM((TILE, D), jnp.bfloat16),
            pltpu.VMEM((3, D), jnp.float32),
            pltpu.VMEM((D,), jnp.float32),
            *[pltpu.VMEM(t.shape, jnp.float32) for t in tables],
            pltpu.VMEM((2, GROUPS, D, GW), jnp.bfloat16),
            pltpu.VMEM((GROUPS, TILE, GW), jnp.float32),
            pltpu.VMEM((1, D), jnp.float32),
            pltpu.SemaphoreType.DMA((3, 6)),
        ],
        out_shape=[jax.ShapeDtypeStruct(kv_shape, jnp.bfloat16)] * GROUPS
        + [jax.ShapeDtypeStruct((TILE, D), jnp.bfloat16)],
        compiler_params=limit(60),
        cost_estimate=pl.CostEstimate(flops=4 * TILE * D * D, bytes_accessed=4 * D * D, transcendentals=0),
        name="project_kv",
    )(sc, tokens, modulation, norm_k, *tables, w_key, w_value)


def project_q(sc, normed, norm_q, tables, w_query):
    q_shape = (GH, TILE, HEAD_DIM)
    return pl.pallas_call(
        q_kernel,
        in_specs=[SMEM] + [VMEM] * 6,
        out_specs=[VMEM] * GROUPS,
        scratch_shapes=[pltpu.VMEM((GROUPS, TILE, GW), jnp.float32), pltpu.VMEM((1, D), jnp.float32)],
        out_shape=[jax.ShapeDtypeStruct(q_shape, jnp.bfloat16)] * GROUPS,
        compiler_params=limit(20),
        cost_estimate=pl.CostEstimate(flops=2 * TILE * D * D, bytes_accessed=2 * D * D, transcendentals=0),
        name="project_q",
    )(sc, normed, norm_q, *tables, w_query)


def query_of(refs, s):
    return jnp.concatenate([refs[2 * s][0], refs[2 * s + 1][0]], axis=0)


def raw_scores(query, keys):
    return lax.dot_general(query, keys, (((1,), (1,)), ((), ())), preferred_element_type=jnp.float32)


def weigh(scores, peak, values):
    expo = jnp.exp2((scores - peak) * SCORE_SCALE).astype(jnp.bfloat16)
    ones = jnp.ones((values.shape[0], HEAD_DIM), jnp.bfloat16)
    both = jnp.dot(expo, jnp.concatenate([values, ones], axis=1), preferred_element_type=jnp.float32)
    return both[:, :HEAD_DIM], both[:, HEAD_DIM:]


def attend(query, segments, state=None):
    scores = [raw_scores(query, keys) for keys, _, _ in segments]
    found = [jnp.max(s, axis=-1, keepdims=True) for s in scores]
    found = [f if there is None else jnp.where(there, f, -1e30) for f, (_, _, there) in zip(found, segments)]
    peak = functools.reduce(jnp.maximum, found if state is None else [state[0], *found])
    total = norm = None
    if state is not None:
        decay = jnp.exp2((state[0] - peak) * SCORE_SCALE)
        total, norm = state[1] * decay, state[2] * decay
    for s, (_, values, there) in zip(scores, segments):
        part, weight = weigh(s, peak if there is None else jnp.where(there, peak, 1e30), values)
        total, norm = (part, weight) if total is None else (total + part, norm + weight)
    return peak, total, norm


def stack_keys(slots, kind):
    return jnp.concatenate([ref[kind, 0] for pair in slots for ref in pair], axis=0)


def segment(slots, there):
    return stack_keys(slots, 0), stack_keys(slots, 1), there


def first_kernel(sc_ref, *refs):
    q = refs[0:4]
    same, other = [refs[4:6], refs[6:8]], [refs[8:10], refs[10:12]]
    rows = [(refs[12 + 4 * r : 14 + 4 * r], refs[14 + 4 * r : 16 + 4 * r], sc_ref[5 + r] == 1) for r in range(2)]
    stat_ref, acc_ref = refs[20:]
    low = lax.broadcasted_iota(jnp.int32, (2 * TILE, HEAD_DIM), 1) < HEAD_DIM // 2

    def store(s, state):
        peak, total, norm = state
        acc_ref[0, s] = total
        stat_ref[0, s] = jnp.where(low, peak, norm)

    halo = [segment([mine, theirs], there) for mine, theirs, there in rows]

    @pl.when(sc_ref[4] == 0)
    def _():
        store(0, attend(query_of(q, 0), [segment([same[0], other[0], other[1]], None), *halo]))
        store(1, attend(query_of(q, 1), [segment([same[1], other[1]], None)]))

    @pl.when(sc_ref[4] == 1)
    def _():
        store(0, attend(query_of(q, 0), [segment([same[0], other[0]], None), *halo]))
        far = [segment([theirs], there) for _, theirs, there in rows]
        store(1, attend(query_of(q, 1), [segment([same[1], other[1], other[0]], None), *far]))


def last_kernel(sc_ref, *refs):
    q = refs[0:4]
    rows = [(refs[4 + 4 * r : 6 + 4 * r], refs[6 + 4 * r : 8 + 4 * r], sc_ref[5 + r] == 1) for r in range(2)]
    stat_in, acc_in = refs[12:14]
    outs = refs[14:18]

    def state(s):
        stat = stat_in[0, s]
        return stat[:, :1], acc_in[0, s], stat[:, HEAD_DIM // 2 : HEAD_DIM // 2 + 1]

    def write(s, result):
        attended = (result[1] / result[2]).astype(jnp.bfloat16)
        outs[2 * s][0] = attended[:TILE]
        outs[2 * s + 1][0] = attended[TILE:]

    @pl.when(sc_ref[4] == 0)
    def _():
        write(0, attend(query_of(q, 0), [segment([theirs], there) for _, theirs, there in rows], state(0)))

    @pl.when(sc_ref[4] == 1)
    def _():
        write(0, state(0))

    write(1, attend(query_of(q, 1), [segment([mine, theirs], there) for mine, theirs, there in rows], state(1)))


Q_SPEC = pl.BlockSpec((1, TILE, HEAD_DIM), lambda h, sc: (h, 0, 0))
KV_SPEC = pl.BlockSpec((2, 1, TILE, HEAD_DIM), lambda h, sc: (0, h, 0, 0))
STATE_SPEC = pl.BlockSpec((1, 2, 2 * TILE, HEAD_DIM), lambda h, sc: (h, 0, 0, 0))
STATE_SHAPE = jax.ShapeDtypeStruct((GH, 2, 2 * TILE, HEAD_DIM), jnp.float32)


def attend_cost(blocks):
    pairs = GH * blocks * 4 * TILE * TILE
    return pl.CostEstimate(flops=4 * pairs * HEAD_DIM, bytes_accessed=12 * TILE * GW * 2, transcendentals=pairs)


def attend_first(sc, queries, tiles):
    return pl.pallas_call(
        first_kernel,
        grid_spec=pltpu.PrefetchScalarGridSpec(
            num_scalar_prefetch=1,
            grid=(GH,),
            in_specs=[Q_SPEC] * 4 + [KV_SPEC] * 16,
            out_specs=[STATE_SPEC] * 2,
        ),
        out_shape=[STATE_SHAPE] * 2,
        compiler_params=limit(32),
        cost_estimate=attend_cost(10),
        name="attend_first",
    )(sc, *queries, *tiles)


def attend_last(sc, queries, tiles, state):
    return pl.pallas_call(
        last_kernel,
        grid_spec=pltpu.PrefetchScalarGridSpec(
            num_scalar_prefetch=1,
            grid=(GH,),
            in_specs=[Q_SPEC] * 4 + [KV_SPEC] * 8 + [STATE_SPEC] * 2,
            out_specs=[Q_SPEC] * GROUPS,
        ),
        out_shape=[jax.ShapeDtypeStruct((GH, TILE, HEAD_DIM), jnp.bfloat16)] * GROUPS,
        compiler_params=limit(32),
        cost_estimate=attend_cost(5),
        name="attend_last",
    )(sc, *queries, *tiles, *state)


def out_kernel(sc_ref, a0, a1, a2, a3, mod_ref, w_ref, out_ref):
    total = None
    for m, ref in enumerate((a0, a1, a2, a3)):
        rows = jnp.concatenate([ref[h] for h in range(GH)], axis=1)
        part = jnp.dot(rows, w_ref[pl.ds(group_of(sc_ref, m), GW), :], preferred_element_type=jnp.float32)
        total = part if total is None else total + part
    out_ref[...] = (total * mod_ref[2:3, :]).astype(jnp.bfloat16)


def project_out(sc, attended, modulation, w_out):
    return pl.pallas_call(
        out_kernel,
        in_specs=[SMEM] + [VMEM] * 6,
        out_specs=VMEM,
        out_shape=jax.ShapeDtypeStruct((TILE, D), jnp.bfloat16),
        compiler_params=limit(20),
        cost_estimate=pl.CostEstimate(flops=2 * TILE * D * D, bytes_accessed=2 * D * D, transcendentals=0),
        name="project_out",
    )(sc, *attended, modulation, w_out)


def square_swap(value, m):
    if m == 0:
        return value
    flip = (m >> 1) * 4 + (m & 1)
    return lax.ppermute(value, ("ta", "wa"), [(i, i ^ flip) for i in range(8)])


def core_swap(value):
    return lax.ppermute(value, "ta", [(i, i ^ 1) for i in range(4)])


def square_body(tokens, modulation, w_query, w_key, w_value, w_out, norm_q, norm_k):
    ta, ha, wa = (lax.axis_index(name) for name in ("ta", "ha", "wa"))
    rows_n = lax.axis_size("ha")
    place_x, core = ta // 2, ta % 2
    near_slot = 1 - (place_x ^ core)
    sc = jnp.stack(
        [2 * place_x + wa, ta, ha, wa, near_slot, (ha > 0).astype(jnp.int32), (ha < rows_n - 1).astype(jnp.int32)]
    ).astype(jnp.int32)
    half, sixth = HEAD_DIM // 2, HEAD_DIM // 6
    first = half - 2 * sixth
    tables = (
        rope_tables(lax.axis_size("ta"), CT, 0, first),
        rope_tables(rows_n, CH, first, sixth),
        rope_tables(lax.axis_size("wa"), CW, first + sixth, sixth),
    )
    *kv, normed = project_kv(sc, tokens.reshape(TILE, D), modulation, norm_k, tables, w_key, w_value)
    up = [(i, i + 1) for i in range(rows_n - 1)]
    down = [(i + 1, i) for i in range(rows_n - 1)]
    def rows_of(tile):
        return lax.ppermute(tile, "ha", up), lax.ppermute(tile, "ha", down)

    def after(value, *others):
        return lax.optimization_barrier((value, *others))[0]

    same = [kv[0], square_swap(kv[1], 1), square_swap(kv[2], 2)]
    halo = [rows_of(tile) for tile in same]
    same.append(square_swap(after(kv[3], same[1], same[2]), 3))
    halo.append(rows_of(same[3]))
    queries = project_q(sc, after(normed, same[1]), norm_q, tables, w_query)
    queries = [square_swap(queries[m], m) for m in range(GROUPS)]
    other = [core_swap(tile) for tile in same]
    halo_other = [[core_swap(tile) for tile in pair] for pair in halo]

    def halo_slot(slot):
        return [part[m][r] for r in range(2) for part in (halo, halo_other) for m in (2 * slot, 2 * slot + 1)]

    state = attend_first(sc, queries, [*same, *other, *halo_slot(0)])
    attended = attend_last(sc, queries, halo_slot(1), state)
    attended = [square_swap(attended[m], m) for m in range(GROUPS)]
    branch = project_out(sc, attended, modulation, w_out)
    return branch.reshape(CT, CH, CW, D)


def solution(mesh):
    square = mesh.shape["ta"] == 4 and mesh.shape["wa"] == 2
    chosen = square_body if square else body
    in_specs = (P("ta", "ha", "wa", None), P(), P(), P(), P(), P(), P(), P())
    out_specs = P("ta", "ha", "wa", None)
    return jax.shard_map(chosen, mesh=mesh, in_specs=in_specs, out_specs=out_specs, check_vma=False)
```

```python
import functools

import jax
import jax.numpy as jnp
import numpy as np
from jax import lax
from jax.experimental import pallas as pl
from jax.experimental.pallas import tpu as pltpu
from jax.sharding import PartitionSpec as P

HEADS = 12
HEAD_DIM = 128
D = 1536
TT = 3
TH = 8
TW = 8
CT = 3
CH = 8
CW = 8


def with_halo(value, sides, width):
    for axis, dim in sides:
        devices, length = (lax.axis_size(axis), value.shape[dim])
        up = [(i, (i + 1) % devices) for i in range(devices - 1)]
        down = [(j, i) for i, j in up]
        last = lax.slice_in_dim(value, length - width, length, axis=dim)
        first = lax.slice_in_dim(value, 0, width, axis=dim)
        before = lax.ppermute(last, axis, up)
        after = lax.ppermute(first, axis, down)
        value = jnp.concatenate([before, value, after], axis=dim)
    return value


def modulate(tokens, modulation):
    values = tokens.astype(jnp.float32)
    center = values - jnp.mean(values, axis=-1, keepdims=True)
    spread = jnp.mean(center * center, axis=-1, keepdims=True)
    return (center * lax.rsqrt(spread + 1e-06) * (1.0 + modulation[1]) + modulation[0]).astype(
        jnp.bfloat16
    )


def rms_gain(values, gain):
    return values * lax.rsqrt(jnp.mean(values * values, axis=-1, keepdims=True) + 1e-06) * gain


def rotate_pairs(values, frame_pos, row_pos, column_pos):
    half = HEAD_DIM // 2
    sixth = HEAD_DIM // 6
    first = half - 2 * sixth
    freq_first = 10000.0 ** (-jnp.arange(first, dtype=jnp.float32) / first)
    freq_rest = 10000.0 ** (-jnp.arange(sixth, dtype=jnp.float32) / sixth)
    shape = values.shape[:3]
    angle_frame = frame_pos[:, None] * freq_first
    angle_row = row_pos[:, None] * freq_rest
    angle_column = column_pos[:, None] * freq_rest
    angles = jnp.concatenate(
        [
            jnp.broadcast_to(angle_frame[:, None, None, :], shape + (first,)),
            jnp.broadcast_to(angle_row[None, :, None, :], shape + (sixth,)),
            jnp.broadcast_to(angle_column[None, None, :, :], shape + (sixth,)),
        ],
        axis=-1,
    )
    cosine = jnp.cos(angles)[:, :, :, None, :]
    sine = jnp.sin(angles)[:, :, :, None, :]
    pairs = values.reshape(shape + (HEADS, half, 2))
    even_part = pairs[..., 0]
    odd_part = pairs[..., 1]
    rotated = jnp.stack(
        [even_part * cosine - odd_part * sine, even_part * sine + odd_part * cosine], axis=-1
    )
    return rotated.reshape(values.shape)


def tile_rows(query, key_pad, value_pad, anchor, extent):
    tile_frames = CT // TT
    tile_rows_n = CH // TH
    tile_columns = CW // TW
    tile_size = TT * TH * TW
    window = 27 * tile_size

    def one_row(index):
        frame_tile = index // tile_rows_n
        row_tile = index % tile_rows_n
        query_row = query
        query_row = query_row.reshape(TT, TH, tile_columns, TW, HEADS, HEAD_DIM).transpose(
            4, 2, 0, 1, 3, 5
        )
        query_row = query_row.reshape(HEADS, tile_columns, tile_size, HEAD_DIM)
        key_tiles = jnp.stack([key_pad])
        value_tiles = jnp.stack([value_pad])
        key_tiles = key_tiles.reshape(tile_columns, window, HEADS, HEAD_DIM).transpose(2, 0, 1, 3)
        value_tiles = value_tiles.reshape(tile_columns, window, HEADS, HEAD_DIM).transpose(
            2, 0, 1, 3
        )
        frames_at = anchor[0] + frame_tile * TT - TT + jnp.arange(3 * TT, dtype=jnp.int32)
        rows_at = anchor[1] + row_tile * TH - TH + jnp.arange(3 * TH, dtype=jnp.int32)
        columns_at = (
            anchor[2]
            + jnp.arange(tile_columns, dtype=jnp.int32)[:, None] * TW
            - TW
            + jnp.arange(3 * TW, dtype=jnp.int32)[None, :]
        )
        frame_ok = (frames_at >= 0) & (frames_at < extent[0])
        row_ok = (rows_at >= 0) & (rows_at < extent[1])
        column_ok = (columns_at >= 0) & (columns_at < extent[2])
        valid = (
            frame_ok[None, :, None, None]
            & row_ok[None, None, :, None]
            & column_ok[:, None, None, :]
        )
        valid = valid.reshape(tile_columns, window)

        def one_head(operands):
            head_query, head_key, head_value = operands
            scores = jnp.einsum(
                "cqd,ckd->cqk", head_query, head_key, preferred_element_type=jnp.float32
            ) * HEAD_DIM ** (-0.5)
            scores = jnp.where(valid[:, None, :], scores, -1e30)
            peak = jnp.max(scores, axis=-1, keepdims=True)
            expo = jnp.exp(scores - peak)
            weights = (expo / jnp.sum(expo, axis=-1, keepdims=True)).astype(jnp.bfloat16)
            return jnp.einsum(
                "cqk,ckd->cqd", weights, head_value, preferred_element_type=jnp.float32
            ).astype(jnp.bfloat16)

        attended = lax.map(one_head, (query_row, key_tiles, value_tiles))
        attended = attended.reshape(HEADS, tile_columns, TT, TH, TW, HEAD_DIM).transpose(
            2, 3, 1, 4, 0, 5
        )
        return attended.reshape(TT, TH, CW, D)

    result = lax.map(one_row, jnp.arange(tile_frames * tile_rows_n, dtype=jnp.int32))
    result = result.reshape(tile_frames, tile_rows_n, TT, TH, CW, D).transpose(0, 2, 1, 3, 4, 5)
    return result.reshape(CT, CH, CW, D)


def body(tokens, modulation, w_query, w_key, w_value, w_out, norm_q, norm_k):
    anchor = (lax.axis_index("ta") * CT, lax.axis_index("ha") * CH, lax.axis_index("wa") * CW)
    extent = (lax.axis_size("ta") * CT, lax.axis_size("ha") * CH, lax.axis_size("wa") * CW)
    frame_pos = (anchor[0] + jnp.arange(CT, dtype=jnp.int32)).astype(jnp.float32)
    row_pos = (anchor[1] + jnp.arange(CH, dtype=jnp.int32)).astype(jnp.float32)
    column_pos = (anchor[2] + jnp.arange(CW, dtype=jnp.int32)).astype(jnp.float32)
    grid = (CT, CH, CW, D)
    normed = modulate(tokens, modulation)
    flat = normed.reshape(-1, D)
    key = rms_gain(jnp.dot(flat, w_key, preferred_element_type=jnp.float32), norm_k).reshape(grid)
    key = rotate_pairs(key, frame_pos, row_pos, column_pos).astype(jnp.bfloat16)
    value = (
        jnp.dot(flat, w_value, preferred_element_type=jnp.float32)
        .astype(jnp.bfloat16)
        .reshape(grid)
    )
    key_value = jnp.stack([key, value])
    framed = with_halo(key_value, (("ta", 1),), TT)
    padded = with_halo(framed, (("ha", 2), ("wa", 3)), TW)
    query = rms_gain(jnp.dot(flat, w_query, preferred_element_type=jnp.float32), norm_q).reshape(
        grid
    )
    query = rotate_pairs(query, frame_pos, row_pos, column_pos).astype(jnp.bfloat16)
    attended = tile_rows(query, padded[0], padded[1], anchor, extent)
    branch = (
        jnp.dot(attended.reshape(-1, D), w_out, preferred_element_type=jnp.float32) * modulation[2]
    )
    return branch.astype(jnp.bfloat16).reshape(grid)


TILE = TT * TH * TW
GROUPS = 4
GH = HEADS // GROUPS
GW = GH * HEAD_DIM
SCORE_SCALE = float(HEAD_DIM ** (-0.5) * np.log2(np.e))


def rope_tables(devices, per_device, low, count):
    n = np.float32(count)
    freq = np.float32(10000.0) ** (-np.arange(count, dtype=np.float32) / n)
    angle = np.arange(devices * per_device, dtype=np.float32)[:, None] * freq[None, :]
    cosine = np.zeros((devices * per_device, HEAD_DIM), np.float32)
    sine = np.zeros((devices * per_device, HEAD_DIM), np.float32)
    for j in range(count):
        lane = 2 * (low + j)
        cosine[:, lane] = cosine[:, lane + 1] = np.cos(angle[:, j])
        sine[:, lane] = -np.sin(angle[:, j])
        sine[:, lane + 1] = np.sin(angle[:, j])
    tables = np.stack([cosine, sine]).reshape(2, devices, per_device, HEAD_DIM)
    return jnp.asarray(tables.transpose(1, 0, 2, 3))


def layer_norm(tokens, mod_ref):
    values = tokens.astype(jnp.float32)
    center = values - jnp.mean(values, axis=-1, keepdims=True)
    spread = jnp.mean(center * center, axis=-1, keepdims=True)
    shift, scale = mod_ref[0:1, :], mod_ref[1:2, :]
    return (center * lax.rsqrt(spread + 1e-06) * (1.0 + scale) + shift).astype(jnp.bfloat16)


def angle_tables(place, ft_ref, rt_ref, ct_ref):
    out = []
    for kind in range(2):
        frame = ft_ref[place[0], kind]
        row = rt_ref[place[1], kind]
        column = ct_ref[place[2], kind]
        full = frame[:, None, None, :] + row[None, :, None, :] + column[None, None, :, :]
        out.append(full.reshape(TILE, HEAD_DIM))
    return out


def rope(x, cosine, sine, even):
    swapped = jnp.where(even, pltpu.roll(x, HEAD_DIM - 1, 1), pltpu.roll(x, 1, 1))
    return x * cosine + swapped * sine


def fold_squares(prod):
    total = None
    for h in range(GH):
        piece = prod[:, h * HEAD_DIM : (h + 1) * HEAD_DIM]
        total = piece * piece if total is None else total + piece * piece
    return total


def group_of(sc_ref, m):
    return pl.multiple_of((sc_ref[0] ^ m) * GW, GW)


def finish_normed(sc_ref, tables, buf, gain_ref, ssq, write):
    cosine, sine = angle_tables((sc_ref[1], sc_ref[2], sc_ref[3]), *tables)
    even = lax.broadcasted_iota(jnp.int32, (TILE, HEAD_DIM), 1) % 2 == 0
    inv = lax.rsqrt(jnp.sum(ssq, axis=-1, keepdims=True) / D + 1e-06)
    for m in range(GROUPS):
        gain = gain_ref[:, pl.ds(group_of(sc_ref, m), GW)]
        for h in range(GH):
            lanes = slice(h * HEAD_DIM, (h + 1) * HEAD_DIM)
            x = buf[m, :, lanes] * inv * gain[:, lanes]
            write(m, h, rope(x, cosine, sine, even).astype(jnp.bfloat16))


def start_all(pairs, sems):
    copies = [pltpu.make_async_copy(source, target, sems.at[n]) for n, (source, target) in enumerate(pairs)]
    for copy in copies:
        copy.start()
    return copies


def wait_all(copies):
    for copy in copies:
        copy.wait()


def weight_blocks(sc_ref, w_hbm, wbuf):
    return [(w_hbm.at[:, pl.ds(group_of(sc_ref, m), GW)], wbuf.at[m]) for m in range(GROUPS)]


def project_normed(sc_ref, normed, weights, wbuf, buf, gain_ref, tables, write):
    ssq = None
    for m in range(GROUPS):
        weights[m].wait()
        prod = jnp.dot(normed, wbuf[m], preferred_element_type=jnp.float32)
        buf[m] = prod
        squares = fold_squares(prod)
        ssq = squares if ssq is None else ssq + squares
    finish_normed(sc_ref, tables, buf, gain_ref, ssq, write)


def kv_kernel(sc_ref, tok_hbm, mod_hbm, nk_hbm, ft_hbm, rt_hbm, ct_hbm, wk_hbm, wv_hbm, *refs):
    kv_hbm, normed_hbm, refs = refs[:4], refs[4], refs[5:]
    tok_ref, mod_ref, nk_ref, ft_ref, rt_ref, ct_ref, wk_buf, wv_buf, buf, gain_ref, normed_ref, kv_ref, sems, out_sems = refs
    sources = (tok_hbm, mod_hbm, nk_hbm, ft_hbm, rt_hbm, ct_hbm)
    small = start_all(zip(sources, refs), sems.at[2])
    key_weights = start_all(weight_blocks(sc_ref, wk_hbm, wk_buf), sems.at[0])
    value_weights = start_all(weight_blocks(sc_ref, wv_hbm, wv_buf), sems.at[1])
    wait_all(small)
    gain_ref[...] = nk_ref[...].reshape(1, D)
    normed = layer_norm(tok_ref[...], mod_ref)
    normed_ref[...] = normed
    results = start_all([(normed_ref, normed_hbm)], out_sems.at[2])

    def write(m, h, x):
        kv_ref[m, 0, h] = x

    project_normed(sc_ref, normed, key_weights, wk_buf, buf, gain_ref, (ft_ref, rt_ref, ct_ref), write)
    results += start_all([(kv_ref.at[m, 0], kv_hbm[m].at[0]) for m in range(GROUPS)], out_sems.at[0])
    for m in range(GROUPS):
        value_weights[m].wait()
        prod = jnp.dot(normed, wv_buf[m], preferred_element_type=jnp.float32)
        for h in range(GH):
            kv_ref[m, 1, h] = prod[:, h * HEAD_DIM : (h + 1) * HEAD_DIM].astype(jnp.bfloat16)
        results.append(pltpu.make_async_copy(kv_ref.at[m, 1], kv_hbm[m].at[1], out_sems.at[1, m]))
        results[-1].start()
    wait_all(results)


def q_kernel(sc_ref, normed_hbm, nq_hbm, ft_hbm, rt_hbm, ct_hbm, wq_hbm, *refs):
    q_hbm, refs = refs[:4], refs[4:]
    normed_ref, nq_ref, ft_ref, rt_ref, ct_ref, wq_buf, buf, gain_ref, q_ref, sems, out_sems = refs
    small = start_all(zip((normed_hbm, nq_hbm, ft_hbm, rt_hbm, ct_hbm), refs), sems.at[1])
    weights = start_all(weight_blocks(sc_ref, wq_hbm, wq_buf), sems.at[0])
    wait_all(small)
    gain_ref[...] = nq_ref[...].reshape(1, D)

    def write(m, h, x):
        q_ref[m, h] = x

    project_normed(sc_ref, normed_ref[...], weights, wq_buf, buf, gain_ref, (ft_ref, rt_ref, ct_ref), write)
    wait_all(start_all([(q_ref.at[m], q_hbm[m]) for m in range(GROUPS)], out_sems))


SMEM = pl.BlockSpec(memory_space=pltpu.SMEM)
VMEM = pl.BlockSpec(memory_space=pltpu.VMEM)
HBM = pl.BlockSpec(memory_space=pl.ANY)


def limit(mib):
    return pltpu.CompilerParams(vmem_limit_bytes=mib * 1024 * 1024)


KV_SHAPE = (2, GH, TILE, HEAD_DIM)
Q_SHAPE = (GH, TILE, HEAD_DIM)


def project_kv(sc, tokens, modulation, norm_k, tables, w_key, w_value):
    return pl.pallas_call(
        kv_kernel,
        in_specs=[SMEM] + [HBM] * 8,
        out_specs=[HBM] * (GROUPS + 1),
        scratch_shapes=[
            pltpu.VMEM((TILE, D), jnp.bfloat16),
            pltpu.VMEM((3, D), jnp.float32),
            pltpu.VMEM((D,), jnp.float32),
            *[pltpu.VMEM(t.shape, jnp.float32) for t in tables],
            pltpu.VMEM((GROUPS, D, GW), jnp.bfloat16),
            pltpu.VMEM((GROUPS, D, GW), jnp.bfloat16),
            pltpu.VMEM((GROUPS, TILE, GW), jnp.float32),
            pltpu.VMEM((1, D), jnp.float32),
            pltpu.VMEM((TILE, D), jnp.bfloat16),
            pltpu.VMEM((GROUPS, *KV_SHAPE), jnp.bfloat16),
            pltpu.SemaphoreType.DMA((3, 6)),
            pltpu.SemaphoreType.DMA((3, GROUPS)),
        ],
        out_shape=[jax.ShapeDtypeStruct(KV_SHAPE, jnp.bfloat16)] * GROUPS
        + [jax.ShapeDtypeStruct((TILE, D), jnp.bfloat16)],
        compiler_params=limit(60),
        cost_estimate=pl.CostEstimate(flops=4 * TILE * D * D, bytes_accessed=4 * D * D, transcendentals=0),
        name="project_kv",
    )(sc, tokens, modulation, norm_k, *tables, w_key, w_value)


def project_q(sc, normed, norm_q, tables, w_query):
    return pl.pallas_call(
        q_kernel,
        in_specs=[SMEM] + [HBM] * 6,
        out_specs=[HBM] * GROUPS,
        scratch_shapes=[
            pltpu.VMEM((TILE, D), jnp.bfloat16),
            pltpu.VMEM((D,), jnp.float32),
            *[pltpu.VMEM(t.shape, jnp.float32) for t in tables],
            pltpu.VMEM((GROUPS, D, GW), jnp.bfloat16),
            pltpu.VMEM((GROUPS, TILE, GW), jnp.float32),
            pltpu.VMEM((1, D), jnp.float32),
            pltpu.VMEM((GROUPS, *Q_SHAPE), jnp.bfloat16),
            pltpu.SemaphoreType.DMA((2, 5)),
            pltpu.SemaphoreType.DMA((GROUPS,)),
        ],
        out_shape=[jax.ShapeDtypeStruct(Q_SHAPE, jnp.bfloat16)] * GROUPS,
        compiler_params=limit(60),
        cost_estimate=pl.CostEstimate(flops=2 * TILE * D * D, bytes_accessed=2 * D * D, transcendentals=0),
        name="project_q",
    )(sc, normed, norm_q, *tables, w_query)


def query_of(refs, s, h):
    return jnp.concatenate([refs[2 * s][h], refs[2 * s + 1][h]], axis=0)


def raw_scores(query, keys):
    return lax.dot_general(query, keys, (((1,), (1,)), ((), ())), preferred_element_type=jnp.float32)


def weigh(scores, peak, values):
    expo = jnp.exp2((scores - peak) * SCORE_SCALE).astype(jnp.bfloat16)
    ones = jnp.ones((values.shape[0], HEAD_DIM), jnp.bfloat16)
    both = jnp.dot(expo, jnp.concatenate([values, ones], axis=1), preferred_element_type=jnp.float32)
    return both[:, :HEAD_DIM], both[:, HEAD_DIM:]


def attend(query, segments, state=None):
    scores = [raw_scores(query, keys) for keys, _, _ in segments]
    found = [jnp.max(s, axis=-1, keepdims=True) for s in scores]
    found = [f if there is None else jnp.where(there, f, -1e30) for f, (_, _, there) in zip(found, segments)]
    peak = functools.reduce(jnp.maximum, found if state is None else [state[0], *found])
    total = norm = None
    if state is not None:
        decay = jnp.exp2((state[0] - peak) * SCORE_SCALE)
        total, norm = state[1] * decay, state[2] * decay
    for s, (_, values, there) in zip(scores, segments):
        part, weight = weigh(s, peak if there is None else jnp.where(there, peak, 1e30), values)
        total, norm = (part, weight) if total is None else (total + part, norm + weight)
    return peak, total, norm


def stack_keys(slots, kind, h):
    return jnp.concatenate([ref[kind, h] for pair in slots for ref in pair], axis=0)


def segment(slots, there, h):
    return stack_keys(slots, 0, h), stack_keys(slots, 1, h), there


def attend_kernel(plan, tile_places, state_slots, final, sc_ref, *refs):
    q, refs = refs[:4], refs[4:]
    tiles = {}
    for name, places in tile_places:
        tiles[name] = [ref if place is None else ref.at[place] for ref, place in zip(refs, places)]
        refs = refs[2:]
    state_in = {s: refs[2 * n : 2 * n + 2] for n, s in enumerate(state_slots)}
    refs = refs[2 * len(state_slots) :]
    low = lax.broadcasted_iota(jnp.int32, (2 * TILE, HEAD_DIM), 1) < HEAD_DIM // 2

    def state(s, h):
        if s not in state_in:
            return None
        stat = state_in[s][0][h]
        return stat[:, :1], state_in[s][1][h], stat[:, HEAD_DIM // 2 : HEAD_DIM // 2 + 1]

    def one_head(slots, h):
        for n, s in enumerate(sorted(slots)):
            segments = [
                segment([tiles[name] for name in names], None if row is None else sc_ref[5 + row] == 1, h)
                for names, row in slots[s]
            ]
            peak, total, norm = attend(query_of(q, s, h), segments, state(s, h)) if segments else state(s, h)
            if final:
                attended = (total / norm).astype(jnp.bfloat16)
                refs[2 * s][h] = attended[:TILE]
                refs[2 * s + 1][h] = attended[TILE:]
            else:
                refs[2 * n][h] = jnp.where(low, peak, norm)
                refs[2 * n + 1][h] = total

    def run(slots):
        for h in range(GH):
            one_head(slots, h)
    if plan[0] == plan[1]:
        run(plan[0])
    else:
        for near in range(2):
            pl.when(sc_ref[4] == near)(functools.partial(run, plan[near]))


STATE_SHAPE = jax.ShapeDtypeStruct((GH, 2 * TILE, HEAD_DIM), jnp.float32)


def attend_call(name, plan, sc, queries, tiles, state):
    final = name == "attend_last"
    state_slots = sorted(state)
    places = tuple((key, tuple(place for _, place in pair)) for key, pair in tiles.items())
    arrays = [array for pair in tiles.values() for array, _ in pair]
    states = [array for s in state_slots for array in state[s]]
    return pl.pallas_call(
        functools.partial(attend_kernel, plan, places, tuple(state_slots), final),
        in_specs=[SMEM] + [VMEM] * (GROUPS + len(arrays) + len(states)),
        out_specs=[VMEM] * 4,
        out_shape=[jax.ShapeDtypeStruct(Q_SHAPE, jnp.bfloat16) if final else STATE_SHAPE] * 4,
        compiler_params=limit(32),
        cost_estimate=pl.CostEstimate(flops=1000, bytes_accessed=1000, transcendentals=0),
        name=name,
    )(sc, *queries, *arrays, *states)


def out_kernel(sc_ref, a0, a1, a2, a3, mod_ref, w_ref, out_ref):
    total = None
    for m, ref in enumerate((a0, a1, a2, a3)):
        rows = jnp.concatenate([ref[h] for h in range(GH)], axis=1)
        part = jnp.dot(rows, w_ref[pl.ds(group_of(sc_ref, m), GW), :], preferred_element_type=jnp.float32)
        total = part if total is None else total + part
    out_ref[...] = (total * mod_ref[2:3, :]).astype(jnp.bfloat16)


def project_out(sc, attended, modulation, w_out):
    return pl.pallas_call(
        out_kernel,
        in_specs=[SMEM] + [VMEM] * 6,
        out_specs=VMEM,
        out_shape=jax.ShapeDtypeStruct((TILE, D), jnp.bfloat16),
        compiler_params=limit(20),
        cost_estimate=pl.CostEstimate(flops=2 * TILE * D * D, bytes_accessed=2 * D * D, transcendentals=0),
        name="project_out",
    )(sc, *attended, modulation, w_out)


def square_swap(value, m):
    if m == 0:
        return value
    flip = (m >> 1) * 4 + (m & 1)
    return lax.ppermute(value, ("ta", "wa"), [(i, i ^ flip) for i in range(8)])


def core_swap(value):
    return lax.ppermute(value, "ta", [(i, i ^ 1) for i in range(4)])


def row_swap(value, first, rows_n):
    pairs = [(i, i + 1) for i in range(first, rows_n - 1, 2)]
    return lax.ppermute(value, "ha", [edge for i, j in pairs for edge in ((i, j), (j, i))])


def after(value, *others):
    return lax.optimization_barrier((value, *others))[0]


def square_body(tokens, modulation, w_query, w_key, w_value, w_out, norm_q, norm_k):
    ta, ha, wa = (lax.axis_index(name) for name in ("ta", "ha", "wa"))
    rows_n = lax.axis_size("ha")
    place_x, core = ta // 2, ta % 2
    near_slot = 1 - (place_x ^ core)
    partner = [ha + 1 - 2 * (ha % 2), ha - 1 + 2 * (ha % 2)]
    sc = jnp.stack(
        [2 * place_x + wa, ta, ha, wa, near_slot, *[((p >= 0) & (p < rows_n)).astype(jnp.int32) for p in partner]]
    ).astype(jnp.int32)
    half, sixth = HEAD_DIM // 2, HEAD_DIM // 6
    first = half - 2 * sixth
    tables = (
        rope_tables(lax.axis_size("ta"), CT, 0, first),
        rope_tables(rows_n, CH, first, sixth),
        rope_tables(lax.axis_size("wa"), CW, first + sixth, sixth),
    )
    *kv, normed = project_kv(sc, tokens.reshape(TILE, D), modulation, norm_k, tables, w_key, w_value)

    def rows_of(tile):
        return [row_swap(tile, first, rows_n) for first in range(2)]

    other0 = core_swap(kv[0])
    halo0 = rows_of(kv[0])
    side = [square_swap(kv[1], 1), square_swap(kv[2], 2)]
    queries = list(project_q(sc, after(normed, other0), norm_q, tables, w_query))
    middle = jnp.stack(after(side, queries[0], *halo0))
    halo12, other12 = rows_of(middle), core_swap(middle)
    mine3 = queries[3][None]
    queries[1:3] = [square_swap(queries[m], m) for m in range(1, 3)]
    corner = square_swap(jnp.concatenate([kv[3], after(mine3, queries[1], queries[2])]), 3)
    queries[3], corner = corner[2], corner[:2]
    halo3, other3 = rows_of(corner), core_swap(corner)
    queries[0] = after(queries[0], *halo12)

    def tiles_of(first, both, last):
        return [(first, None), (both, 0), (both, 1), (last, None)]

    same, other = tiles_of(kv[0], middle, corner), tiles_of(other0, other12, other3)
    halo = [tiles_of(halo0[r], halo12[r], halo3[r]) for r in range(2)]
    swapped = [[core_swap(tile) for tile in pair] for pair in (halo0, halo12)]

    def call(name, plan, state):
        tiles = {}
        for s in range(2):
            at = slice(2 * s, 2 * s + 2)
            tiles[f"same{s}"], tiles[f"other{s}"] = same[at], other[at]
            for r in range(2):
                tiles[f"same{s}{r}"], tiles[f"other{s}{r}"] = halo[r][at], halo_other[r][at]
        used = {n for p in plan for segs in p.values() for names, _ in segs for n in names}
        return attend_call(name, plan, sc, queries, {n: t for n, t in tiles.items() if n in used}, state)

    rows = [tuple(((f"same{s}{r}", f"other{s}{r}"), r) for r in range(2)) for s in range(2)]
    far = [tuple(((f"other{s}{r}",), r) for r in range(2)) for s in range(2)]
    own = [("same0", "other0"), ("same1", "other1")]
    swapped_early = [*swapped, halo3]
    halo_other = [tiles_of(*[pair[r] for pair in swapped_early]) for r in range(2)]
    state = call(
        "attend_own",
        ({0: (((*own[0], "other1"), None),), 1: ((own[1], None),)}, {0: ((own[0], None),), 1: (((*own[1], "other0"), None),)}),
        {},
    )
    state = call("attend_halo", ({0: rows[0], 1: ()}, {0: rows[0], 1: far[0]}), {0: state[:2], 1: state[2:]})
    swapped.append([core_swap(after(tile, state[0])) for tile in halo3])
    halo_other = [tiles_of(*[pair[r] for pair in swapped]) for r in range(2)]
    attended = call("attend_last", ({0: far[1], 1: rows[1]}, {0: (), 1: rows[1]}), {0: state[:2], 1: state[2:]})
    attended = [square_swap(attended[m], m) for m in range(GROUPS)]
    branch = project_out(sc, attended, modulation, w_out)
    return branch.reshape(CT, CH, CW, D)


def solution(mesh):
    square = mesh.shape["ta"] == 4 and mesh.shape["wa"] == 2
    chosen = square_body if square else body
    in_specs = (P("ta", "ha", "wa", None), P(), P(), P(), P(), P(), P(), P())
    out_specs = P("ta", "ha", "wa", None)
    return jax.shard_map(chosen, mesh=mesh, in_specs=in_specs, out_specs=out_specs, check_vma=False)
```

```python
import functools

import jax
import jax.numpy as jnp
import numpy as np
from jax import lax
from jax.experimental import pallas as pl
from jax.experimental.pallas import tpu as pltpu
from jax.sharding import PartitionSpec as P

HEADS = 12
HEAD_DIM = 128
D = 1536
TT = 3
TH = 8
TW = 8
CT = 3
CH = 8
CW = 8


def with_halo(value, sides, width):
    for axis, dim in sides:
        devices, length = (lax.axis_size(axis), value.shape[dim])
        up = [(i, (i + 1) % devices) for i in range(devices - 1)]
        down = [(j, i) for i, j in up]
        last = lax.slice_in_dim(value, length - width, length, axis=dim)
        first = lax.slice_in_dim(value, 0, width, axis=dim)
        before = lax.ppermute(last, axis, up)
        after = lax.ppermute(first, axis, down)
        value = jnp.concatenate([before, value, after], axis=dim)
    return value


def modulate(tokens, modulation):
    values = tokens.astype(jnp.float32)
    center = values - jnp.mean(values, axis=-1, keepdims=True)
    spread = jnp.mean(center * center, axis=-1, keepdims=True)
    return (center * lax.rsqrt(spread + 1e-06) * (1.0 + modulation[1]) + modulation[0]).astype(
        jnp.bfloat16
    )


def rms_gain(values, gain):
    return values * lax.rsqrt(jnp.mean(values * values, axis=-1, keepdims=True) + 1e-06) * gain


def rotate_pairs(values, frame_pos, row_pos, column_pos):
    half = HEAD_DIM // 2
    sixth = HEAD_DIM // 6
    first = half - 2 * sixth
    freq_first = 10000.0 ** (-jnp.arange(first, dtype=jnp.float32) / first)
    freq_rest = 10000.0 ** (-jnp.arange(sixth, dtype=jnp.float32) / sixth)
    shape = values.shape[:3]
    angle_frame = frame_pos[:, None] * freq_first
    angle_row = row_pos[:, None] * freq_rest
    angle_column = column_pos[:, None] * freq_rest
    angles = jnp.concatenate(
        [
            jnp.broadcast_to(angle_frame[:, None, None, :], shape + (first,)),
            jnp.broadcast_to(angle_row[None, :, None, :], shape + (sixth,)),
            jnp.broadcast_to(angle_column[None, None, :, :], shape + (sixth,)),
        ],
        axis=-1,
    )
    cosine = jnp.cos(angles)[:, :, :, None, :]
    sine = jnp.sin(angles)[:, :, :, None, :]
    pairs = values.reshape(shape + (HEADS, half, 2))
    even_part = pairs[..., 0]
    odd_part = pairs[..., 1]
    rotated = jnp.stack(
        [even_part * cosine - odd_part * sine, even_part * sine + odd_part * cosine], axis=-1
    )
    return rotated.reshape(values.shape)


def tile_rows(query, key_pad, value_pad, anchor, extent):
    tile_frames = CT // TT
    tile_rows_n = CH // TH
    tile_columns = CW // TW
    tile_size = TT * TH * TW
    window = 27 * tile_size

    def one_row(index):
        frame_tile = index // tile_rows_n
        row_tile = index % tile_rows_n
        query_row = query
        query_row = query_row.reshape(TT, TH, tile_columns, TW, HEADS, HEAD_DIM).transpose(
            4, 2, 0, 1, 3, 5
        )
        query_row = query_row.reshape(HEADS, tile_columns, tile_size, HEAD_DIM)
        key_tiles = jnp.stack([key_pad])
        value_tiles = jnp.stack([value_pad])
        key_tiles = key_tiles.reshape(tile_columns, window, HEADS, HEAD_DIM).transpose(2, 0, 1, 3)
        value_tiles = value_tiles.reshape(tile_columns, window, HEADS, HEAD_DIM).transpose(
            2, 0, 1, 3
        )
        frames_at = anchor[0] + frame_tile * TT - TT + jnp.arange(3 * TT, dtype=jnp.int32)
        rows_at = anchor[1] + row_tile * TH - TH + jnp.arange(3 * TH, dtype=jnp.int32)
        columns_at = (
            anchor[2]
            + jnp.arange(tile_columns, dtype=jnp.int32)[:, None] * TW
            - TW
            + jnp.arange(3 * TW, dtype=jnp.int32)[None, :]
        )
        frame_ok = (frames_at >= 0) & (frames_at < extent[0])
        row_ok = (rows_at >= 0) & (rows_at < extent[1])
        column_ok = (columns_at >= 0) & (columns_at < extent[2])
        valid = (
            frame_ok[None, :, None, None]
            & row_ok[None, None, :, None]
            & column_ok[:, None, None, :]
        )
        valid = valid.reshape(tile_columns, window)

        def one_head(operands):
            head_query, head_key, head_value = operands
            scores = jnp.einsum(
                "cqd,ckd->cqk", head_query, head_key, preferred_element_type=jnp.float32
            ) * HEAD_DIM ** (-0.5)
            scores = jnp.where(valid[:, None, :], scores, -1e30)
            peak = jnp.max(scores, axis=-1, keepdims=True)
            expo = jnp.exp(scores - peak)
            weights = (expo / jnp.sum(expo, axis=-1, keepdims=True)).astype(jnp.bfloat16)
            return jnp.einsum(
                "cqk,ckd->cqd", weights, head_value, preferred_element_type=jnp.float32
            ).astype(jnp.bfloat16)

        attended = lax.map(one_head, (query_row, key_tiles, value_tiles))
        attended = attended.reshape(HEADS, tile_columns, TT, TH, TW, HEAD_DIM).transpose(
            2, 3, 1, 4, 0, 5
        )
        return attended.reshape(TT, TH, CW, D)

    result = lax.map(one_row, jnp.arange(tile_frames * tile_rows_n, dtype=jnp.int32))
    result = result.reshape(tile_frames, tile_rows_n, TT, TH, CW, D).transpose(0, 2, 1, 3, 4, 5)
    return result.reshape(CT, CH, CW, D)


def body(tokens, modulation, w_query, w_key, w_value, w_out, norm_q, norm_k):
    anchor = (lax.axis_index("ta") * CT, lax.axis_index("ha") * CH, lax.axis_index("wa") * CW)
    extent = (lax.axis_size("ta") * CT, lax.axis_size("ha") * CH, lax.axis_size("wa") * CW)
    frame_pos = (anchor[0] + jnp.arange(CT, dtype=jnp.int32)).astype(jnp.float32)
    row_pos = (anchor[1] + jnp.arange(CH, dtype=jnp.int32)).astype(jnp.float32)
    column_pos = (anchor[2] + jnp.arange(CW, dtype=jnp.int32)).astype(jnp.float32)
    grid = (CT, CH, CW, D)
    normed = modulate(tokens, modulation)
    flat = normed.reshape(-1, D)
    key = rms_gain(jnp.dot(flat, w_key, preferred_element_type=jnp.float32), norm_k).reshape(grid)
    key = rotate_pairs(key, frame_pos, row_pos, column_pos).astype(jnp.bfloat16)
    value = (
        jnp.dot(flat, w_value, preferred_element_type=jnp.float32)
        .astype(jnp.bfloat16)
        .reshape(grid)
    )
    key_value = jnp.stack([key, value])
    framed = with_halo(key_value, (("ta", 1),), TT)
    padded = with_halo(framed, (("ha", 2), ("wa", 3)), TW)
    query = rms_gain(jnp.dot(flat, w_query, preferred_element_type=jnp.float32), norm_q).reshape(
        grid
    )
    query = rotate_pairs(query, frame_pos, row_pos, column_pos).astype(jnp.bfloat16)
    attended = tile_rows(query, padded[0], padded[1], anchor, extent)
    branch = (
        jnp.dot(attended.reshape(-1, D), w_out, preferred_element_type=jnp.float32) * modulation[2]
    )
    return branch.astype(jnp.bfloat16).reshape(grid)


TILE = TT * TH * TW
GROUPS = 4
GH = HEADS // GROUPS
GW = GH * HEAD_DIM
SCORE_SCALE = float(HEAD_DIM ** (-0.5) * np.log2(np.e))


def rope_tables(devices, per_device, low, count):
    n = np.float32(count)
    freq = np.float32(10000.0) ** (-np.arange(count, dtype=np.float32) / n)
    angle = np.arange(devices * per_device, dtype=np.float32)[:, None] * freq[None, :]
    cosine = np.zeros((devices * per_device, HEAD_DIM), np.float32)
    sine = np.zeros((devices * per_device, HEAD_DIM), np.float32)
    for j in range(count):
        lane = 2 * (low + j)
        cosine[:, lane] = cosine[:, lane + 1] = np.cos(angle[:, j])
        sine[:, lane] = -np.sin(angle[:, j])
        sine[:, lane + 1] = np.sin(angle[:, j])
    tables = np.stack([cosine, sine]).reshape(2, devices, per_device, HEAD_DIM)
    return jnp.asarray(tables.transpose(1, 0, 2, 3))


def layer_norm(tokens, mod_ref):
    values = tokens.astype(jnp.float32)
    center = values - jnp.mean(values, axis=-1, keepdims=True)
    spread = jnp.mean(center * center, axis=-1, keepdims=True)
    shift, scale = mod_ref[0:1, :], mod_ref[1:2, :]
    return (center * lax.rsqrt(spread + 1e-06) * (1.0 + scale) + shift).astype(jnp.bfloat16)


def angle_tables(place, ft_ref, rt_ref, ct_ref):
    out = []
    for kind in range(2):
        frame = ft_ref[place[0], kind]
        row = rt_ref[place[1], kind]
        column = ct_ref[place[2], kind]
        full = frame[:, None, None, :] + row[None, :, None, :] + column[None, None, :, :]
        out.append(full.reshape(TILE, HEAD_DIM))
    return out


def rope(x, cosine, sine, even):
    swapped = jnp.where(even, pltpu.roll(x, HEAD_DIM - 1, 1), pltpu.roll(x, 1, 1))
    return x * cosine + swapped * sine


def mesh_place():
    ta, ha, wa = (lax.axis_index(name) for name in ("ta", "ha", "wa"))
    return 2 * (ta // 2) + wa, ta, ha, wa


def group_at(group, m):
    return pl.multiple_of((group ^ m) * GW, GW)


def start_all(pairs, sems):
    copies = [pltpu.make_async_copy(source, target, sems.at[n]) for n, (source, target) in enumerate(pairs)]
    for copy in copies:
        copy.start()
    return copies


def wait_all(copies):
    for copy in copies:
        copy.wait()


def weight_blocks(group, w_hbm, wbuf):
    return [(w_hbm.at[:, pl.ds(group_at(group, m), GW)], wbuf.at[m]) for m in range(GROUPS)]


def project_normed(group, normed, weights, wbuf, buf, gain_ref, angles, write):
    cosine, sine = angles
    even = lax.broadcasted_iota(jnp.int32, (TILE, HEAD_DIM), 1) % 2 == 0
    ssq = None
    for m in range(GROUPS):
        weights[m].wait()
        prod = jnp.dot(normed, wbuf[m], preferred_element_type=jnp.float32)
        gain = gain_ref[:, pl.ds(group_at(group, m), GW)]
        for h in range(GH):
            lanes = slice(h * HEAD_DIM, (h + 1) * HEAD_DIM)
            x = prod[:, lanes]
            ssq = x * x if ssq is None else ssq + x * x
            buf[m, :, lanes] = rope(x * gain[:, lanes], cosine, sine, even)
    inv = lax.rsqrt(jnp.sum(ssq, axis=-1, keepdims=True) / D + 1e-06)
    for m in range(GROUPS):
        for h in range(GH):
            write(m, h, (buf[m, :, h * HEAD_DIM : (h + 1) * HEAD_DIM] * inv).astype(jnp.bfloat16))


def kv_kernel(tok_hbm, mod_hbm, nk_hbm, ft_hbm, rt_hbm, ct_hbm, wk_hbm, wv_hbm, *refs):
    kv_ref, normed_ref, refs = refs[:4], refs[4], refs[5:]
    tok_ref, mod_ref, nk_ref, ft_ref, rt_ref, ct_ref, wk_buf, wv_buf, buf, gain_ref, sems = refs
    sources = (tok_hbm, mod_hbm, nk_hbm, ft_hbm, rt_hbm, ct_hbm)
    small = start_all(zip(sources, refs), sems.at[2])
    group, *place = mesh_place()
    key_weights = start_all(weight_blocks(group, wk_hbm, wk_buf), sems.at[0])
    value_weights = start_all(weight_blocks(group, wv_hbm, wv_buf), sems.at[1])
    wait_all(small)
    angles = angle_tables(place, ft_ref, rt_ref, ct_ref)
    gain_ref[...] = nk_ref[...].reshape(1, D)
    normed = layer_norm(tok_ref[...], mod_ref)
    normed_ref[...] = normed

    def write(m, h, x):
        kv_ref[m][0, h] = x

    project_normed(group, normed, key_weights, wk_buf, buf, gain_ref, angles, write)
    for m in range(GROUPS):
        value_weights[m].wait()
        prod = jnp.dot(normed, wv_buf[m], preferred_element_type=jnp.float32)
        for h in range(GH):
            kv_ref[m][1, h] = prod[:, h * HEAD_DIM : (h + 1) * HEAD_DIM].astype(jnp.bfloat16)


def q_kernel(normed_hbm, nq_hbm, ft_hbm, rt_hbm, ct_hbm, wq_hbm, token_hbm, *refs):
    q_ref, made_ref, refs = refs[:4], refs[4], refs[5:]
    made_ref[...] = jnp.zeros_like(made_ref)
    normed_ref, nq_ref, ft_ref, rt_ref, ct_ref, wq_buf, buf, gain_ref, sems = refs
    small = start_all(zip((normed_hbm, nq_hbm, ft_hbm, rt_hbm, ct_hbm), refs), sems.at[1])
    group, *place = mesh_place()
    weights = start_all(weight_blocks(group, wq_hbm, wq_buf), sems.at[0])
    wait_all(small)
    angles = angle_tables(place, ft_ref, rt_ref, ct_ref)
    gain_ref[...] = nq_ref[...].reshape(1, D)

    def write(m, h, x):
        q_ref[m][h] = x

    project_normed(group, normed_ref[...], weights, wq_buf, buf, gain_ref, angles, write)


SMEM = pl.BlockSpec(memory_space=pltpu.SMEM)
VMEM = pl.BlockSpec(memory_space=pltpu.VMEM)
HBM = pl.BlockSpec(memory_space=pl.ANY)


def limit(mib):
    return pltpu.CompilerParams(vmem_limit_bytes=mib * 1024 * 1024)


KV_SHAPE = (2, GH, TILE, HEAD_DIM)
Q_SHAPE = (GH, TILE, HEAD_DIM)


def project_kv(tokens, modulation, norm_k, tables, w_key, w_value):
    return pl.pallas_call(
        kv_kernel,
        in_specs=[HBM] * 8,
        out_specs=[VMEM] * (GROUPS + 1),
        scratch_shapes=[
            pltpu.VMEM((TILE, D), jnp.bfloat16),
            pltpu.VMEM((3, D), jnp.float32),
            pltpu.VMEM((D,), jnp.float32),
            *[pltpu.VMEM(t.shape, jnp.float32) for t in tables],
            pltpu.VMEM((GROUPS, D, GW), jnp.bfloat16),
            pltpu.VMEM((GROUPS, D, GW), jnp.bfloat16),
            pltpu.VMEM((GROUPS, TILE, GW), jnp.float32),
            pltpu.VMEM((1, D), jnp.float32),
            pltpu.SemaphoreType.DMA((3, 6)),
        ],
        out_shape=[pltpu.VMEM(KV_SHAPE, jnp.bfloat16)] * GROUPS + [pltpu.VMEM((TILE, D), jnp.bfloat16)],
        compiler_params=limit(54),
        cost_estimate=pl.CostEstimate(flops=4 * TILE * D * D, bytes_accessed=4 * D * D, transcendentals=0),
        name="project_kv",
    )(tokens, modulation, norm_k, *tables, w_key, w_value)


def project_q(normed, norm_q, tables, w_query, token):
    return pl.pallas_call(
        q_kernel,
        in_specs=[HBM] * 7,
        out_specs=[VMEM] * (GROUPS + 1),
        scratch_shapes=[
            pltpu.VMEM((TILE, D), jnp.bfloat16),
            pltpu.VMEM((D,), jnp.float32),
            *[pltpu.VMEM(t.shape, jnp.float32) for t in tables],
            pltpu.VMEM((GROUPS, D, GW), jnp.bfloat16),
            pltpu.VMEM((GROUPS, TILE, GW), jnp.float32),
            pltpu.VMEM((1, D), jnp.float32),
            pltpu.SemaphoreType.DMA((2, 5)),
        ],
        out_shape=[pltpu.VMEM(Q_SHAPE, jnp.bfloat16)] * GROUPS + [TOKEN],
        compiler_params=limit(46),
        cost_estimate=pl.CostEstimate(flops=2 * TILE * D * D, bytes_accessed=2 * D * D, transcendentals=0),
        name="project_q",
    )(normed, norm_q, *tables, w_query, token)


def query_of(refs, s, h):
    return jnp.concatenate([refs[2 * s][h], refs[2 * s + 1][h]], axis=0)


def raw_scores(query, keys):
    return lax.dot_general(query, keys, (((1,), (1,)), ((), ())), preferred_element_type=jnp.float32)


def weigh(scores, peak, values):
    expo = jnp.exp2((scores - peak) * SCORE_SCALE).astype(jnp.bfloat16)
    ones = jnp.ones((values.shape[0], HEAD_DIM), jnp.bfloat16)
    both = jnp.dot(expo, jnp.concatenate([values, ones], axis=1), preferred_element_type=jnp.float32)
    return both[:, :HEAD_DIM], both[:, HEAD_DIM:]


def attend(query, segments, state=None):
    scores = [raw_scores(query, keys) for keys, _, _ in segments]
    found = [jnp.max(s, axis=-1, keepdims=True) for s in scores]
    found = [f if there is None else jnp.where(there, f, -1e30) for f, (_, _, there) in zip(found, segments)]
    peak = functools.reduce(jnp.maximum, found if state is None else [state[0], *found])
    total = norm = None
    if state is not None:
        decay = jnp.exp2((state[0] - peak) * SCORE_SCALE)
        total, norm = state[1] * decay, state[2] * decay
    for s, (_, values, there) in zip(scores, segments):
        part, weight = weigh(s, peak if there is None else jnp.where(there, peak, 1e30), values)
        total, norm = (part, weight) if total is None else (total + part, norm + weight)
    return peak, total, norm


def attend_kernel(plan, arrays_n, state_slots, final, sc_ref, *refs):
    q, arrays, refs = refs[:4], refs[4 : 4 + arrays_n], refs[4 + arrays_n :]
    state_in = {s: refs[2 * n : 2 * n + 2] for n, s in enumerate(state_slots)}
    *refs, token_ref = refs[2 * len(state_slots) :]
    token_ref[...] = jnp.zeros_like(token_ref)
    low = lax.broadcasted_iota(jnp.int32, (2 * TILE, HEAD_DIM), 1) < HEAD_DIM // 2

    def stack_keys(tiles, kind, h):
        return jnp.concatenate([arrays[n][(*place, kind, h)] for n, place in tiles], axis=0)

    def state(s, h):
        if s not in state_in:
            return None
        stat = state_in[s][0][h]
        return stat[:, :1], state_in[s][1][h], stat[:, HEAD_DIM // 2 : HEAD_DIM // 2 + 1]

    def run(slots):
        for h in range(GH):
            for n, s in enumerate(sorted(slots)):
                segments = [
                    (stack_keys(tiles, 0, h), stack_keys(tiles, 1, h), None if row is None else sc_ref[5 + row] == 1)
                    for tiles, row in slots[s]
                ]
                peak, total, norm = attend(query_of(q, s, h), segments, state(s, h)) if segments else state(s, h)
                if final:
                    attended = (total / norm).astype(jnp.bfloat16)
                    refs[2 * s][h] = attended[:TILE]
                    refs[2 * s + 1][h] = attended[TILE:]
                else:
                    refs[2 * n][h] = jnp.where(low, peak, norm)
                    refs[2 * n + 1][h] = total

    if plan[0] == plan[1]:
        run(plan[0])
    else:
        for near in range(2):
            pl.when(sc_ref[4] == near)(functools.partial(run, plan[near]))


TOKEN = jax.ShapeDtypeStruct((8, HEAD_DIM), jnp.float32)
STATE_SHAPE = jax.ShapeDtypeStruct((GH, 2 * TILE, HEAD_DIM), jnp.float32)


def attend_call(name, plan, sc, queries, arrays, state):
    final = name == "attend_last"
    state_slots = sorted(state)
    states = [array for s in state_slots for array in state[s]]
    return pl.pallas_call(
        functools.partial(attend_kernel, plan, len(arrays), tuple(state_slots), final),
        in_specs=[SMEM] + [VMEM] * (GROUPS + len(arrays) + len(states)),
        out_specs=[VMEM] * (5 if final else 2 * len(plan[0]) + 1),
        out_shape=[*([jax.ShapeDtypeStruct(Q_SHAPE, jnp.bfloat16)] * 4 if final else [STATE_SHAPE] * (2 * len(plan[0]))), TOKEN],
        compiler_params=limit(32),
        cost_estimate=pl.CostEstimate(flops=1000, bytes_accessed=1000, transcendentals=0),
        name=name,
    )(sc, *queries, *arrays, *states)


OUT_PARTS = 3


def out_kernel(a0, a1, a2, a3, mod_ref, w_ref, out_hbm, out_ref, sems):
    group = mesh_place()[0]
    rows = [jnp.concatenate([ref[h] for h in range(GH)], axis=1) for ref in (a0, a1, a2, a3)]
    width = D // OUT_PARTS
    copies = []
    for n in range(OUT_PARTS):
        lanes = slice(n * width, (n + 1) * width)
        total = None
        for m in range(GROUPS):
            part = jnp.dot(rows[m], w_ref[pl.ds(group_at(group, m), GW), lanes], preferred_element_type=jnp.float32)
            total = part if total is None else total + part
        out_ref[:, lanes] = (total * mod_ref[2:3, lanes]).astype(jnp.bfloat16)
        copies.append(pltpu.make_async_copy(out_ref.at[:, lanes], out_hbm.at[:, lanes], sems.at[n]))
        copies[-1].start()
    wait_all(copies)


def project_out(attended, modulation, w_out):
    return pl.pallas_call(
        out_kernel,
        in_specs=[VMEM] * 6,
        out_specs=HBM,
        scratch_shapes=[pltpu.VMEM((TILE, D), jnp.bfloat16), pltpu.SemaphoreType.DMA((OUT_PARTS,))],
        out_shape=jax.ShapeDtypeStruct((TILE, D), jnp.bfloat16),
        compiler_params=limit(20),
        cost_estimate=pl.CostEstimate(flops=2 * TILE * D * D, bytes_accessed=2 * D * D, transcendentals=0),
        name="project_out",
    )(*attended, modulation, w_out)


def square_swap(value, m):
    if m == 0:
        return value
    flip = (m >> 1) * 4 + (m & 1)
    return lax.ppermute(value, ("ta", "wa"), [(i, i ^ flip) for i in range(8)])


def core_swap(value):
    return lax.ppermute(value, "ta", [(i, i ^ 1) for i in range(4)])


def row_swap(value, first, rows_n):
    pairs = [(i, i + 1) for i in range(first, rows_n - 1, 2)]
    return lax.ppermute(value, "ha", [edge for i, j in pairs for edge in ((i, j), (j, i))])


def after(value, *others):
    return lax.optimization_barrier((value, *others))[0]


def hold(value, token):
    return jnp.where(token[0] < 1.0, value, jnp.zeros((), value.dtype))


def square_body(tokens, modulation, w_query, w_key, w_value, w_out, norm_q, norm_k):
    ta, ha, wa = (lax.axis_index(name) for name in ("ta", "ha", "wa"))
    rows_n = lax.axis_size("ha")
    place_x, core = ta // 2, ta % 2
    near_slot = 1 - (place_x ^ core)
    partner = [ha + 1 - 2 * (ha % 2), ha - 1 + 2 * (ha % 2)]
    sc = jnp.stack(
        [2 * place_x + wa, ta, ha, wa, near_slot, *[((p >= 0) & (p < rows_n)).astype(jnp.int32) for p in partner]]
    ).astype(jnp.int32)
    half, sixth = HEAD_DIM // 2, HEAD_DIM // 6
    first = half - 2 * sixth
    tables = (
        rope_tables(lax.axis_size("ta"), CT, 0, first),
        rope_tables(rows_n, CH, first, sixth),
        rope_tables(lax.axis_size("wa"), CW, first + sixth, sixth),
    )
    *kv, normed = project_kv(tokens.reshape(TILE, D), modulation, norm_k, tables, w_key, w_value)

    def rows_of(tile):
        return [row_swap(tile, first, rows_n) for first in range(2)]

    other0 = core_swap(kv[0])
    halo0 = rows_of(kv[0])
    side = [square_swap(kv[1], 1), square_swap(kv[2], 2)]
    *queries, made = project_q(after(normed, other0), norm_q, tables, w_query, normed)
    middle = jnp.stack(after(side, queries[0], *halo0))
    halo12, other12 = rows_of(middle), core_swap(middle)
    mine3 = queries[3][None]
    queries[1:3] = [square_swap(queries[m], m) for m in range(1, 3)]
    corner = square_swap(jnp.concatenate([kv[3], after(mine3, queries[1], queries[2])]), 3)
    queries[0] = after(queries[0], *halo12)
    swapped0 = [core_swap(tile) for tile in halo0]
    halo_parts = {"same": [halo0, halo12, None], "other": [swapped0, None, None]}
    own = {"same": [(kv[0], ()), (middle, (0,)), (middle, (1,)), None], "other": [(other0, ()), (other12, (0,)), (other12, (1,)), None]}

    def halo_tiles(row):
        made = {}
        for kind, parts in halo_parts.items():
            c0, c12, c3 = [None if part is None else part[row] for part in parts]
            made[kind] = [(c0, ()), (c12, (0,)), (c12, (1,)), (c3, ())]
        return made

    def own_keys(kinds):
        return [(own[kind][m], kind, m) for kind, m in kinds], None

    def row_keys(kinds, row):
        return [(halo_tiles(row)[kind][m], kind, m) for kind, m in kinds], row

    def call(name, plans, state):
        numbers, arrays, numbered = {}, [], []
        for slots in plans:
            made = {}
            for s, segments in slots.items():
                made[s] = ()
                for tiles, row in segments:
                    ids = []
                    for (array, place), kind, m in tiles:
                        key = (id(array), place)
                        if key not in numbers:
                            known = [n for n, other in enumerate(arrays) if other is array]
                            if not known:
                                arrays.append(array)
                                known = [len(arrays) - 1]
                            numbers[key] = (known[0], place)
                        ids.append(numbers[key])
                    made[s] += ((tuple(ids), row),)
            numbered.append(made)
        return attend_call(name, tuple(numbered), sc, queries, arrays, state)

    def both(*places):
        return [(kind, m) for kind in ("same", "other") for m in places]

    def rows_keys(kinds):
        return [row_keys(kinds, r) for r in range(2)]

    cross = [("other", 2), ("other", 3)], [("other", 0), ("other", 1)]
    queries[3], corner = corner[2], corner[:2]
    own["same"][3], own["other"][3] = (corner, ()), (core_swap(corner), ())
    halo_parts["other"][1] = [core_swap(tile) for tile in halo12]
    *state, made = call(
        "attend_own",
        (
            {0: [own_keys(both(0, 1) + cross[0])], 1: [own_keys(both(2, 3))]},
            {0: [own_keys(both(0, 1))], 1: [own_keys(both(2, 3) + cross[1])]},
        ),
        {},
    )
    halo3 = rows_of(corner)
    halo_parts["same"][2] = halo3
    halo_parts["other"][2] = [core_swap(hold(tile, made)) for tile in halo3]
    *state, made = call(
        "attend_halo", ({0: rows_keys(both(0, 1)), 1: []},) * 2, {0: state[:2], 1: state[2:]}
    )
    *attended, made = call(
        "attend_last",
        ({0: rows_keys(cross[0]), 1: rows_keys(both(2, 3))}, {0: [], 1: rows_keys(both(2, 3) + cross[1])}),
        {0: state[:2], 1: state[2:]},
    )
    attended = [square_swap(attended[m], m) for m in range(GROUPS)]
    branch = project_out(attended, modulation, w_out)
    return branch.reshape(CT, CH, CW, D)


def solution(mesh):
    square = mesh.shape["ta"] == 4 and mesh.shape["wa"] == 2
    chosen = square_body if square else body
    in_specs = (P("ta", "ha", "wa", None), P(), P(), P(), P(), P(), P(), P())
    out_specs = P("ta", "ha", "wa", None)
    return jax.shard_map(chosen, mesh=mesh, in_specs=in_specs, out_specs=out_specs, check_vma=False)
```

```python
import functools

import jax
import jax.numpy as jnp
import numpy as np
from jax import lax
from jax.experimental import pallas as pl
from jax.experimental.pallas import tpu as pltpu
from jax.sharding import PartitionSpec as P

HEADS = 12
HEAD_DIM = 128
D = 1536
TT = 3
TH = 8
TW = 8
CT = 3
CH = 8
CW = 8


def with_halo(value, sides, width):
    for axis, dim in sides:
        devices, length = (lax.axis_size(axis), value.shape[dim])
        up = [(i, (i + 1) % devices) for i in range(devices - 1)]
        down = [(j, i) for i, j in up]
        last = lax.slice_in_dim(value, length - width, length, axis=dim)
        first = lax.slice_in_dim(value, 0, width, axis=dim)
        before = lax.ppermute(last, axis, up)
        after = lax.ppermute(first, axis, down)
        value = jnp.concatenate([before, value, after], axis=dim)
    return value


def modulate(tokens, modulation):
    values = tokens.astype(jnp.float32)
    center = values - jnp.mean(values, axis=-1, keepdims=True)
    spread = jnp.mean(center * center, axis=-1, keepdims=True)
    return (center * lax.rsqrt(spread + 1e-06) * (1.0 + modulation[1]) + modulation[0]).astype(
        jnp.bfloat16
    )


def rms_gain(values, gain):
    return values * lax.rsqrt(jnp.mean(values * values, axis=-1, keepdims=True) + 1e-06) * gain


def rotate_pairs(values, frame_pos, row_pos, column_pos):
    half = HEAD_DIM // 2
    sixth = HEAD_DIM // 6
    first = half - 2 * sixth
    freq_first = 10000.0 ** (-jnp.arange(first, dtype=jnp.float32) / first)
    freq_rest = 10000.0 ** (-jnp.arange(sixth, dtype=jnp.float32) / sixth)
    shape = values.shape[:3]
    angle_frame = frame_pos[:, None] * freq_first
    angle_row = row_pos[:, None] * freq_rest
    angle_column = column_pos[:, None] * freq_rest
    angles = jnp.concatenate(
        [
            jnp.broadcast_to(angle_frame[:, None, None, :], shape + (first,)),
            jnp.broadcast_to(angle_row[None, :, None, :], shape + (sixth,)),
            jnp.broadcast_to(angle_column[None, None, :, :], shape + (sixth,)),
        ],
        axis=-1,
    )
    cosine = jnp.cos(angles)[:, :, :, None, :]
    sine = jnp.sin(angles)[:, :, :, None, :]
    pairs = values.reshape(shape + (HEADS, half, 2))
    even_part = pairs[..., 0]
    odd_part = pairs[..., 1]
    rotated = jnp.stack(
        [even_part * cosine - odd_part * sine, even_part * sine + odd_part * cosine], axis=-1
    )
    return rotated.reshape(values.shape)


def tile_rows(query, key_pad, value_pad, anchor, extent):
    tile_frames = CT // TT
    tile_rows_n = CH // TH
    tile_columns = CW // TW
    tile_size = TT * TH * TW
    window = 27 * tile_size

    def one_row(index):
        frame_tile = index // tile_rows_n
        row_tile = index % tile_rows_n
        query_row = query
        query_row = query_row.reshape(TT, TH, tile_columns, TW, HEADS, HEAD_DIM).transpose(
            4, 2, 0, 1, 3, 5
        )
        query_row = query_row.reshape(HEADS, tile_columns, tile_size, HEAD_DIM)
        key_tiles = jnp.stack([key_pad])
        value_tiles = jnp.stack([value_pad])
        key_tiles = key_tiles.reshape(tile_columns, window, HEADS, HEAD_DIM).transpose(2, 0, 1, 3)
        value_tiles = value_tiles.reshape(tile_columns, window, HEADS, HEAD_DIM).transpose(
            2, 0, 1, 3
        )
        frames_at = anchor[0] + frame_tile * TT - TT + jnp.arange(3 * TT, dtype=jnp.int32)
        rows_at = anchor[1] + row_tile * TH - TH + jnp.arange(3 * TH, dtype=jnp.int32)
        columns_at = (
            anchor[2]
            + jnp.arange(tile_columns, dtype=jnp.int32)[:, None] * TW
            - TW
            + jnp.arange(3 * TW, dtype=jnp.int32)[None, :]
        )
        frame_ok = (frames_at >= 0) & (frames_at < extent[0])
        row_ok = (rows_at >= 0) & (rows_at < extent[1])
        column_ok = (columns_at >= 0) & (columns_at < extent[2])
        valid = (
            frame_ok[None, :, None, None]
            & row_ok[None, None, :, None]
            & column_ok[:, None, None, :]
        )
        valid = valid.reshape(tile_columns, window)

        def one_head(operands):
            head_query, head_key, head_value = operands
            scores = jnp.einsum(
                "cqd,ckd->cqk", head_query, head_key, preferred_element_type=jnp.float32
            ) * HEAD_DIM ** (-0.5)
            scores = jnp.where(valid[:, None, :], scores, -1e30)
            peak = jnp.max(scores, axis=-1, keepdims=True)
            expo = jnp.exp(scores - peak)
            weights = (expo / jnp.sum(expo, axis=-1, keepdims=True)).astype(jnp.bfloat16)
            return jnp.einsum(
                "cqk,ckd->cqd", weights, head_value, preferred_element_type=jnp.float32
            ).astype(jnp.bfloat16)

        attended = lax.map(one_head, (query_row, key_tiles, value_tiles))
        attended = attended.reshape(HEADS, tile_columns, TT, TH, TW, HEAD_DIM).transpose(
            2, 3, 1, 4, 0, 5
        )
        return attended.reshape(TT, TH, CW, D)

    result = lax.map(one_row, jnp.arange(tile_frames * tile_rows_n, dtype=jnp.int32))
    result = result.reshape(tile_frames, tile_rows_n, TT, TH, CW, D).transpose(0, 2, 1, 3, 4, 5)
    return result.reshape(CT, CH, CW, D)


def body(tokens, modulation, w_query, w_key, w_value, w_out, norm_q, norm_k):
    anchor = (lax.axis_index("ta") * CT, lax.axis_index("ha") * CH, lax.axis_index("wa") * CW)
    extent = (lax.axis_size("ta") * CT, lax.axis_size("ha") * CH, lax.axis_size("wa") * CW)
    frame_pos = (anchor[0] + jnp.arange(CT, dtype=jnp.int32)).astype(jnp.float32)
    row_pos = (anchor[1] + jnp.arange(CH, dtype=jnp.int32)).astype(jnp.float32)
    column_pos = (anchor[2] + jnp.arange(CW, dtype=jnp.int32)).astype(jnp.float32)
    grid = (CT, CH, CW, D)
    normed = modulate(tokens, modulation)
    flat = normed.reshape(-1, D)
    key = rms_gain(jnp.dot(flat, w_key, preferred_element_type=jnp.float32), norm_k).reshape(grid)
    key = rotate_pairs(key, frame_pos, row_pos, column_pos).astype(jnp.bfloat16)
    value = (
        jnp.dot(flat, w_value, preferred_element_type=jnp.float32)
        .astype(jnp.bfloat16)
        .reshape(grid)
    )
    key_value = jnp.stack([key, value])
    framed = with_halo(key_value, (("ta", 1),), TT)
    padded = with_halo(framed, (("ha", 2), ("wa", 3)), TW)
    query = rms_gain(jnp.dot(flat, w_query, preferred_element_type=jnp.float32), norm_q).reshape(
        grid
    )
    query = rotate_pairs(query, frame_pos, row_pos, column_pos).astype(jnp.bfloat16)
    attended = tile_rows(query, padded[0], padded[1], anchor, extent)
    branch = (
        jnp.dot(attended.reshape(-1, D), w_out, preferred_element_type=jnp.float32) * modulation[2]
    )
    return branch.astype(jnp.bfloat16).reshape(grid)


TILE = TT * TH * TW
GROUPS = 4
GH = HEADS // GROUPS
GW = GH * HEAD_DIM
SCORE_SCALE = float(HEAD_DIM ** (-0.5) * np.log2(np.e))


def rope_tables(devices, per_device, low, count):
    n = np.float32(count)
    freq = np.float32(10000.0) ** (-np.arange(count, dtype=np.float32) / n)
    angle = np.arange(devices * per_device, dtype=np.float32)[:, None] * freq[None, :]
    cosine = np.zeros((devices * per_device, HEAD_DIM), np.float32)
    sine = np.zeros((devices * per_device, HEAD_DIM), np.float32)
    for j in range(count):
        lane = 2 * (low + j)
        cosine[:, lane] = cosine[:, lane + 1] = np.cos(angle[:, j])
        sine[:, lane] = -np.sin(angle[:, j])
        sine[:, lane + 1] = np.sin(angle[:, j])
    tables = np.stack([cosine, sine]).reshape(2, devices, per_device, HEAD_DIM)
    return jnp.asarray(tables.transpose(1, 0, 2, 3))


def layer_norm(tokens, mod_ref):
    values = tokens.astype(jnp.float32)
    center = values - jnp.mean(values, axis=-1, keepdims=True)
    spread = jnp.mean(center * center, axis=-1, keepdims=True)
    shift, scale = mod_ref[0:1, :], mod_ref[1:2, :]
    return (center * lax.rsqrt(spread + 1e-06) * (1.0 + scale) + shift).astype(jnp.bfloat16)


def angle_tables(place, ft_ref, rt_ref, ct_ref):
    out = []
    for kind in range(2):
        frame = ft_ref[place[0], kind]
        row = rt_ref[place[1], kind]
        column = ct_ref[place[2], kind]
        full = frame[:, None, None, :] + row[None, :, None, :] + column[None, None, :, :]
        out.append(full.reshape(TILE, HEAD_DIM))
    return out


def rope(x, cosine, sine, even):
    swapped = jnp.where(even, pltpu.roll(x, HEAD_DIM - 1, 1), pltpu.roll(x, 1, 1))
    return x * cosine + swapped * sine


def mesh_place():
    ta, ha, wa = (lax.axis_index(name) for name in ("ta", "ha", "wa"))
    return 2 * (ta // 2) + wa, ta, ha, wa


def group_at(group, m):
    return pl.multiple_of((group ^ m) * GW, GW)


def start_all(pairs, sems):
    copies = [pltpu.make_async_copy(source, target, sems.at[n]) for n, (source, target) in enumerate(pairs)]
    for copy in copies:
        copy.start()
    return copies


def wait_all(copies):
    for copy in copies:
        copy.wait()


def weight_blocks(group, w_hbm, wbuf):
    return [(w_hbm.at[:, pl.ds(group_at(group, m), GW)], wbuf.at[m]) for m in range(GROUPS)]


def project_normed(group, normed, weights, wbuf, buf, gain_ref, angles, write, beside=()):
    cosine, sine = angles
    even = lax.broadcasted_iota(jnp.int32, (TILE, HEAD_DIM), 1) % 2 == 0
    ssq = None

    def rotate(m, prod, ssq):
        gain = gain_ref[:, pl.ds(group_at(group, m), GW)]
        for h in range(GH):
            lanes = slice(h * HEAD_DIM, (h + 1) * HEAD_DIM)
            x = prod[:, lanes]
            ssq = x * x if ssq is None else ssq + x * x
            buf[m, :, lanes] = rope(x * gain[:, lanes], cosine, sine, even)
        return ssq

    before = None
    for m in range(GROUPS):
        weights[m].wait()
        prod = jnp.dot(normed, wbuf[m], preferred_element_type=jnp.float32)
        if before is not None:
            ssq = rotate(m - 1, before, ssq)
        before = prod
    steps = list(beside)
    if steps:
        steps.pop(0)()
    ssq = rotate(GROUPS - 1, before, ssq)
    inv = lax.rsqrt(jnp.sum(ssq, axis=-1, keepdims=True) / D + 1e-06)
    for m in range(GROUPS):
        if steps:
            steps.pop(0)()
        for h in range(GH):
            write(m, h, (buf[m, :, h * HEAD_DIM : (h + 1) * HEAD_DIM] * inv).astype(jnp.bfloat16))


def kv_kernel(tok_hbm, mod_hbm, nk_hbm, ft_hbm, rt_hbm, ct_hbm, wk_hbm, wv_hbm, *refs):
    kv_ref, normed_ref, refs = refs[:4], refs[4], refs[5:]
    tok_ref, mod_ref, nk_ref, ft_ref, rt_ref, ct_ref, wk_buf, wv_buf, buf, gain_ref, sems = refs
    sources = (tok_hbm, mod_hbm, nk_hbm, ft_hbm, rt_hbm, ct_hbm)
    small = start_all(zip(sources, refs), sems.at[2])
    group, *place = mesh_place()
    key_weights = start_all(weight_blocks(group, wk_hbm, wk_buf), sems.at[0])
    value_weights = start_all(weight_blocks(group, wv_hbm, wv_buf), sems.at[1])
    wait_all(small)
    angles = angle_tables(place, ft_ref, rt_ref, ct_ref)
    gain_ref[...] = nk_ref[...].reshape(1, D)
    normed = layer_norm(tok_ref[...], mod_ref)
    normed_ref[...] = normed

    def write(m, h, x):
        kv_ref[m][0, h] = x

    def value_block(m):
        value_weights[m].wait()
        prod = jnp.dot(normed, wv_buf[m], preferred_element_type=jnp.float32)
        for h in range(GH):
            kv_ref[m][1, h] = prod[:, h * HEAD_DIM : (h + 1) * HEAD_DIM].astype(jnp.bfloat16)

    beside = [functools.partial(value_block, m) for m in range(GROUPS)]
    project_normed(group, normed, key_weights, wk_buf, buf, gain_ref, angles, write, beside)


def q_kernel(normed_hbm, nq_hbm, ft_hbm, rt_hbm, ct_hbm, wq_hbm, token_hbm, *refs):
    q_ref, made_ref, refs = refs[:4], refs[4], refs[5:]
    made_ref[...] = jnp.zeros_like(made_ref)
    normed_ref, nq_ref, ft_ref, rt_ref, ct_ref, wq_buf, buf, gain_ref, sems = refs
    small = start_all(zip((normed_hbm, nq_hbm, ft_hbm, rt_hbm, ct_hbm), refs), sems.at[1])
    group, *place = mesh_place()
    weights = start_all(weight_blocks(group, wq_hbm, wq_buf), sems.at[0])
    wait_all(small)
    angles = angle_tables(place, ft_ref, rt_ref, ct_ref)
    gain_ref[...] = nq_ref[...].reshape(1, D)

    def write(m, h, x):
        q_ref[m][h] = x

    project_normed(group, normed_ref[...], weights, wq_buf, buf, gain_ref, angles, write)


SMEM = pl.BlockSpec(memory_space=pltpu.SMEM)
VMEM = pl.BlockSpec(memory_space=pltpu.VMEM)
HBM = pl.BlockSpec(memory_space=pl.ANY)


def limit(mib):
    return pltpu.CompilerParams(vmem_limit_bytes=mib * 1024 * 1024)


KV_SHAPE = (2, GH, TILE, HEAD_DIM)
Q_SHAPE = (GH, TILE, HEAD_DIM)


def project_kv(tokens, modulation, norm_k, tables, w_key, w_value):
    return pl.pallas_call(
        kv_kernel,
        in_specs=[HBM] * 8,
        out_specs=[VMEM] * (GROUPS + 1),
        scratch_shapes=[
            pltpu.VMEM((TILE, D), jnp.bfloat16),
            pltpu.VMEM((3, D), jnp.float32),
            pltpu.VMEM((D,), jnp.float32),
            *[pltpu.VMEM(t.shape, jnp.float32) for t in tables],
            pltpu.VMEM((GROUPS, D, GW), jnp.bfloat16),
            pltpu.VMEM((GROUPS, D, GW), jnp.bfloat16),
            pltpu.VMEM((GROUPS, TILE, GW), jnp.float32),
            pltpu.VMEM((1, D), jnp.float32),
            pltpu.SemaphoreType.DMA((3, 6)),
        ],
        out_shape=[pltpu.VMEM(KV_SHAPE, jnp.bfloat16)] * GROUPS + [pltpu.VMEM((TILE, D), jnp.bfloat16)],
        compiler_params=limit(54),
        cost_estimate=pl.CostEstimate(flops=4 * TILE * D * D, bytes_accessed=4 * D * D, transcendentals=0),
        name="project_kv",
    )(tokens, modulation, norm_k, *tables, w_key, w_value)


def project_q(normed, norm_q, tables, w_query, token):
    return pl.pallas_call(
        q_kernel,
        in_specs=[HBM] * 7,
        out_specs=[VMEM] * (GROUPS + 1),
        scratch_shapes=[
            pltpu.VMEM((TILE, D), jnp.bfloat16),
            pltpu.VMEM((D,), jnp.float32),
            *[pltpu.VMEM(t.shape, jnp.float32) for t in tables],
            pltpu.VMEM((GROUPS, D, GW), jnp.bfloat16),
            pltpu.VMEM((GROUPS, TILE, GW), jnp.float32),
            pltpu.VMEM((1, D), jnp.float32),
            pltpu.SemaphoreType.DMA((2, 5)),
        ],
        out_shape=[pltpu.VMEM(Q_SHAPE, jnp.bfloat16)] * GROUPS + [TOKEN],
        compiler_params=limit(46),
        cost_estimate=pl.CostEstimate(flops=2 * TILE * D * D, bytes_accessed=2 * D * D, transcendentals=0),
        name="project_q",
    )(normed, norm_q, *tables, w_query, token)


def query_of(refs, s, h):
    return jnp.concatenate([refs[2 * s][h], refs[2 * s + 1][h]], axis=0)


def raw_scores(query, keys):
    return lax.dot_general(query, keys, (((1,), (1,)), ((), ())), preferred_element_type=jnp.float32)


def score(query, segments):
    keys = jnp.concatenate([segment[0] for segment in segments], axis=0)
    scores = raw_scores(query, keys)
    at, parts = 0, []
    for segment in segments:
        parts.append(scores[:, at : at + segment[0].shape[0]])
        at += segment[0].shape[0]
    return parts


def attend(scores, segments, state):
    found = [jnp.max(s, axis=-1, keepdims=True) for s in scores]
    found = [f if there is None else jnp.where(there, f, -1e30) for f, (_, _, there) in zip(found, segments)]
    peak = functools.reduce(jnp.maximum, found if state is None else [state[0], *found])
    weights = []
    for s, (_, _, there) in zip(scores, segments):
        low = peak if there is None else jnp.where(there, peak, 1e30)
        weights.append(jnp.exp2((s - low) * SCORE_SCALE).astype(jnp.bfloat16))
    weights = jnp.concatenate(weights, axis=1)
    values = jnp.concatenate([segment[1] for segment in segments], axis=0)
    ones = jnp.ones((values.shape[0], HEAD_DIM), jnp.bfloat16)
    both = jnp.dot(weights, jnp.concatenate([values, ones], axis=1), preferred_element_type=jnp.float32)
    total, norm = both[:, :HEAD_DIM], both[:, HEAD_DIM:]
    if state is not None:
        decay = jnp.exp2((state[0] - peak) * SCORE_SCALE)
        total, norm = total + state[1] * decay, norm + state[2] * decay
    return peak, total, norm


def attend_kernel(plan, arrays_n, state_slots, final, sc_ref, *refs):
    q, arrays, refs = refs[:4], refs[4 : 4 + arrays_n], refs[4 + arrays_n :]
    state_in = {s: refs[2 * n : 2 * n + 2] for n, s in enumerate(state_slots)}
    *refs, token_ref = refs[2 * len(state_slots) :]
    token_ref[...] = jnp.zeros_like(token_ref)
    low = lax.broadcasted_iota(jnp.int32, (2 * TILE, HEAD_DIM), 1) < HEAD_DIM // 2

    def stack_keys(tiles, kind, h):
        return jnp.concatenate([arrays[n][(*place, kind, h)] for n, place in tiles], axis=0)

    def state(s, h):
        if s not in state_in:
            return None
        stat = state_in[s][0][h]
        return stat[:, :1], state_in[s][1][h], stat[:, HEAD_DIM // 2 : HEAD_DIM // 2 + 1]

    def run(slots):
        jobs = [(h, n, s) for h in range(GH) for n, s in enumerate(sorted(slots))]

        def begin(job):
            h, _, s = job
            segments = [
                (stack_keys(tiles, 0, h), stack_keys(tiles, 1, h), None if row is None else sc_ref[5 + row] == 1)
                for tiles, row in slots[s]
            ]
            return segments, score(query_of(q, s, h), segments) if segments else None

        begun = begin(jobs[0])
        for place, (h, n, s) in enumerate(jobs):
            segments, scores = begun
            begun = begin(jobs[place + 1]) if place + 1 < len(jobs) else None
            peak, total, norm = attend(scores, segments, state(s, h)) if segments else state(s, h)
            if final:
                attended = (total / norm).astype(jnp.bfloat16)
                refs[2 * s][h] = attended[:TILE]
                refs[2 * s + 1][h] = attended[TILE:]
            else:
                refs[2 * n][h] = jnp.where(low, peak, norm)
                refs[2 * n + 1][h] = total

    if plan[0] == plan[1]:
        run(plan[0])
    else:
        for near in range(2):
            pl.when(sc_ref[4] == near)(functools.partial(run, plan[near]))


TOKEN = jax.ShapeDtypeStruct((8, HEAD_DIM), jnp.float32)
STATE_SHAPE = jax.ShapeDtypeStruct((GH, 2 * TILE, HEAD_DIM), jnp.float32)


def attend_call(name, plan, sc, queries, arrays, state):
    final = name == "attend_last"
    state_slots = sorted(state)
    states = [array for s in state_slots for array in state[s]]
    return pl.pallas_call(
        functools.partial(attend_kernel, plan, len(arrays), tuple(state_slots), final),
        in_specs=[SMEM] + [VMEM] * (GROUPS + len(arrays) + len(states)),
        out_specs=[VMEM] * (5 if final else 2 * len(plan[0]) + 1),
        out_shape=[*([jax.ShapeDtypeStruct(Q_SHAPE, jnp.bfloat16)] * 4 if final else [STATE_SHAPE] * (2 * len(plan[0]))), TOKEN],
        compiler_params=limit(32),
        cost_estimate=pl.CostEstimate(flops=1000, bytes_accessed=1000, transcendentals=0),
        name=name,
    )(sc, *queries, *arrays, *states)


OUT_PARTS = 3


def heads_wide(ref):
    return jnp.concatenate([ref[h] for h in range(GH)], axis=1)


def part_kernel(a0, a1, a2, w_ref, out_ref):
    group = mesh_place()[0]
    total = None
    for m, ref in enumerate((a0, a1, a2)):
        rows = w_ref[pl.ds(group_at(group, m), GW), :]
        part = jnp.dot(heads_wide(ref), rows, preferred_element_type=jnp.float32)
        total = part if total is None else total + part
    out_ref[...] = total


def out_kernel(part_ref, a3, mod_ref, w_ref, out_hbm, out_ref, sems):
    group = mesh_place()[0]
    rows = heads_wide(a3)
    width = D // OUT_PARTS
    copies = []
    for n in range(OUT_PARTS):
        lanes = slice(n * width, (n + 1) * width)
        last = jnp.dot(rows, w_ref[pl.ds(group_at(group, GROUPS - 1), GW), lanes], preferred_element_type=jnp.float32)
        out_ref[:, lanes] = ((part_ref[:, lanes] + last) * mod_ref[2:3, lanes]).astype(jnp.bfloat16)
        copies.append(pltpu.make_async_copy(out_ref.at[:, lanes], out_hbm.at[:, lanes], sems.at[n]))
        copies[-1].start()
    wait_all(copies)


def project_out(attended, modulation, w_out):
    part = pl.pallas_call(
        part_kernel,
        in_specs=[VMEM] * 4,
        out_specs=VMEM,
        out_shape=pltpu.VMEM((TILE, D), jnp.float32),
        compiler_params=limit(20),
        cost_estimate=pl.CostEstimate(flops=2 * TILE * D * D, bytes_accessed=2 * D * D, transcendentals=0),
        name="project_part",
    )(*attended[:3], w_out)
    return pl.pallas_call(
        out_kernel,
        in_specs=[VMEM] * 4,
        out_specs=HBM,
        scratch_shapes=[pltpu.VMEM((TILE, D), jnp.bfloat16), pltpu.SemaphoreType.DMA((OUT_PARTS,))],
        out_shape=jax.ShapeDtypeStruct((TILE, D), jnp.bfloat16),
        compiler_params=limit(20),
        cost_estimate=pl.CostEstimate(flops=2 * TILE * D * GW, bytes_accessed=2 * D * GW, transcendentals=0),
        name="project_out",
    )(part, attended[3], modulation, w_out)


def square_swap(value, m):
    if m == 0:
        return value
    flip = (m >> 1) * 4 + (m & 1)
    return lax.ppermute(value, ("ta", "wa"), [(i, i ^ flip) for i in range(8)])


def core_swap(value):
    return lax.ppermute(value, "ta", [(i, i ^ 1) for i in range(4)])


def row_swap(value, first, rows_n):
    pairs = [(i, i + 1) for i in range(first, rows_n - 1, 2)]
    return lax.ppermute(value, "ha", [edge for i, j in pairs for edge in ((i, j), (j, i))])


def after(value, *others):
    return lax.optimization_barrier((value, *others))[0]


def hold(value, token):
    return jnp.where(token[0] < 1.0, value, jnp.zeros((), value.dtype))


def square_body(tokens, modulation, w_query, w_key, w_value, w_out, norm_q, norm_k):
    ta, ha, wa = (lax.axis_index(name) for name in ("ta", "ha", "wa"))
    rows_n = lax.axis_size("ha")
    place_x, core = ta // 2, ta % 2
    near_slot = 1 - (place_x ^ core)
    partner = [ha + 1 - 2 * (ha % 2), ha - 1 + 2 * (ha % 2)]
    sc = jnp.stack(
        [2 * place_x + wa, ta, ha, wa, near_slot, *[((p >= 0) & (p < rows_n)).astype(jnp.int32) for p in partner]]
    ).astype(jnp.int32)
    half, sixth = HEAD_DIM // 2, HEAD_DIM // 6
    first = half - 2 * sixth
    tables = (
        rope_tables(lax.axis_size("ta"), CT, 0, first),
        rope_tables(rows_n, CH, first, sixth),
        rope_tables(lax.axis_size("wa"), CW, first + sixth, sixth),
    )
    *kv, normed = project_kv(tokens.reshape(TILE, D), modulation, norm_k, tables, w_key, w_value)

    def rows_of(tile):
        return [row_swap(tile, first, rows_n) for first in range(2)]

    other0 = core_swap(kv[0])
    halo0 = rows_of(kv[0])
    side = [square_swap(kv[1], 1), square_swap(kv[2], 2)]
    *queries, made = project_q(after(normed, other0), norm_q, tables, w_query, normed)
    middle = jnp.stack(after(side, queries[0], *halo0))
    halo12, other12 = rows_of(middle), core_swap(middle)
    mine3 = queries[3][None]
    queries[1:3] = [square_swap(queries[m], m) for m in range(1, 3)]
    corner = square_swap(jnp.concatenate([kv[3], after(mine3, queries[1], queries[2])]), 3)
    queries[0] = after(queries[0], *halo12)
    swapped0 = [core_swap(tile) for tile in halo0]
    halo_parts = {"same": [halo0, halo12, None], "other": [swapped0, None, None]}
    own = {"same": [(kv[0], ()), (middle, (0,)), (middle, (1,)), None], "other": [(other0, ()), (other12, (0,)), (other12, (1,)), None]}

    def halo_tiles(row):
        made = {}
        for kind, parts in halo_parts.items():
            c0, c12, c3 = [None if part is None else part[row] for part in parts]
            made[kind] = [(c0, ()), (c12, (0,)), (c12, (1,)), (c3, ())]
        return made

    def own_keys(kinds):
        return [(own[kind][m], kind, m) for kind, m in kinds], None

    def row_keys(kinds, row):
        return [(halo_tiles(row)[kind][m], kind, m) for kind, m in kinds], row

    def call(name, plans, state):
        numbers, arrays, numbered = {}, [], []
        for slots in plans:
            made = {}
            for s, segments in slots.items():
                made[s] = ()
                for tiles, row in segments:
                    ids = []
                    for (array, place), kind, m in tiles:
                        key = (id(array), place)
                        if key not in numbers:
                            known = [n for n, other in enumerate(arrays) if other is array]
                            if not known:
                                arrays.append(array)
                                known = [len(arrays) - 1]
                            numbers[key] = (known[0], place)
                        ids.append(numbers[key])
                    made[s] += ((tuple(ids), row),)
            numbered.append(made)
        return attend_call(name, tuple(numbered), sc, queries, arrays, state)

    def both(*places):
        return [(kind, m) for kind in ("same", "other") for m in places]

    def rows_keys(kinds):
        return [row_keys(kinds, r) for r in range(2)]

    cross = [("other", 2), ("other", 3)], [("other", 0), ("other", 1)]
    queries[3], corner = corner[2], corner[:2]
    own["same"][3], own["other"][3] = (corner, ()), (core_swap(corner), ())
    halo_parts["other"][1] = [core_swap(tile) for tile in halo12]
    *state, made = call(
        "attend_own",
        (
            {0: [own_keys(both(0, 1) + cross[0])], 1: [own_keys(both(2, 3))]},
            {0: [own_keys(both(0, 1))], 1: [own_keys(both(2, 3) + cross[1])]},
        ),
        {},
    )
    halo3 = rows_of(corner)
    halo_parts["same"][2] = halo3
    halo_parts["other"][2] = [core_swap(hold(tile, made)) for tile in halo3]
    *state, made = call(
        "attend_halo", ({0: rows_keys(both(0, 1)), 1: []},) * 2, {0: state[:2], 1: state[2:]}
    )
    *attended, made = call(
        "attend_last",
        ({0: rows_keys(cross[0]), 1: rows_keys(both(2, 3))}, {0: [], 1: rows_keys(both(2, 3) + cross[1])}),
        {0: state[:2], 1: state[2:]},
    )
    attended = [square_swap(attended[m], m) for m in range(GROUPS)]
    branch = project_out(attended, modulation, w_out)
    return branch.reshape(CT, CH, CW, D)


def solution(mesh):
    square = mesh.shape["ta"] == 4 and mesh.shape["wa"] == 2
    chosen = square_body if square else body
    in_specs = (P("ta", "ha", "wa", None), P(), P(), P(), P(), P(), P(), P())
    out_specs = P("ta", "ha", "wa", None)
    return jax.shard_map(chosen, mesh=mesh, in_specs=in_specs, out_specs=out_specs, check_vma=False)
```

```python
import functools

import jax
import jax.numpy as jnp
import numpy as np
from jax import lax
from jax.experimental import pallas as pl
from jax.experimental.pallas import tpu as pltpu
from jax.sharding import PartitionSpec as P

HEADS = 12
HEAD_DIM = 128
D = 1536
TT = 3
TH = 8
TW = 8
CT = 3
CH = 8
CW = 8


def with_halo(value, sides, width):
    for axis, dim in sides:
        devices, length = (lax.axis_size(axis), value.shape[dim])
        up = [(i, (i + 1) % devices) for i in range(devices - 1)]
        down = [(j, i) for i, j in up]
        last = lax.slice_in_dim(value, length - width, length, axis=dim)
        first = lax.slice_in_dim(value, 0, width, axis=dim)
        before = lax.ppermute(last, axis, up)
        after = lax.ppermute(first, axis, down)
        value = jnp.concatenate([before, value, after], axis=dim)
    return value


def modulate(tokens, modulation):
    values = tokens.astype(jnp.float32)
    center = values - jnp.mean(values, axis=-1, keepdims=True)
    spread = jnp.mean(center * center, axis=-1, keepdims=True)
    return (center * lax.rsqrt(spread + 1e-06) * (1.0 + modulation[1]) + modulation[0]).astype(
        jnp.bfloat16
    )


def rms_gain(values, gain):
    return values * lax.rsqrt(jnp.mean(values * values, axis=-1, keepdims=True) + 1e-06) * gain


def rotate_pairs(values, frame_pos, row_pos, column_pos):
    half = HEAD_DIM // 2
    sixth = HEAD_DIM // 6
    first = half - 2 * sixth
    freq_first = 10000.0 ** (-jnp.arange(first, dtype=jnp.float32) / first)
    freq_rest = 10000.0 ** (-jnp.arange(sixth, dtype=jnp.float32) / sixth)
    shape = values.shape[:3]
    angle_frame = frame_pos[:, None] * freq_first
    angle_row = row_pos[:, None] * freq_rest
    angle_column = column_pos[:, None] * freq_rest
    angles = jnp.concatenate(
        [
            jnp.broadcast_to(angle_frame[:, None, None, :], shape + (first,)),
            jnp.broadcast_to(angle_row[None, :, None, :], shape + (sixth,)),
            jnp.broadcast_to(angle_column[None, None, :, :], shape + (sixth,)),
        ],
        axis=-1,
    )
    cosine = jnp.cos(angles)[:, :, :, None, :]
    sine = jnp.sin(angles)[:, :, :, None, :]
    pairs = values.reshape(shape + (HEADS, half, 2))
    even_part = pairs[..., 0]
    odd_part = pairs[..., 1]
    rotated = jnp.stack(
        [even_part * cosine - odd_part * sine, even_part * sine + odd_part * cosine], axis=-1
    )
    return rotated.reshape(values.shape)


def tile_rows(query, key_pad, value_pad, anchor, extent):
    tile_frames = CT // TT
    tile_rows_n = CH // TH
    tile_columns = CW // TW
    tile_size = TT * TH * TW
    window = 27 * tile_size

    def one_row(index):
        frame_tile = index // tile_rows_n
        row_tile = index % tile_rows_n
        query_row = query
        query_row = query_row.reshape(TT, TH, tile_columns, TW, HEADS, HEAD_DIM).transpose(
            4, 2, 0, 1, 3, 5
        )
        query_row = query_row.reshape(HEADS, tile_columns, tile_size, HEAD_DIM)
        key_tiles = jnp.stack([key_pad])
        value_tiles = jnp.stack([value_pad])
        key_tiles = key_tiles.reshape(tile_columns, window, HEADS, HEAD_DIM).transpose(2, 0, 1, 3)
        value_tiles = value_tiles.reshape(tile_columns, window, HEADS, HEAD_DIM).transpose(
            2, 0, 1, 3
        )
        frames_at = anchor[0] + frame_tile * TT - TT + jnp.arange(3 * TT, dtype=jnp.int32)
        rows_at = anchor[1] + row_tile * TH - TH + jnp.arange(3 * TH, dtype=jnp.int32)
        columns_at = (
            anchor[2]
            + jnp.arange(tile_columns, dtype=jnp.int32)[:, None] * TW
            - TW
            + jnp.arange(3 * TW, dtype=jnp.int32)[None, :]
        )
        frame_ok = (frames_at >= 0) & (frames_at < extent[0])
        row_ok = (rows_at >= 0) & (rows_at < extent[1])
        column_ok = (columns_at >= 0) & (columns_at < extent[2])
        valid = (
            frame_ok[None, :, None, None]
            & row_ok[None, None, :, None]
            & column_ok[:, None, None, :]
        )
        valid = valid.reshape(tile_columns, window)

        def one_head(operands):
            head_query, head_key, head_value = operands
            scores = jnp.einsum(
                "cqd,ckd->cqk", head_query, head_key, preferred_element_type=jnp.float32
            ) * HEAD_DIM ** (-0.5)
            scores = jnp.where(valid[:, None, :], scores, -1e30)
            peak = jnp.max(scores, axis=-1, keepdims=True)
            expo = jnp.exp(scores - peak)
            weights = (expo / jnp.sum(expo, axis=-1, keepdims=True)).astype(jnp.bfloat16)
            return jnp.einsum(
                "cqk,ckd->cqd", weights, head_value, preferred_element_type=jnp.float32
            ).astype(jnp.bfloat16)

        attended = lax.map(one_head, (query_row, key_tiles, value_tiles))
        attended = attended.reshape(HEADS, tile_columns, TT, TH, TW, HEAD_DIM).transpose(
            2, 3, 1, 4, 0, 5
        )
        return attended.reshape(TT, TH, CW, D)

    result = lax.map(one_row, jnp.arange(tile_frames * tile_rows_n, dtype=jnp.int32))
    result = result.reshape(tile_frames, tile_rows_n, TT, TH, CW, D).transpose(0, 2, 1, 3, 4, 5)
    return result.reshape(CT, CH, CW, D)


def body(tokens, modulation, w_query, w_key, w_value, w_out, norm_q, norm_k):
    anchor = (lax.axis_index("ta") * CT, lax.axis_index("ha") * CH, lax.axis_index("wa") * CW)
    extent = (lax.axis_size("ta") * CT, lax.axis_size("ha") * CH, lax.axis_size("wa") * CW)
    frame_pos = (anchor[0] + jnp.arange(CT, dtype=jnp.int32)).astype(jnp.float32)
    row_pos = (anchor[1] + jnp.arange(CH, dtype=jnp.int32)).astype(jnp.float32)
    column_pos = (anchor[2] + jnp.arange(CW, dtype=jnp.int32)).astype(jnp.float32)
    grid = (CT, CH, CW, D)
    normed = modulate(tokens, modulation)
    flat = normed.reshape(-1, D)
    key = rms_gain(jnp.dot(flat, w_key, preferred_element_type=jnp.float32), norm_k).reshape(grid)
    key = rotate_pairs(key, frame_pos, row_pos, column_pos).astype(jnp.bfloat16)
    value = (
        jnp.dot(flat, w_value, preferred_element_type=jnp.float32)
        .astype(jnp.bfloat16)
        .reshape(grid)
    )
    key_value = jnp.stack([key, value])
    framed = with_halo(key_value, (("ta", 1),), TT)
    padded = with_halo(framed, (("ha", 2), ("wa", 3)), TW)
    query = rms_gain(jnp.dot(flat, w_query, preferred_element_type=jnp.float32), norm_q).reshape(
        grid
    )
    query = rotate_pairs(query, frame_pos, row_pos, column_pos).astype(jnp.bfloat16)
    attended = tile_rows(query, padded[0], padded[1], anchor, extent)
    branch = (
        jnp.dot(attended.reshape(-1, D), w_out, preferred_element_type=jnp.float32) * modulation[2]
    )
    return branch.astype(jnp.bfloat16).reshape(grid)


TILE = TT * TH * TW
GROUPS = 4
GH = HEADS // GROUPS
GW = GH * HEAD_DIM
SCORE_SCALE = float(HEAD_DIM ** (-0.5) * np.log2(np.e))


def rope_tables(devices, per_device, low, count):
    n = np.float32(count)
    freq = np.float32(10000.0) ** (-np.arange(count, dtype=np.float32) / n)
    angle = np.arange(devices * per_device, dtype=np.float32)[:, None] * freq[None, :]
    cosine = np.zeros((devices * per_device, HEAD_DIM), np.float32)
    sine = np.zeros((devices * per_device, HEAD_DIM), np.float32)
    for j in range(count):
        lane = 2 * (low + j)
        cosine[:, lane] = cosine[:, lane + 1] = np.cos(angle[:, j])
        sine[:, lane] = -np.sin(angle[:, j])
        sine[:, lane + 1] = np.sin(angle[:, j])
    tables = np.stack([cosine, sine]).reshape(2, devices, per_device, HEAD_DIM)
    return jnp.asarray(tables.transpose(1, 0, 2, 3))


def layer_norm(tokens, mod_ref):
    values = tokens.astype(jnp.float32)
    center = values - jnp.mean(values, axis=-1, keepdims=True)
    spread = jnp.mean(center * center, axis=-1, keepdims=True)
    shift, scale = mod_ref[0:1, :], mod_ref[1:2, :]
    return (center * lax.rsqrt(spread + 1e-06) * (1.0 + scale) + shift).astype(jnp.bfloat16)


def angle_tables(place, ft_ref, rt_ref, ct_ref):
    out = []
    for kind in range(2):
        frame = ft_ref[place[0], kind]
        row = rt_ref[place[1], kind]
        column = ct_ref[place[2], kind]
        full = frame[:, None, None, :] + row[None, :, None, :] + column[None, None, :, :]
        out.append(full.reshape(TILE, HEAD_DIM))
    return out


def rope(x, cosine, sine, even):
    swapped = jnp.where(even, pltpu.roll(x, HEAD_DIM - 1, 1), pltpu.roll(x, 1, 1))
    return x * cosine + swapped * sine


def mesh_place():
    ta, ha, wa = (lax.axis_index(name) for name in ("ta", "ha", "wa"))
    return 2 * (ta // 2) + wa, ta, ha, wa


def group_at(group, m):
    return pl.multiple_of((group ^ m) * GW, GW)


def start_all(pairs, sems):
    copies = [pltpu.make_async_copy(source, target, sems.at[n]) for n, (source, target) in enumerate(pairs)]
    for copy in copies:
        copy.start()
    return copies


def wait_all(copies):
    for copy in copies:
        copy.wait()


def weight_blocks(group, w_hbm, wbuf):
    return [(w_hbm.at[:, pl.ds(group_at(group, m), GW)], wbuf.at[m]) for m in range(GROUPS)]


def project_normed(group, normed, weights, wbuf, buf, gain_ref, angles, write, beside=()):
    cosine, sine = angles
    even = lax.broadcasted_iota(jnp.int32, (TILE, HEAD_DIM), 1) % 2 == 0
    ssq = None

    def rotate(m, prod, ssq):
        gain = gain_ref[:, pl.ds(group_at(group, m), GW)]
        for h in range(GH):
            lanes = slice(h * HEAD_DIM, (h + 1) * HEAD_DIM)
            x = prod[:, lanes]
            ssq = x * x if ssq is None else ssq + x * x
            buf[m, :, lanes] = rope(x * gain[:, lanes], cosine, sine, even)
        return ssq

    before = None
    for m in range(GROUPS):
        weights[m].wait()
        prod = jnp.dot(normed, wbuf[m], preferred_element_type=jnp.float32)
        if before is not None:
            ssq = rotate(m - 1, before, ssq)
        before = prod
    steps = list(beside)
    if steps:
        steps.pop(0)()
    ssq = rotate(GROUPS - 1, before, ssq)
    inv = lax.rsqrt(jnp.sum(ssq, axis=-1, keepdims=True) / D + 1e-06)
    for m in range(GROUPS):
        if steps:
            steps.pop(0)()
        for h in range(GH):
            write(m, h, (buf[m, :, h * HEAD_DIM : (h + 1) * HEAD_DIM] * inv).astype(jnp.bfloat16))


def kv_kernel(tok_hbm, mod_hbm, nk_hbm, ft_hbm, rt_hbm, ct_hbm, wk_hbm, wv_hbm, *refs):
    kv_ref, normed_ref, refs = refs[:4], refs[4], refs[5:]
    tok_ref, mod_ref, nk_ref, ft_ref, rt_ref, ct_ref, wk_buf, wv_buf, buf, gain_ref, sems = refs
    sources = (tok_hbm, mod_hbm, nk_hbm, ft_hbm, rt_hbm, ct_hbm)
    small = start_all(zip(sources, refs), sems.at[2])
    group, *place = mesh_place()
    key_weights = start_all(weight_blocks(group, wk_hbm, wk_buf), sems.at[0])
    value_weights = start_all(weight_blocks(group, wv_hbm, wv_buf), sems.at[1])
    wait_all(small)
    angles = angle_tables(place, ft_ref, rt_ref, ct_ref)
    gain_ref[...] = nk_ref[...].reshape(1, D)
    normed = layer_norm(tok_ref[...], mod_ref)
    normed_ref[...] = normed

    def write(m, h, x):
        kv_ref[m][0, h] = x

    def value_block(m):
        value_weights[m].wait()
        prod = jnp.dot(normed, wv_buf[m], preferred_element_type=jnp.float32)
        for h in range(GH):
            kv_ref[m][1, h] = prod[:, h * HEAD_DIM : (h + 1) * HEAD_DIM].astype(jnp.bfloat16)

    beside = [functools.partial(value_block, m) for m in range(GROUPS)]
    project_normed(group, normed, key_weights, wk_buf, buf, gain_ref, angles, write, beside)


def q_kernel(normed_hbm, nq_hbm, ft_hbm, rt_hbm, ct_hbm, wq_hbm, token_hbm, *refs):
    q_ref, made_ref, refs = refs[:4], refs[4], refs[5:]
    made_ref[...] = jnp.zeros_like(made_ref)
    normed_ref, nq_ref, ft_ref, rt_ref, ct_ref, wq_buf, buf, gain_ref, sems = refs
    small = start_all(zip((normed_hbm, nq_hbm, ft_hbm, rt_hbm, ct_hbm), refs), sems.at[1])
    group, *place = mesh_place()
    weights = start_all(weight_blocks(group, wq_hbm, wq_buf), sems.at[0])
    wait_all(small)
    angles = angle_tables(place, ft_ref, rt_ref, ct_ref)
    gain_ref[...] = nq_ref[...].reshape(1, D)

    def write(m, h, x):
        q_ref[m][h] = x

    project_normed(group, normed_ref[...], weights, wq_buf, buf, gain_ref, angles, write)


SMEM = pl.BlockSpec(memory_space=pltpu.SMEM)
VMEM = pl.BlockSpec(memory_space=pltpu.VMEM)
HBM = pl.BlockSpec(memory_space=pl.ANY)


def limit(mib):
    return pltpu.CompilerParams(vmem_limit_bytes=mib * 1024 * 1024)


KV_SHAPE = (2, GH, TILE, HEAD_DIM)
Q_SHAPE = (GH, TILE, HEAD_DIM)


def project_kv(tokens, modulation, norm_k, tables, w_key, w_value):
    return pl.pallas_call(
        kv_kernel,
        in_specs=[HBM] * 8,
        out_specs=[VMEM] * (GROUPS + 1),
        scratch_shapes=[
            pltpu.VMEM((TILE, D), jnp.bfloat16),
            pltpu.VMEM((3, D), jnp.float32),
            pltpu.VMEM((D,), jnp.float32),
            *[pltpu.VMEM(t.shape, jnp.float32) for t in tables],
            pltpu.VMEM((GROUPS, D, GW), jnp.bfloat16),
            pltpu.VMEM((GROUPS, D, GW), jnp.bfloat16),
            pltpu.VMEM((GROUPS, TILE, GW), jnp.float32),
            pltpu.VMEM((1, D), jnp.float32),
            pltpu.SemaphoreType.DMA((3, 6)),
        ],
        out_shape=[pltpu.VMEM(KV_SHAPE, jnp.bfloat16)] * GROUPS + [pltpu.VMEM((TILE, D), jnp.bfloat16)],
        compiler_params=limit(54),
        cost_estimate=pl.CostEstimate(flops=4 * TILE * D * D, bytes_accessed=4 * D * D, transcendentals=0),
        name="project_kv",
    )(tokens, modulation, norm_k, *tables, w_key, w_value)


def project_q(normed, norm_q, tables, w_query, token):
    return pl.pallas_call(
        q_kernel,
        in_specs=[HBM] * 7,
        out_specs=[VMEM] * (GROUPS + 1),
        scratch_shapes=[
            pltpu.VMEM((TILE, D), jnp.bfloat16),
            pltpu.VMEM((D,), jnp.float32),
            *[pltpu.VMEM(t.shape, jnp.float32) for t in tables],
            pltpu.VMEM((GROUPS, D, GW), jnp.bfloat16),
            pltpu.VMEM((GROUPS, TILE, GW), jnp.float32),
            pltpu.VMEM((1, D), jnp.float32),
            pltpu.SemaphoreType.DMA((2, 5)),
        ],
        out_shape=[pltpu.VMEM(Q_SHAPE, jnp.bfloat16)] * GROUPS + [TOKEN],
        compiler_params=limit(46),
        cost_estimate=pl.CostEstimate(flops=2 * TILE * D * D, bytes_accessed=2 * D * D, transcendentals=0),
        name="project_q",
    )(normed, norm_q, *tables, w_query, token)


def query_of(refs, s, h):
    return jnp.concatenate([refs[2 * s][h], refs[2 * s + 1][h]], axis=0)


def raw_scores(query, keys):
    return lax.dot_general(query, keys, (((1,), (1,)), ((), ())), preferred_element_type=jnp.float32)


def score(query, segments):
    keys = jnp.concatenate([segment[0] for segment in segments], axis=0)
    scores = raw_scores(query, keys)
    at, parts = 0, []
    for segment in segments:
        parts.append(scores[:, at : at + segment[0].shape[0]])
        at += segment[0].shape[0]
    return parts


def attend(scores, segments, state):
    found = [jnp.max(s, axis=-1, keepdims=True) for s in scores]
    found = [f if there is None else jnp.where(there, f, -1e30) for f, (_, _, there) in zip(found, segments)]
    peak = functools.reduce(jnp.maximum, found if state is None else [state[0], *found])
    weights = []
    for s, (_, _, there) in zip(scores, segments):
        low = peak if there is None else jnp.where(there, peak, 1e30)
        weights.append(jnp.exp2((s - low) * SCORE_SCALE).astype(jnp.bfloat16))
    weights = jnp.concatenate(weights, axis=1)
    values = jnp.concatenate([segment[1] for segment in segments], axis=0)
    ones = jnp.ones((values.shape[0], HEAD_DIM), jnp.bfloat16)
    both = jnp.dot(weights, jnp.concatenate([values, ones], axis=1), preferred_element_type=jnp.float32)
    total, norm = both[:, :HEAD_DIM], both[:, HEAD_DIM:]
    if state is not None:
        decay = jnp.exp2((state[0] - peak) * SCORE_SCALE)
        total, norm = total + state[1] * decay, norm + state[2] * decay
    return peak, total, norm


def attend_kernel(plan, arrays_n, state_slots, final, sc_ref, *refs):
    q, arrays, refs = [*refs[:3], refs[3].at[2]], refs[4 : 4 + arrays_n], refs[4 + arrays_n :]
    state_in = {s: refs[2 * n : 2 * n + 2] for n, s in enumerate(state_slots)}
    *refs, token_ref = refs[2 * len(state_slots) :]
    token_ref[...] = jnp.zeros_like(token_ref)
    low = lax.broadcasted_iota(jnp.int32, (2 * TILE, HEAD_DIM), 1) < HEAD_DIM // 2

    def stack_keys(tiles, kind, h):
        return jnp.concatenate([arrays[n][(*place, kind, h)] for n, place in tiles], axis=0)

    def state(s, h):
        if s not in state_in:
            return None
        stat = state_in[s][0][h]
        return stat[:, :1], state_in[s][1][h], stat[:, HEAD_DIM // 2 : HEAD_DIM // 2 + 1]

    def run(slots):
        jobs = [(h, n, s) for h in range(GH) for n, s in enumerate(sorted(slots))]

        def begin(job):
            h, _, s = job
            segments = [
                (stack_keys(tiles, 0, h), stack_keys(tiles, 1, h), None if row is None else sc_ref[5 + row] == 1)
                for tiles, row in slots[s]
            ]
            return segments, score(query_of(q, s, h), segments) if segments else None

        begun = begin(jobs[0])
        for place, (h, n, s) in enumerate(jobs):
            segments, scores = begun
            begun = begin(jobs[place + 1]) if place + 1 < len(jobs) else None
            peak, total, norm = attend(scores, segments, state(s, h)) if segments else state(s, h)
            if final:
                attended = (total / norm).astype(jnp.bfloat16)
                refs[2 * s][h] = attended[:TILE]
                refs[2 * s + 1][h] = attended[TILE:]
            else:
                refs[2 * n][h] = jnp.where(low, peak, norm)
                refs[2 * n + 1][h] = total

    if plan[0] == plan[1]:
        run(plan[0])
    else:
        for near in range(2):
            pl.when(sc_ref[4] == near)(functools.partial(run, plan[near]))


TOKEN = jax.ShapeDtypeStruct((8, HEAD_DIM), jnp.float32)
STATE_SHAPE = jax.ShapeDtypeStruct((GH, 2 * TILE, HEAD_DIM), jnp.float32)


def attend_call(name, plan, sc, queries, arrays, state):
    final = name == "attend_last"
    state_slots = sorted(state)
    states = [array for s in state_slots for array in state[s]]
    return pl.pallas_call(
        functools.partial(attend_kernel, plan, len(arrays), tuple(state_slots), final),
        in_specs=[SMEM] + [VMEM] * (GROUPS + len(arrays) + len(states)),
        out_specs=[VMEM] * (5 if final else 2 * len(plan[0]) + 1),
        out_shape=[*([jax.ShapeDtypeStruct(Q_SHAPE, jnp.bfloat16)] * 4 if final else [STATE_SHAPE] * (2 * len(plan[0]))), TOKEN],
        compiler_params=limit(32),
        cost_estimate=pl.CostEstimate(flops=1000, bytes_accessed=1000, transcendentals=0),
        name=name,
    )(sc, *queries, *arrays, *states)


OUT_PARTS = 3


def heads_wide(ref):
    return jnp.concatenate([ref[h] for h in range(GH)], axis=1)


def part_kernel(a0, a1, a2, w_ref, out_ref):
    group = mesh_place()[0]
    total = None
    for m, ref in enumerate((a0, a1, a2)):
        rows = w_ref[pl.ds(group_at(group, m), GW), :]
        part = jnp.dot(heads_wide(ref), rows, preferred_element_type=jnp.float32)
        total = part if total is None else total + part
    out_ref[...] = total


def out_kernel(part_ref, a3, mod_ref, w_ref, out_hbm, out_ref, sems):
    group = mesh_place()[0]
    rows = heads_wide(a3)
    width = D // OUT_PARTS
    copies = []
    for n in range(OUT_PARTS):
        lanes = slice(n * width, (n + 1) * width)
        last = jnp.dot(rows, w_ref[pl.ds(group_at(group, GROUPS - 1), GW), lanes], preferred_element_type=jnp.float32)
        out_ref[:, lanes] = ((part_ref[:, lanes] + last) * mod_ref[2:3, lanes]).astype(jnp.bfloat16)
        copies.append(pltpu.make_async_copy(out_ref.at[:, lanes], out_hbm.at[:, lanes], sems.at[n]))
        copies[-1].start()
    wait_all(copies)


def project_out(attended, modulation, w_out):
    part = pl.pallas_call(
        part_kernel,
        in_specs=[VMEM] * 4,
        out_specs=VMEM,
        out_shape=pltpu.VMEM((TILE, D), jnp.float32),
        compiler_params=limit(20),
        cost_estimate=pl.CostEstimate(flops=2 * TILE * D * D, bytes_accessed=2 * D * D, transcendentals=0),
        name="project_part",
    )(*attended[:3], w_out)
    return pl.pallas_call(
        out_kernel,
        in_specs=[VMEM] * 4,
        out_specs=HBM,
        scratch_shapes=[pltpu.VMEM((TILE, D), jnp.bfloat16), pltpu.SemaphoreType.DMA((OUT_PARTS,))],
        out_shape=jax.ShapeDtypeStruct((TILE, D), jnp.bfloat16),
        compiler_params=limit(20),
        cost_estimate=pl.CostEstimate(flops=2 * TILE * D * GW, bytes_accessed=2 * D * GW, transcendentals=0),
        name="project_out",
    )(part, attended[3], modulation, w_out)


def square_swap(value, m):
    if m == 0:
        return value
    flip = (m >> 1) * 4 + (m & 1)
    return lax.ppermute(value, ("ta", "wa"), [(i, i ^ flip) for i in range(8)])


def core_swap(value):
    return lax.ppermute(value, "ta", [(i, i ^ 1) for i in range(4)])


def row_swap(value, first, rows_n):
    pairs = [(i, i + 1) for i in range(first, rows_n - 1, 2)]
    return lax.ppermute(value, "ha", [edge for i, j in pairs for edge in ((i, j), (j, i))])


def after(value, *others):
    return lax.optimization_barrier((value, *others))[0]


def hold(value, token):
    return jnp.where(token[0] < 1.0, value, jnp.zeros((), value.dtype))


def square_body(tokens, modulation, w_query, w_key, w_value, w_out, norm_q, norm_k):
    ta, ha, wa = (lax.axis_index(name) for name in ("ta", "ha", "wa"))
    rows_n = lax.axis_size("ha")
    place_x, core = ta // 2, ta % 2
    near_slot = 1 - (place_x ^ core)
    partner = [ha + 1 - 2 * (ha % 2), ha - 1 + 2 * (ha % 2)]
    sc = jnp.stack(
        [2 * place_x + wa, ta, ha, wa, near_slot, *[((p >= 0) & (p < rows_n)).astype(jnp.int32) for p in partner]]
    ).astype(jnp.int32)
    half, sixth = HEAD_DIM // 2, HEAD_DIM // 6
    first = half - 2 * sixth
    tables = (
        rope_tables(lax.axis_size("ta"), CT, 0, first),
        rope_tables(rows_n, CH, first, sixth),
        rope_tables(lax.axis_size("wa"), CW, first + sixth, sixth),
    )
    *kv, normed = project_kv(tokens.reshape(TILE, D), modulation, norm_k, tables, w_key, w_value)

    def rows_of(tile):
        return [row_swap(tile, first, rows_n) for first in range(2)]

    halo0 = rows_of(kv[0])
    other0 = core_swap(kv[0])
    side = [square_swap(kv[1], 1), square_swap(kv[2], 2)]
    *queries, made = project_q(after(normed, other0), norm_q, tables, w_query, normed)
    middle = jnp.stack(after(side, queries[0], *halo0))
    halo12, other12 = rows_of(middle), core_swap(middle)
    mine3 = queries[3][None]
    queries[1:3] = [square_swap(queries[m], m) for m in range(1, 3)]
    corner = square_swap(jnp.concatenate([kv[3], mine3]), 3)
    queries[0] = after(queries[0], *halo12)
    swapped0 = [core_swap(tile) for tile in halo0]
    halo_parts = {"same": [halo0, halo12, None], "other": [swapped0, None, None]}
    own = {"same": [(kv[0], ()), (middle, (0,)), (middle, (1,)), None], "other": [(other0, ()), (other12, (0,)), (other12, (1,)), None]}

    def halo_tiles(row):
        made = {}
        for kind, parts in halo_parts.items():
            c0, c12, c3 = [None if part is None else part[row] for part in parts]
            made[kind] = [(c0, ()), (c12, (0,)), (c12, (1,)), (c3, ())]
        return made

    def own_keys(kinds):
        return [(own[kind][m], kind, m) for kind, m in kinds], None

    def row_keys(kinds, row):
        return [(halo_tiles(row)[kind][m], kind, m) for kind, m in kinds], row

    def call(name, plans, state):
        numbers, arrays, numbered = {}, [], []
        for slots in plans:
            made = {}
            for s, segments in slots.items():
                made[s] = ()
                for tiles, row in segments:
                    ids = []
                    for (array, place), kind, m in tiles:
                        key = (id(array), place)
                        if key not in numbers:
                            known = [n for n, other in enumerate(arrays) if other is array]
                            if not known:
                                arrays.append(array)
                                known = [len(arrays) - 1]
                            numbers[key] = (known[0], place)
                        ids.append(numbers[key])
                    made[s] += ((tuple(ids), row),)
            numbered.append(made)
        return attend_call(name, tuple(numbered), sc, [*queries[:3], bundle], arrays, state)

    def both(*places):
        return [(kind, m) for kind in ("same", "other") for m in places]

    def rows_keys(kinds):
        return [row_keys(kinds, r) for r in range(2)]

    cross = [("other", 2), ("other", 3)], [("other", 0), ("other", 1)]
    queries[3], bundle, corner = None, corner, corner[:2]
    own["same"][3], own["other"][3] = (bundle, ()), (core_swap(bundle), ())
    halo_parts["other"][1] = [core_swap(tile) for tile in halo12]
    *state, made = call(
        "attend_own",
        (
            {0: [own_keys(both(0, 1) + cross[0])], 1: [own_keys(both(2, 3))]},
            {0: [own_keys(both(0, 1))], 1: [own_keys(both(2, 3) + cross[1])]},
        ),
        {},
    )
    halo3 = rows_of(corner)
    halo_parts["same"][2] = halo3
    halo_parts["other"][2] = [core_swap(hold(tile, made)) for tile in halo3]
    *state, made = call(
        "attend_halo", ({0: rows_keys(both(0, 1)), 1: []},) * 2, {0: state[:2], 1: state[2:]}
    )
    *attended, made = call(
        "attend_last",
        ({0: rows_keys(cross[0]), 1: rows_keys(both(2, 3))}, {0: [], 1: rows_keys(both(2, 3) + cross[1])}),
        {0: state[:2], 1: state[2:]},
    )
    attended = [square_swap(attended[m], m) for m in reversed(range(GROUPS))][::-1]
    branch = project_out(attended, modulation, w_out)
    return branch.reshape(CT, CH, CW, D)


def solution(mesh):
    square = mesh.shape["ta"] == 4 and mesh.shape["wa"] == 2
    chosen = square_body if square else body
    in_specs = (P("ta", "ha", "wa", None), P(), P(), P(), P(), P(), P(), P())
    out_specs = P("ta", "ha", "wa", None)
    return jax.shard_map(chosen, mesh=mesh, in_specs=in_specs, out_specs=out_specs, check_vma=False)
```

```python
import functools

import jax
import jax.numpy as jnp
import numpy as np
from jax import lax
from jax.experimental import pallas as pl
from jax.experimental.pallas import tpu as pltpu
from jax.sharding import PartitionSpec as P

HEADS = 12
HEAD_DIM = 128
D = 1536
TT = 3
TH = 8
TW = 8
CT = 3
CH = 8
CW = 8


def with_halo(value, sides, width):
    for axis, dim in sides:
        devices, length = (lax.axis_size(axis), value.shape[dim])
        up = [(i, (i + 1) % devices) for i in range(devices - 1)]
        down = [(j, i) for i, j in up]
        last = lax.slice_in_dim(value, length - width, length, axis=dim)
        first = lax.slice_in_dim(value, 0, width, axis=dim)
        before = lax.ppermute(last, axis, up)
        after = lax.ppermute(first, axis, down)
        value = jnp.concatenate([before, value, after], axis=dim)
    return value


def modulate(tokens, modulation):
    values = tokens.astype(jnp.float32)
    center = values - jnp.mean(values, axis=-1, keepdims=True)
    spread = jnp.mean(center * center, axis=-1, keepdims=True)
    return (center * lax.rsqrt(spread + 1e-06) * (1.0 + modulation[1]) + modulation[0]).astype(
        jnp.bfloat16
    )


def rms_gain(values, gain):
    return values * lax.rsqrt(jnp.mean(values * values, axis=-1, keepdims=True) + 1e-06) * gain


def rotate_pairs(values, frame_pos, row_pos, column_pos):
    half = HEAD_DIM // 2
    sixth = HEAD_DIM // 6
    first = half - 2 * sixth
    freq_first = 10000.0 ** (-jnp.arange(first, dtype=jnp.float32) / first)
    freq_rest = 10000.0 ** (-jnp.arange(sixth, dtype=jnp.float32) / sixth)
    shape = values.shape[:3]
    angle_frame = frame_pos[:, None] * freq_first
    angle_row = row_pos[:, None] * freq_rest
    angle_column = column_pos[:, None] * freq_rest
    angles = jnp.concatenate(
        [
            jnp.broadcast_to(angle_frame[:, None, None, :], shape + (first,)),
            jnp.broadcast_to(angle_row[None, :, None, :], shape + (sixth,)),
            jnp.broadcast_to(angle_column[None, None, :, :], shape + (sixth,)),
        ],
        axis=-1,
    )
    cosine = jnp.cos(angles)[:, :, :, None, :]
    sine = jnp.sin(angles)[:, :, :, None, :]
    pairs = values.reshape(shape + (HEADS, half, 2))
    even_part = pairs[..., 0]
    odd_part = pairs[..., 1]
    rotated = jnp.stack(
        [even_part * cosine - odd_part * sine, even_part * sine + odd_part * cosine], axis=-1
    )
    return rotated.reshape(values.shape)


def tile_rows(query, key_pad, value_pad, anchor, extent):
    tile_frames = CT // TT
    tile_rows_n = CH // TH
    tile_columns = CW // TW
    tile_size = TT * TH * TW
    window = 27 * tile_size

    def one_row(index):
        frame_tile = index // tile_rows_n
        row_tile = index % tile_rows_n
        query_row = query
        query_row = query_row.reshape(TT, TH, tile_columns, TW, HEADS, HEAD_DIM).transpose(
            4, 2, 0, 1, 3, 5
        )
        query_row = query_row.reshape(HEADS, tile_columns, tile_size, HEAD_DIM)
        key_tiles = jnp.stack([key_pad])
        value_tiles = jnp.stack([value_pad])
        key_tiles = key_tiles.reshape(tile_columns, window, HEADS, HEAD_DIM).transpose(2, 0, 1, 3)
        value_tiles = value_tiles.reshape(tile_columns, window, HEADS, HEAD_DIM).transpose(
            2, 0, 1, 3
        )
        frames_at = anchor[0] + frame_tile * TT - TT + jnp.arange(3 * TT, dtype=jnp.int32)
        rows_at = anchor[1] + row_tile * TH - TH + jnp.arange(3 * TH, dtype=jnp.int32)
        columns_at = (
            anchor[2]
            + jnp.arange(tile_columns, dtype=jnp.int32)[:, None] * TW
            - TW
            + jnp.arange(3 * TW, dtype=jnp.int32)[None, :]
        )
        frame_ok = (frames_at >= 0) & (frames_at < extent[0])
        row_ok = (rows_at >= 0) & (rows_at < extent[1])
        column_ok = (columns_at >= 0) & (columns_at < extent[2])
        valid = (
            frame_ok[None, :, None, None]
            & row_ok[None, None, :, None]
            & column_ok[:, None, None, :]
        )
        valid = valid.reshape(tile_columns, window)

        def one_head(operands):
            head_query, head_key, head_value = operands
            scores = jnp.einsum(
                "cqd,ckd->cqk", head_query, head_key, preferred_element_type=jnp.float32
            ) * HEAD_DIM ** (-0.5)
            scores = jnp.where(valid[:, None, :], scores, -1e30)
            peak = jnp.max(scores, axis=-1, keepdims=True)
            expo = jnp.exp(scores - peak)
            weights = (expo / jnp.sum(expo, axis=-1, keepdims=True)).astype(jnp.bfloat16)
            return jnp.einsum(
                "cqk,ckd->cqd", weights, head_value, preferred_element_type=jnp.float32
            ).astype(jnp.bfloat16)

        attended = lax.map(one_head, (query_row, key_tiles, value_tiles))
        attended = attended.reshape(HEADS, tile_columns, TT, TH, TW, HEAD_DIM).transpose(
            2, 3, 1, 4, 0, 5
        )
        return attended.reshape(TT, TH, CW, D)

    result = lax.map(one_row, jnp.arange(tile_frames * tile_rows_n, dtype=jnp.int32))
    result = result.reshape(tile_frames, tile_rows_n, TT, TH, CW, D).transpose(0, 2, 1, 3, 4, 5)
    return result.reshape(CT, CH, CW, D)


def body(tokens, modulation, w_query, w_key, w_value, w_out, norm_q, norm_k):
    anchor = (lax.axis_index("ta") * CT, lax.axis_index("ha") * CH, lax.axis_index("wa") * CW)
    extent = (lax.axis_size("ta") * CT, lax.axis_size("ha") * CH, lax.axis_size("wa") * CW)
    frame_pos = (anchor[0] + jnp.arange(CT, dtype=jnp.int32)).astype(jnp.float32)
    row_pos = (anchor[1] + jnp.arange(CH, dtype=jnp.int32)).astype(jnp.float32)
    column_pos = (anchor[2] + jnp.arange(CW, dtype=jnp.int32)).astype(jnp.float32)
    grid = (CT, CH, CW, D)
    normed = modulate(tokens, modulation)
    flat = normed.reshape(-1, D)
    key = rms_gain(jnp.dot(flat, w_key, preferred_element_type=jnp.float32), norm_k).reshape(grid)
    key = rotate_pairs(key, frame_pos, row_pos, column_pos).astype(jnp.bfloat16)
    value = (
        jnp.dot(flat, w_value, preferred_element_type=jnp.float32)
        .astype(jnp.bfloat16)
        .reshape(grid)
    )
    key_value = jnp.stack([key, value])
    framed = with_halo(key_value, (("ta", 1),), TT)
    padded = with_halo(framed, (("ha", 2), ("wa", 3)), TW)
    query = rms_gain(jnp.dot(flat, w_query, preferred_element_type=jnp.float32), norm_q).reshape(
        grid
    )
    query = rotate_pairs(query, frame_pos, row_pos, column_pos).astype(jnp.bfloat16)
    attended = tile_rows(query, padded[0], padded[1], anchor, extent)
    branch = (
        jnp.dot(attended.reshape(-1, D), w_out, preferred_element_type=jnp.float32) * modulation[2]
    )
    return branch.astype(jnp.bfloat16).reshape(grid)


TILE = TT * TH * TW
GROUPS = 4
GH = HEADS // GROUPS
GW = GH * HEAD_DIM
SCORE_SCALE = float(HEAD_DIM ** (-0.5) * np.log2(np.e))


def rope_tables(devices, per_device, low, count):
    n = np.float32(count)
    freq = np.float32(10000.0) ** (-np.arange(count, dtype=np.float32) / n)
    angle = np.arange(devices * per_device, dtype=np.float32)[:, None] * freq[None, :]
    cosine = np.zeros((devices * per_device, HEAD_DIM), np.float32)
    sine = np.zeros((devices * per_device, HEAD_DIM), np.float32)
    for j in range(count):
        lane = 2 * (low + j)
        cosine[:, lane] = cosine[:, lane + 1] = np.cos(angle[:, j])
        sine[:, lane] = -np.sin(angle[:, j])
        sine[:, lane + 1] = np.sin(angle[:, j])
    tables = np.stack([cosine, sine]).reshape(2, devices, per_device, HEAD_DIM)
    return jnp.asarray(tables.transpose(1, 0, 2, 3))


def layer_norm(tokens, mod_ref):
    values = tokens.astype(jnp.float32)
    center = values - jnp.mean(values, axis=-1, keepdims=True)
    spread = jnp.mean(center * center, axis=-1, keepdims=True)
    shift, scale = mod_ref[0:1, :], mod_ref[1:2, :]
    return (center * lax.rsqrt(spread + 1e-06) * (1.0 + scale) + shift).astype(jnp.bfloat16)


def angle_tables(place, ft_ref, rt_ref, ct_ref):
    out = []
    for kind in range(2):
        frame = ft_ref[place[0], kind]
        row = rt_ref[place[1], kind]
        column = ct_ref[place[2], kind]
        full = frame[:, None, None, :] + row[None, :, None, :] + column[None, None, :, :]
        out.append(full.reshape(TILE, HEAD_DIM))
    return out


def rope(x, cosine, sine, even):
    swapped = jnp.where(even, pltpu.roll(x, HEAD_DIM - 1, 1), pltpu.roll(x, 1, 1))
    return x * cosine + swapped * sine


def mesh_place():
    ta, ha, wa = (lax.axis_index(name) for name in ("ta", "ha", "wa"))
    return 2 * (ta // 2) + wa, ta, ha, wa


def group_at(group, m):
    return pl.multiple_of((group ^ m) * GW, GW)


def start_all(pairs, sems):
    copies = [pltpu.make_async_copy(source, target, sems.at[n]) for n, (source, target) in enumerate(pairs)]
    for copy in copies:
        copy.start()
    return copies


def wait_all(copies):
    for copy in copies:
        copy.wait()


def weight_blocks(group, w_hbm, wbuf):
    return [(w_hbm.at[:, pl.ds(group_at(group, m), GW)], wbuf.at[m]) for m in range(GROUPS)]


def project_normed(group, normed, weights, wbuf, buf, gain_ref, angles, write, beside=()):
    cosine, sine = angles
    even = lax.broadcasted_iota(jnp.int32, (TILE, HEAD_DIM), 1) % 2 == 0
    ssq = None

    def rotate(m, prod, ssq):
        gain = gain_ref[:, pl.ds(group_at(group, m), GW)]
        for h in range(GH):
            lanes = slice(h * HEAD_DIM, (h + 1) * HEAD_DIM)
            x = prod[:, lanes]
            ssq = x * x if ssq is None else ssq + x * x
            buf[m, :, lanes] = rope(x * gain[:, lanes], cosine, sine, even)
        return ssq

    before = None
    for m in range(GROUPS):
        weights[m].wait()
        prod = jnp.dot(normed, wbuf[m], preferred_element_type=jnp.float32)
        if before is not None:
            ssq = rotate(m - 1, before, ssq)
        before = prod
    steps = list(beside)
    if steps:
        steps.pop(0)()
    ssq = rotate(GROUPS - 1, before, ssq)
    inv = lax.rsqrt(jnp.sum(ssq, axis=-1, keepdims=True) / D + 1e-06)
    for m in range(GROUPS):
        if steps:
            steps.pop(0)()
        for h in range(GH):
            write(m, h, (buf[m, :, h * HEAD_DIM : (h + 1) * HEAD_DIM] * inv).astype(jnp.bfloat16))


def kv_kernel(tok_hbm, mod_hbm, nk_hbm, ft_hbm, rt_hbm, ct_hbm, wk_hbm, wv_hbm, *refs):
    kv_ref, normed_ref, refs = refs[:4], refs[4], refs[5:]
    tok_ref, mod_ref, nk_ref, ft_ref, rt_ref, ct_ref, wk_buf, wv_buf, buf, gain_ref, sems = refs
    sources = (tok_hbm, mod_hbm, nk_hbm, ft_hbm, rt_hbm, ct_hbm)
    small = start_all(zip(sources, refs), sems.at[2])
    group, *place = mesh_place()
    key_weights = start_all(weight_blocks(group, wk_hbm, wk_buf), sems.at[0])
    value_weights = start_all(weight_blocks(group, wv_hbm, wv_buf), sems.at[1])
    wait_all(small)
    angles = angle_tables(place, ft_ref, rt_ref, ct_ref)
    gain_ref[...] = nk_ref[...].reshape(1, D)
    normed = layer_norm(tok_ref[...], mod_ref)
    normed_ref[...] = normed

    def write(m, h, x):
        kv_ref[m][0, h] = x

    def value_block(m):
        value_weights[m].wait()
        prod = jnp.dot(normed, wv_buf[m], preferred_element_type=jnp.float32)
        for h in range(GH):
            kv_ref[m][1, h] = prod[:, h * HEAD_DIM : (h + 1) * HEAD_DIM].astype(jnp.bfloat16)

    beside = [functools.partial(value_block, m) for m in range(GROUPS)]
    project_normed(group, normed, key_weights, wk_buf, buf, gain_ref, angles, write, beside)


def q_kernel(normed_hbm, nq_hbm, ft_hbm, rt_hbm, ct_hbm, wq_hbm, token_hbm, *refs):
    q_ref, made_ref, refs = refs[:4], refs[4], refs[5:]
    made_ref[...] = jnp.zeros_like(made_ref)
    normed_ref, nq_ref, ft_ref, rt_ref, ct_ref, wq_buf, buf, gain_ref, sems = refs
    small = start_all(zip((normed_hbm, nq_hbm, ft_hbm, rt_hbm, ct_hbm), refs), sems.at[1])
    group, *place = mesh_place()
    weights = start_all(weight_blocks(group, wq_hbm, wq_buf), sems.at[0])
    wait_all(small)
    angles = angle_tables(place, ft_ref, rt_ref, ct_ref)
    gain_ref[...] = nq_ref[...].reshape(1, D)

    def write(m, h, x):
        q_ref[m][h] = x

    project_normed(group, normed_ref[...], weights, wq_buf, buf, gain_ref, angles, write)


SMEM = pl.BlockSpec(memory_space=pltpu.SMEM)
VMEM = pl.BlockSpec(memory_space=pltpu.VMEM)
HBM = pl.BlockSpec(memory_space=pl.ANY)


def limit(mib):
    return pltpu.CompilerParams(vmem_limit_bytes=mib * 1024 * 1024)


KV_SHAPE = (2, GH, TILE, HEAD_DIM)
Q_SHAPE = (GH, TILE, HEAD_DIM)


def project_kv(tokens, modulation, norm_k, tables, w_key, w_value):
    return pl.pallas_call(
        kv_kernel,
        in_specs=[HBM] * 8,
        out_specs=[VMEM] * (GROUPS + 1),
        scratch_shapes=[
            pltpu.VMEM((TILE, D), jnp.bfloat16),
            pltpu.VMEM((3, D), jnp.float32),
            pltpu.VMEM((D,), jnp.float32),
            *[pltpu.VMEM(t.shape, jnp.float32) for t in tables],
            pltpu.VMEM((GROUPS, D, GW), jnp.bfloat16),
            pltpu.VMEM((GROUPS, D, GW), jnp.bfloat16),
            pltpu.VMEM((GROUPS, TILE, GW), jnp.float32),
            pltpu.VMEM((1, D), jnp.float32),
            pltpu.SemaphoreType.DMA((3, 6)),
        ],
        out_shape=[pltpu.VMEM(KV_SHAPE, jnp.bfloat16)] * GROUPS + [pltpu.VMEM((TILE, D), jnp.bfloat16)],
        compiler_params=limit(54),
        cost_estimate=pl.CostEstimate(flops=4 * TILE * D * D, bytes_accessed=4 * D * D, transcendentals=0),
        name="project_kv",
    )(tokens, modulation, norm_k, *tables, w_key, w_value)


def project_q(normed, norm_q, tables, w_query, token):
    return pl.pallas_call(
        q_kernel,
        in_specs=[HBM] * 7,
        out_specs=[VMEM] * (GROUPS + 1),
        scratch_shapes=[
            pltpu.VMEM((TILE, D), jnp.bfloat16),
            pltpu.VMEM((D,), jnp.float32),
            *[pltpu.VMEM(t.shape, jnp.float32) for t in tables],
            pltpu.VMEM((GROUPS, D, GW), jnp.bfloat16),
            pltpu.VMEM((GROUPS, TILE, GW), jnp.float32),
            pltpu.VMEM((1, D), jnp.float32),
            pltpu.SemaphoreType.DMA((2, 5)),
        ],
        out_shape=[pltpu.VMEM(Q_SHAPE, jnp.bfloat16)] * GROUPS + [TOKEN],
        compiler_params=limit(46),
        cost_estimate=pl.CostEstimate(flops=2 * TILE * D * D, bytes_accessed=2 * D * D, transcendentals=0),
        name="project_q",
    )(normed, norm_q, *tables, w_query, token)


def query_of(refs, s, h):
    return jnp.concatenate([refs[2 * s][h], refs[2 * s + 1][h]], axis=0)


def raw_scores(query, keys):
    return lax.dot_general(query, keys, (((1,), (1,)), ((), ())), preferred_element_type=jnp.float32)


def score(query, segments):
    keys = jnp.concatenate([segment[0] for segment in segments], axis=0)
    scores = raw_scores(query, keys)
    at, parts = 0, []
    for segment in segments:
        parts.append(scores[:, at : at + segment[0].shape[0]])
        at += segment[0].shape[0]
    return parts


def attend(scores, segments, state):
    found = [jnp.max(s, axis=-1, keepdims=True) for s in scores]
    found = [f if there is None else jnp.where(there, f, -1e30) for f, (_, _, there) in zip(found, segments)]
    peak = functools.reduce(jnp.maximum, found if state is None else [state[0], *found])
    weights = []
    for s, (_, _, there) in zip(scores, segments):
        low = peak if there is None else jnp.where(there, peak, 1e30)
        weights.append(jnp.exp2((s - low) * SCORE_SCALE).astype(jnp.bfloat16))
    weights = jnp.concatenate(weights, axis=1)
    values = jnp.concatenate([segment[1] for segment in segments], axis=0)
    ones = jnp.ones((values.shape[0], HEAD_DIM), jnp.bfloat16)
    both = jnp.dot(weights, jnp.concatenate([values, ones], axis=1), preferred_element_type=jnp.float32)
    total, norm = both[:, :HEAD_DIM], both[:, HEAD_DIM:]
    if state is not None:
        decay = jnp.exp2((state[0] - peak) * SCORE_SCALE)
        total, norm = total + state[1] * decay, norm + state[2] * decay
    return peak, total, norm


def attend_kernel(plan, arrays_n, state_slots, final, sc_ref, *refs):
    q, arrays, refs = [*refs[:3], refs[3].at[2]], refs[4 : 4 + arrays_n], refs[4 + arrays_n :]
    state_in = {s: refs[2 * n : 2 * n + 2] for n, s in enumerate(state_slots)}
    *refs, token_ref = refs[2 * len(state_slots) :]
    token_ref[...] = jnp.zeros_like(token_ref)
    low = lax.broadcasted_iota(jnp.int32, (2 * TILE, HEAD_DIM), 1) < HEAD_DIM // 2

    def stack_keys(tiles, kind, h):
        return jnp.concatenate([arrays[n][(*place, kind, h)] for n, place in tiles], axis=0)

    def state(s, h):
        if s not in state_in:
            return None
        stat = state_in[s][0][h]
        return stat[:, :1], state_in[s][1][h], stat[:, HEAD_DIM // 2 : HEAD_DIM // 2 + 1]

    def run(slots):
        jobs = [(h, n, s) for h in range(GH) for n, s in enumerate(sorted(slots))]

        def begin(job):
            h, _, s = job
            segments = [
                (stack_keys(tiles, 0, h), stack_keys(tiles, 1, h), None if row is None else sc_ref[5 + row] == 1)
                for tiles, row in slots[s]
            ]
            return segments, score(query_of(q, s, h), segments) if segments else None

        begun = begin(jobs[0])
        for place, (h, n, s) in enumerate(jobs):
            segments, scores = begun
            begun = begin(jobs[place + 1]) if place + 1 < len(jobs) else None
            peak, total, norm = attend(scores, segments, state(s, h)) if segments else state(s, h)
            if final:
                attended = (total / norm).astype(jnp.bfloat16)
                refs[2 * s][h] = attended[:TILE]
                refs[2 * s + 1][h] = attended[TILE:]
            else:
                refs[2 * n][h] = jnp.where(low, peak, norm)
                refs[2 * n + 1][h] = total

    if plan[0] == plan[1]:
        run(plan[0])
    else:
        for near in range(2):
            pl.when(sc_ref[4] == near)(functools.partial(run, plan[near]))


TOKEN = jax.ShapeDtypeStruct((8, HEAD_DIM), jnp.float32)
STATE_SHAPE = jax.ShapeDtypeStruct((GH, 2 * TILE, HEAD_DIM), jnp.float32)


def attend_call(name, plan, sc, queries, arrays, state):
    final = name == "attend_last"
    state_slots = sorted(state)
    states = [array for s in state_slots for array in state[s]]
    return pl.pallas_call(
        functools.partial(attend_kernel, plan, len(arrays), tuple(state_slots), final),
        in_specs=[SMEM] + [VMEM] * (GROUPS + len(arrays) + len(states)),
        out_specs=[VMEM] * (5 if final else 2 * len(plan[0]) + 1),
        out_shape=[*([jax.ShapeDtypeStruct(Q_SHAPE, jnp.bfloat16)] * 4 if final else [STATE_SHAPE] * (2 * len(plan[0]))), TOKEN],
        compiler_params=limit(24),
        cost_estimate=pl.CostEstimate(flops=1000, bytes_accessed=1000, transcendentals=0),
        name=name,
    )(sc, *queries, *arrays, *states)


OUT_PARTS = 3


def heads_wide(ref):
    return jnp.concatenate([ref[h] for h in range(GH)], axis=1)


def part_kernel(a0, a1, a2, w_ref, out_ref):
    group = mesh_place()[0]
    total = None
    for m, ref in enumerate((a0, a1, a2)):
        rows = w_ref[pl.ds(group_at(group, m), GW), :]
        part = jnp.dot(heads_wide(ref), rows, preferred_element_type=jnp.float32)
        total = part if total is None else total + part
    out_ref[...] = total


def out_kernel(part_ref, a3, mod_ref, w_ref, out_hbm, out_ref, sems):
    group = mesh_place()[0]
    rows = heads_wide(a3)
    width = D // OUT_PARTS
    copies = []
    for n in range(OUT_PARTS):
        lanes = slice(n * width, (n + 1) * width)
        last = jnp.dot(rows, w_ref[pl.ds(group_at(group, GROUPS - 1), GW), lanes], preferred_element_type=jnp.float32)
        out_ref[:, lanes] = ((part_ref[:, lanes] + last) * mod_ref[2:3, lanes]).astype(jnp.bfloat16)
        copies.append(pltpu.make_async_copy(out_ref.at[:, lanes], out_hbm.at[:, lanes], sems.at[n]))
        copies[-1].start()
    wait_all(copies)


def project_out(attended, modulation, w_out):
    part = pl.pallas_call(
        part_kernel,
        in_specs=[VMEM] * 4,
        out_specs=VMEM,
        out_shape=pltpu.VMEM((TILE, D), jnp.float32),
        compiler_params=limit(20),
        cost_estimate=pl.CostEstimate(flops=2 * TILE * D * D, bytes_accessed=2 * D * D, transcendentals=0),
        name="project_part",
    )(*attended[:3], w_out)
    return pl.pallas_call(
        out_kernel,
        in_specs=[VMEM] * 4,
        out_specs=HBM,
        scratch_shapes=[pltpu.VMEM((TILE, D), jnp.bfloat16), pltpu.SemaphoreType.DMA((OUT_PARTS,))],
        out_shape=jax.ShapeDtypeStruct((TILE, D), jnp.bfloat16),
        compiler_params=limit(20),
        cost_estimate=pl.CostEstimate(flops=2 * TILE * D * GW, bytes_accessed=2 * D * GW, transcendentals=0),
        name="project_out",
    )(part, attended[3], modulation, w_out)


def square_swap(value, m):
    if m == 0:
        return value
    flip = (m >> 1) * 4 + (m & 1)
    return lax.ppermute(value, ("ta", "wa"), [(i, i ^ flip) for i in range(8)])


def core_swap(value):
    return lax.ppermute(value, "ta", [(i, i ^ 1) for i in range(4)])


def row_swap(value, first, rows_n):
    pairs = [(i, i + 1) for i in range(first, rows_n - 1, 2)]
    return lax.ppermute(value, "ha", [edge for i, j in pairs for edge in ((i, j), (j, i))])


def after(value, *others):
    return lax.optimization_barrier((value, *others))[0]


def hold(value, token):
    return jnp.where(token[0] < 1.0, value, jnp.zeros((), value.dtype))


def square_body(tokens, modulation, w_query, w_key, w_value, w_out, norm_q, norm_k):
    ta, ha, wa = (lax.axis_index(name) for name in ("ta", "ha", "wa"))
    rows_n = lax.axis_size("ha")
    place_x, core = ta // 2, ta % 2
    near_slot = 1 - (place_x ^ core)
    partner = [ha + 1 - 2 * (ha % 2), ha - 1 + 2 * (ha % 2)]
    sc = jnp.stack(
        [2 * place_x + wa, ta, ha, wa, near_slot, *[((p >= 0) & (p < rows_n)).astype(jnp.int32) for p in partner]]
    ).astype(jnp.int32)
    half, sixth = HEAD_DIM // 2, HEAD_DIM // 6
    first = half - 2 * sixth
    tables = (
        rope_tables(lax.axis_size("ta"), CT, 0, first),
        rope_tables(rows_n, CH, first, sixth),
        rope_tables(lax.axis_size("wa"), CW, first + sixth, sixth),
    )
    *kv, normed = project_kv(tokens.reshape(TILE, D), modulation, norm_k, tables, w_key, w_value)

    def rows_of(tile):
        return [row_swap(tile, first, rows_n) for first in range(2)]

    halo0 = rows_of(kv[0])
    other0 = core_swap(kv[0])
    side = [square_swap(kv[1], 1), square_swap(kv[2], 2)]
    *queries, made = project_q(after(normed, other0), norm_q, tables, w_query, normed)
    middle = jnp.stack(after(side, queries[0], *halo0))
    halo12, other12 = rows_of(middle), core_swap(middle)
    mine3 = queries[3][None]
    queries[1:3] = [square_swap(queries[m], m) for m in range(1, 3)]
    corner = square_swap(jnp.concatenate([kv[3], mine3]), 3)
    queries[0] = after(queries[0], *halo12)
    swapped0 = [core_swap(tile) for tile in halo0]
    halo_parts = {"same": [halo0, halo12, None], "other": [swapped0, None, None]}
    own = {"same": [(kv[0], ()), (middle, (0,)), (middle, (1,)), None], "other": [(other0, ()), (other12, (0,)), (other12, (1,)), None]}

    def halo_tiles(row):
        made = {}
        for kind, parts in halo_parts.items():
            c0, c12, c3 = [None if part is None else part[row] for part in parts]
            made[kind] = [(c0, ()), (c12, (0,)), (c12, (1,)), (c3, ())]
        return made

    def own_keys(kinds):
        return [(own[kind][m], kind, m) for kind, m in kinds], None

    def row_keys(kinds, row):
        return [(halo_tiles(row)[kind][m], kind, m) for kind, m in kinds], row

    def call(name, plans, state):
        numbers, arrays, numbered = {}, [], []
        for slots in plans:
            made = {}
            for s, segments in slots.items():
                made[s] = ()
                for tiles, row in segments:
                    ids = []
                    for (array, place), kind, m in tiles:
                        key = (id(array), place)
                        if key not in numbers:
                            known = [n for n, other in enumerate(arrays) if other is array]
                            if not known:
                                arrays.append(array)
                                known = [len(arrays) - 1]
                            numbers[key] = (known[0], place)
                        ids.append(numbers[key])
                    made[s] += ((tuple(ids), row),)
            numbered.append(made)
        return attend_call(name, tuple(numbered), sc, [*queries[:3], bundle], arrays, state)

    def both(*places):
        return [(kind, m) for kind in ("same", "other") for m in places]

    def rows_keys(kinds):
        return [row_keys(kinds, r) for r in range(2)]

    cross = [("other", 2), ("other", 3)], [("other", 0), ("other", 1)]
    queries[3], bundle, corner = None, corner, corner[:2]
    own["same"][3], own["other"][3] = (bundle, ()), (core_swap(bundle), ())
    halo_parts["other"][1] = [core_swap(tile) for tile in halo12]
    *state, made = call(
        "attend_own",
        (
            {0: [own_keys(both(0, 1) + cross[0])], 1: [own_keys(both(2, 3))]},
            {0: [own_keys(both(0, 1))], 1: [own_keys(both(2, 3) + cross[1])]},
        ),
        {},
    )
    halo3 = rows_of(corner)
    halo_parts["same"][2] = halo3
    halo_parts["other"][2] = [core_swap(hold(tile, made)) for tile in halo3]
    *state, made = call(
        "attend_halo", ({0: rows_keys(both(0, 1)), 1: []},) * 2, {0: state[:2], 1: state[2:]}
    )
    *attended, made = call(
        "attend_last",
        ({0: rows_keys(cross[0]), 1: rows_keys(both(2, 3))}, {0: [], 1: rows_keys(both(2, 3) + cross[1])}),
        {0: state[:2], 1: state[2:]},
    )
    attended = [square_swap(attended[m], m) for m in reversed(range(GROUPS))][::-1]
    branch = project_out(attended, modulation, w_out)
    return branch.reshape(CT, CH, CW, D)


def solution(mesh):
    square = mesh.shape["ta"] == 4 and mesh.shape["wa"] == 2
    chosen = square_body if square else body
    in_specs = (P("ta", "ha", "wa", None), P(), P(), P(), P(), P(), P(), P())
    out_specs = P("ta", "ha", "wa", None)
    return jax.shard_map(chosen, mesh=mesh, in_specs=in_specs, out_specs=out_specs, check_vma=False)
```
